128 devices in a mesh: src: 4 (over x_lo, core), tgt: 32 (over z, y, x_hi).
Axes of the slice: x: 4 (x_hi: 2, x_lo: 2; x = x_hi * 2 + x_lo), y: 4, z: 4, core: 2. Of those that a mesh axis runs over, the one named last changes fastest.
Arguments:
- src_features: float32 [50, 32768], P(None, 'src'), may hold values from -6 to 6
- src_mass: float32 [32768], P('src'), may hold values from 6.1035157e-06 to 0.00061035156
- section_ids: int32 [32768], P('src'), may hold values from 0 to 31
- shard_counts: int32 [4], replicated, may hold values from 1 to 8192, 16384 in all
- section_offsets: float32 [50, 32], replicated, may hold values from -0.3125 to 0.3125
- tgt_features: float32 [50, 32768], P(None, 'tgt'), may hold values from -6 to 6
- tgt_mass: float32 [32768], P('tgt'), may hold values from 3.0517579e-06 to 0.00030517578
Outputs:
- src_potential: float32 [16384], P('src')
- tgt_potential: float32 [32768], P('tgt')
- self_potential: float32 [16384], P('src')
The draws below stay inside these ranges and needn't reach their ends.
Inputs may be any that keep to these rules, and one draw needn't show every extreme that they name: The entries sum to 16384 and the largest equals 8192; block k uses its first shard_counts[k] slots.
All inputs are finite; a program needn't handle non-finite values.
Results may differ from the reference program's by a relative error of at most 0.0003.
Values sent between devices are 32-bit elements; how exact they have to be, the bound alone decides.
A program may use at most 64 MiB of HBM per device.

```python
import math
import jax
import jax.numpy as jnp
import numpy as np
from jax import lax

P_SIZE = 50
SECTIONS = 32
ITERS = 3
CAP = 8192
RAW_SLOTS = 32768
SRC_CELLS = 16384
TGT_CELLS = 32768
N_SRC = 4


def draw_src_features(key, part):
    key = jax.random.fold_in(key, 11)
    return jnp.clip(jax.random.normal(key, (P_SIZE, RAW_SLOTS), jnp.float32) * 0.03, -6.0, 6.0)


def draw_tgt_features(key, part):
    key = jax.random.fold_in(key, 12)
    return jnp.clip(jax.random.normal(key, (P_SIZE, TGT_CELLS), jnp.float32) * 0.03, -6.0, 6.0)


def set_ends(result, key, low, top_value):
    longest = result.shape.index(max(result.shape))
    spots = []
    for shift in (0, 1):
        where = [jax.random.randint(jax.random.fold_in(key, axis), (), 0, length) for axis, length in enumerate(result.shape)]
        where[longest] = (where[longest] + shift) % result.shape[longest]
        spots.append(tuple(where))
    return result.at[spots[0]].set(low).at[spots[1]].set(top_value)


def levels(key, shape, cuts, low, top_value):
    gain = 1.0
    for axis_at, blocks in cuts:
        draws = jax.random.uniform(jax.random.fold_in(jax.random.fold_in(key, 6), axis_at), (blocks,), jnp.float32, low / len(cuts), top_value / len(cuts))
        gain = gain * jnp.repeat(jnp.exp(draws), shape[axis_at] // blocks).reshape((-1,) + (1,) * (len(shape) - 1 - axis_at))
    return gain


def profile(count, total, most, lean):
    weights = [(1 << 20) // math.isqrt(grade ** lean) + 1 for grade in range(2, count + 1)]
    surplus, given = total - most - (count - 1), [1] * (count - 1)
    while surplus > 0:
        movable = [i for i in range(count - 1) if given[i] < most]
        mass, remaining = sum([weights[i] for i in movable]), surplus
        for i in movable:
            addition = min(most - given[i], max(1, remaining * weights[i] // mass), surplus)
            given[i] = given[i] + addition
            surplus = surplus - addition
    return np.array([most] + given)


def ragged(stream_key, number_of, total, most, slope):
    if number_of == 2:
        one = jax.random.randint(stream_key, (), max(1, total - most), min(most, total - 1) + 1)
        return jnp.stack([one, total - one])
    tallies = jnp.asarray(profile(number_of, total, most, slope), jnp.int32)
    twos = (number_of - 1) // 2
    giver, taker = tallies[1:1 + 2 * twos:2], tallies[2:2 + 2 * twos:2]
    margin = jnp.minimum(giver - 1, most - taker)
    shifted = jax.random.randint(jax.random.fold_in(stream_key, 1), (twos,), 0, 1 << 20) % (margin + 1)
    tallies = tallies.at[1:1 + 2 * twos:2].set(giver - shifted).at[2:2 + 2 * twos:2].set(taker + shifted)
    return tallies[jax.random.permutation(jax.random.fold_in(stream_key, 2), number_of)]


def noise(stream_key, dims, scale, most, held_as=jnp.bfloat16):
    drawn = scale * jax.random.normal(stream_key, dims, jnp.float32)
    return jnp.clip(drawn, min=-most, max=most).astype(held_as)


def setup_inputs(seed: int = 0) -> dict:
    arg_keys = jax.random.split(jax.random.key(seed), 8)
    src_features = draw_src_features(jax.random.fold_in(arg_keys[7], 71), 0)
    src_mass = jnp.clip(jnp.exp(math.log(0.00061035156) - 4.6051702 * jax.random.uniform(arg_keys[1], (RAW_SLOTS,), jnp.float32) ** levels(arg_keys[1], (RAW_SLOTS,), ((0, 4),), -0.2, 0.2)), 6.10351571594947e-06, 0.00061035156)
    section_ids = set_ends(jax.random.randint(arg_keys[2], (RAW_SLOTS,), 0, SECTIONS), jax.random.fold_in(arg_keys[2], 1), 0, SECTIONS - 1).astype(jnp.int32)
    shard_counts = ragged(arg_keys[3], N_SRC, SRC_CELLS, CAP, 2).astype(jnp.int32)
    section_offsets = noise(arg_keys[4], (P_SIZE, SECTIONS), 0.02, 0.3125, jnp.float32)
    tgt_features = draw_tgt_features(jax.random.fold_in(arg_keys[7], 71), 0)
    tgt_mass = jnp.clip(jnp.exp(math.log(0.00030517578) - 4.6051702 * jax.random.uniform(arg_keys[6], (TGT_CELLS,), jnp.float32) ** levels(arg_keys[6], (TGT_CELLS,), ((0, 32),), -0.2, 0.2)), 3.051757857974735e-06, 0.00030517578)
    return {"src_features": src_features, "src_mass": src_mass, "section_ids": section_ids, "shard_counts": shard_counts, "section_offsets": section_offsets, "tgt_features": tgt_features, "tgt_mass": tgt_mass}


EPS = 0.05
TAU = 1.0 / (1.0 + EPS)


def row_lse(xa, sqa, xb, sqb, weight):
    rows = xa.shape[1]
    size = min(512, rows)
    count = rows // size
    blocks = xa.reshape(xa.shape[0], count, size).transpose(1, 0, 2)
    sq_blocks = sqa.reshape(count, size)

    def one(item):
        cross = jnp.dot(item[0].T, xb, precision=lax.Precision.HIGHEST, preferred_element_type=jnp.float32)
        cost = item[1][:, None] + sqb[None, :] - 2.0 * cross
        scores = weight[None, :] - cost / EPS
        peak = jnp.max(scores, axis=1)
        return peak + jnp.log(jnp.sum(jnp.exp(scores - peak[:, None]), axis=1))

    return lax.map(one, (blocks, sq_blocks)).reshape(rows)


def reference(src_features, src_mass, section_ids, shard_counts, section_offsets, tgt_features, tgt_mass):
    starts = (jnp.cumsum(shard_counts) - shard_counts).astype(jnp.int32)
    position = jnp.arange(SRC_CELLS, dtype=jnp.int32)
    owner = jnp.sum((position[:, None] >= starts[None, 1:]).astype(jnp.int32), axis=1).astype(jnp.int32)
    raw_index = (owner * CAP + position - starts[owner]).astype(jnp.int32)
    corrected = src_features - section_offsets[:, section_ids]
    src_x = corrected[:, raw_index]
    log_src = jnp.log(src_mass[raw_index])
    log_tgt = jnp.log(tgt_mass)
    sq_src = jnp.sum(src_x * src_x, axis=0)
    sq_tgt = jnp.sum(tgt_features * tgt_features, axis=0)
    src_pot = jnp.zeros((SRC_CELLS,), jnp.float32)
    tgt_pot = jnp.zeros((TGT_CELLS,), jnp.float32)
    self_pot = jnp.zeros((SRC_CELLS,), jnp.float32)
    for step in range(ITERS):
        new_f = -TAU * EPS * row_lse(src_x, sq_src, tgt_features, sq_tgt, log_tgt + tgt_pot / EPS)
        new_p = -TAU * EPS * row_lse(src_x, sq_src, src_x, sq_src, log_src + self_pot / EPS)
        src_pot = new_f
        self_pot = 0.5 * (self_pot + new_p)
        tgt_pot = -TAU * EPS * row_lse(tgt_features, sq_tgt, src_x, sq_src, log_src + src_pot / EPS)
    return src_pot, tgt_pot, self_pot
```

```python
import jax
import jax.numpy as jnp
from jax import lax
from jax.experimental import pallas as pl
from jax.experimental.pallas import tpu as pltpu
from jax.sharding import PartitionSpec as P

COMPONENTS = 50
ROWS = 56
SECTIONS = 32
ITERS = 3
CAP = 8192
GROUP = 2048
HALF = 1024
SPAN = GROUP + 128
LEAD = GROUP
WIDTH = LEAD + CAP + SPAN

EPS = 0.05
TAU = 1.0 / (1.0 + EPS)
LOG2E = 1.4426950408889634
SCALE = LOG2E / EPS

F32 = jnp.float32
BF16 = jnp.bfloat16
MESH = pl.DeviceIdType.MESH
TILE = 256
CHUNK = 512


def place():
    src, tgt = lax.axis_index("src"), lax.axis_index("tgt")
    z, rest = lax.div(tgt, 8), lax.rem(tgt, 8)
    return (
        lax.div(src, 2),
        lax.rem(src, 2),
        lax.div(z, 2),
        lax.rem(z, 2),
        lax.div(rest, 2),
        lax.rem(rest, 2),
    )


def device(x_lo, core, z_hi, z_lo, y, x_hi):
    return (x_lo * 2 + core, (z_hi * 2 + z_lo) * 8 + y * 2 + x_hi)


def pieces(value):
    high = value.astype(BF16)
    rest = value - high.astype(F32)
    middle = rest.astype(BF16)
    return high, middle, (rest - middle.astype(F32)).astype(BF16)


def relay_kernel(counts_ref, feats_ref, mass_ref, ids_ref, offsets_ref, out_ref, held):
    x_lo, core, z_hi, z_lo, y, x_hi = place()
    mine = x_lo * 2 + core
    start = jnp.int32(0)
    for k in range(3):
        start = start + jnp.where(k < mine, counts_ref[k], 0)
    count = counts_ref[mine]
    three = jnp.concatenate([p.astype(F32) for p in pieces(offsets_ref[...])], axis=1).astype(BF16)
    for at in range(0, CAP, 1024):
        ids = ids_ref[:, at : at + 1024]
        section = lax.rem(lax.broadcasted_iota(jnp.int32, (3 * SECTIONS, 1024), 0), SECTIONS)
        onehot = jnp.where(section == ids, 1.0, 0.0).astype(BF16)
        shift = jnp.dot(three, onehot, preferred_element_type=F32)
        to = slice(LEAD + at, LEAD + at + 1024)
        held[48:ROWS, to] = jnp.zeros((ROWS - 48, 1024), F32)
        held[0:COMPONENTS, to] = feats_ref[:, at : at + 1024] - shift
        held[COMPONENTS : COMPONENTS + 1, to] = mass_ref[:, at : at + 1024]
    lane = lax.broadcasted_iota(jnp.int32, (ROWS, 128), 1)

    def contribute(index, carry):
        to_x = lax.rem(x_lo + lax.div(index, 2), 2)
        to_core = lax.rem(core + lax.rem(index, 2), 2)
        base = (to_x * 2 + to_core) * (2 * GROUP) + z_lo * GROUP - start
        at = jnp.clip(base, -LEAD, CAP) + LEAD
        aligned = pl.multiple_of(lax.div(at, 128) * 128, 128)
        off = lax.rem(at, 128)
        turn = lax.rem(128 - off, 128)
        before = pltpu.roll(held[:, pl.ds(aligned, 128)], turn, 1)
        for t in range(GROUP // 128):
            after = pltpu.roll(
                held[:, pl.ds(pl.multiple_of(aligned + (t + 1) * 128, 128), 128)], turn, 1
            )
            value = jnp.where(lane < 128 - off, before, after)
            local = lane + (base + t * 128)
            value = jnp.where((local >= 0) & (local < count), value, 0.0)
            out_ref[index, :, t * 128 : (t + 1) * 128] = value
            before = after
        return carry

    lax.fori_loop(0, 4, contribute, 0)


def log_sum(parts):
    peak = jnp.max(parts, axis=0)
    return peak + jnp.log2(jnp.sum(jnp.exp2(parts - peak[None]), axis=0))


def lse_pass(lhs, rhs, bufs, count, put):
    tiles = GROUP // TILE
    chunk = min(CHUNK, count)

    def both(j_made, made, j_used, used, peak):
        columns = rhs[:, pl.ds(pl.multiple_of(j_made * TILE, TILE), TILE)]
        top, total = None, None
        for at in range(0, count, chunk):
            s = jnp.dot(lhs[at : at + chunk, :], columns, preferred_element_type=F32)
            made[at : at + chunk, :] = s
            here = jnp.max(s, axis=0, keepdims=True)
            top = here if top is None else jnp.maximum(top, here)
            if peak is not None:
                e = jnp.exp2(used[at : at + chunk, :] - peak)
                part = jnp.sum(e, axis=0, keepdims=True)
                total = part if total is None else total + part
        if peak is not None:
            put(j_used, peak + jnp.log2(total))
        return top

    first = both(0, bufs[0], None, None, None)

    def body(pair, peak):
        j = 2 * pair
        peak = both(j + 1, bufs[1], j, bufs[0], peak)
        return both(lax.rem(j + 2, tiles), bufs[0], j + 1, bufs[1], peak)

    lax.fori_loop(0, tiles // 2, body, first)


def to_rows(ref, row):
    for r in range(row.shape[1] // 128):
        ref[r : r + 1, :] = row[:, r * 128 : (r + 1) * 128]


def set_weights(lhs, fixed, weight):
    rows = weight.shape[0]
    parts = [p.astype(F32) for p in pieces(weight)]
    stacked = jnp.concatenate(parts + [jnp.zeros((128 - 3 * rows, 128), F32)], axis=0)
    turned = stacked.T
    lane = lax.rem(lax.broadcasted_iota(jnp.int32, (128, 128), 1), rows)
    for c in range(rows):
        at = slice(c * 128, (c + 1) * 128)
        lhs[at, 128:256] = jnp.where(lane == c, turned, 0.0).astype(BF16) + fixed[at, :]


def set_left(lhs, fixed, one, two, three):
    zero = jnp.zeros((64, 128), F32)
    for c in range(one.shape[1] // 128):
        at = slice(c * 128, (c + 1) * 128)
        first = jnp.concatenate([one[:, at].astype(F32), two[:, at].astype(F32)], axis=0)
        second = jnp.concatenate([zero, three[:, at].astype(F32)], axis=0)
        lhs[at, 0:128] = first.T.astype(BF16)
        fixed[at, :] = second.T.astype(BF16)


def set_right(rhs, one, two, three):
    rhs[0:64, :] = one
    rhs[64:128, :] = two
    row = lax.broadcasted_iota(jnp.int32, (64, GROUP), 0)
    rhs[128:192, :] = jnp.where(row < 48, 1.0, 0.0).astype(BF16)
    rhs[192:256, :] = three


def padded(cells, centre):
    row = lax.broadcasted_iota(jnp.int32, cells.shape, 0)
    kept = jnp.where(row < COMPONENTS, cells - centre, 0.0)
    return jnp.concatenate([kept, jnp.zeros((64 - ROWS, cells.shape[1]), F32)], axis=0)


def sinkhorn_kernel(
    con_ref, tgt_ref, mass_ref,
    src_out, tgt_out, self_out,
    from_own, from_opp, opp, landed, ybuf, xfull, sbuf,
    lhs_x, lhs_y, lhs_s, fix_x, fix_y, fix_s, rhs_x, rhs_y, buf_a, buf_b,
    sq_x, sq_y, sq_s, log_x, log_y, log_s, pot_p, pot_s, wide,
    fy, fz, py, pz, gb, pots, fin,
    relay_send, relay_recv, opp_send, opp_recv, own_sem, tgt_sem, self_sem, local_sem,
    fy_send, fy_recv, fz_send, fz_recv, py_send, py_recv, pz_send, pz_recv,
    gb_send, gb_recv, pot_send, pot_recv, fin_send, fin_recv,
):
    x_lo, core, z_hi, z_lo, y, x_hi = place()
    sibling = device(x_lo, 1 - core, z_hi, z_lo, y, x_hi)
    twin = device(x_lo, core, z_hi, 1 - z_lo, y, x_hi)
    across = device(1 - x_lo, core, z_hi, z_lo, y, 1 - x_hi)
    straight = lax.rem(x_lo + core, 2)
    opposite = device(1 - x_lo, core, z_hi, z_lo, y, lax.rem(x_hi + straight, 2))
    y_hi, y_lo = lax.div(y, 2), lax.rem(y, 2)
    partner = device(
        lax.rem(x_lo + y_hi, 2), lax.rem(core + y_lo, 2), z_hi, lax.rem(z_lo + z_hi, 2), y, x_hi
    )
    alone = (y + z_hi) == 0
    g = x_lo * 4 + core * 2 + z_lo
    zx = z_hi * 2 + x_hi

    def y_peer(k):
        return device(x_lo, core, z_hi, z_lo, k, x_hi)

    def zx_peer(k):
        return device(x_lo, core, lax.div(k, 2), z_lo, y, lax.rem(k, 2))

    def g_peer(k):
        return device(lax.div(k, 4), lax.rem(lax.div(k, 2), 2), z_hi, lax.rem(k, 2), y, x_hi)

    y_others = [lax.rem(y + d, 4) for d in range(1, 4)]
    zx_others = [lax.rem(zx + d, 4) for d in range(1, 4)]
    g_others = [lax.rem(g + d, 8) for d in range(1, 8)]

    barrier = pltpu.get_barrier_semaphore()
    peers = [y_peer(k) for k in y_others] + [zx_peer(k) for k in zx_others]
    peers += [g_peer(k) for k in g_others] + [across]
    for peer in peers:
        pl.semaphore_signal(barrier, inc=1, device_id=peer, device_id_type=MESH)

    ybuf[z_lo, 48:ROWS, :] = jnp.zeros((ROWS - 48, HALF), F32)
    ybuf[z_lo, 0:COMPONENTS, :] = tgt_ref[...]
    ybuf[z_lo, COMPONENTS : COMPONENTS + 1, :] = mass_ref[...]

    pl.semaphore_wait(barrier, len(peers))

    def remote(src, dst, send, recv, to):
        return pltpu.make_async_remote_copy(
            src_ref=src, dst_ref=dst, send_sem=send, recv_sem=recv, device_id=to,
            device_id_type=MESH,
        )

    parts = [slice(c * 512, (c + 1) * 512) for c in range(4)]
    relays = [
        remote(con_ref.at[3, :, s], from_opp.at[:, s], relay_send.at[c], relay_recv.at[c], sibling)
        for c, s in enumerate(parts)
    ]
    for copy in relays:
        copy.start()
    own = remote(con_ref.at[1], from_own, own_sem.at[0], own_sem.at[1], sibling)
    own.start()
    tgt = remote(ybuf.at[z_lo], ybuf.at[z_lo], tgt_sem.at[0], tgt_sem.at[1], twin)
    tgt.start()
    onward = [
        remote(opp.at[:, s], landed.at[:, s], opp_send.at[c], opp_recv.at[c], opposite)
        for c, s in enumerate(parts)
    ]
    for c, s in enumerate(parts):
        relays[c].wait_recv()
        opp[:, s] = con_ref[2, :, s] + from_opp[:, s]
        onward[c].start()

    remote(ybuf.at[1 - z_lo], ybuf.at[1 - z_lo], tgt_sem.at[0], tgt_sem.at[1], twin).wait_recv()
    cells = jnp.concatenate([ybuf[0], ybuf[1]], axis=1)
    centre = jnp.sum(cells, axis=1, keepdims=True) * (1.0 / GROUP)
    kept = padded(cells, centre)
    to_rows(sq_y, jnp.sum(kept * kept, axis=0, keepdims=True) * SCALE)
    to_rows(log_y, jnp.log2(cells[COMPONENTS : COMPONENTS + 1, :]))
    high, middle, unused = pieces(kept)
    set_left(lhs_y, fix_y, high, high, middle)
    set_right(rhs_y, high, high, middle)
    set_weights(lhs_y, fix_y, log_y[...] - sq_y[...])

    own.wait_recv()
    for copy in onward:
        copy.wait_recv()
    cells = con_ref[0] + from_own[...] + landed[...]
    xfull[...] = cells
    half = pl.ds(pl.multiple_of(x_hi * HALF, HALF), HALF)
    shared = remote(xfull.at[:, half], sbuf, self_sem.at[0], self_sem.at[1], partner)
    kept_here = pltpu.make_async_copy(xfull.at[:, half], sbuf, local_sem)

    @pl.when(alone)
    def _():
        kept_here.start()

    @pl.when(jnp.logical_not(alone))
    def _():
        shared.start()

    kept = padded(cells, centre)
    to_rows(sq_x, jnp.sum(kept * kept, axis=0, keepdims=True) * SCALE)
    to_rows(log_x, jnp.log2(cells[COMPONENTS : COMPONENTS + 1, :]))
    high, middle, unused = pieces(kept * (2.0 * SCALE))
    set_right(rhs_x, high, middle, high)
    set_left(lhs_x, fix_x, high, middle, high)
    for copy in relays + onward + [own, tgt]:
        copy.wait_send()

    pot_p[...] = jnp.zeros_like(pot_p)
    pot_s[...] = jnp.zeros_like(pot_s)

    def put_wide(j, value):
        wide[pl.ds(2 * j, 1), :] = value[:, 0:128]
        wide[pl.ds(2 * j + 1, 1), :] = value[:, 128:256]

    def spread(box, it, me, others, peer, send, recv):
        for k in others:
            remote(box.at[it, me], box.at[it, me], send.at[it, k], recv.at[it, me], peer(k)).start()

    def collect(box, it, me, others, peer, send, recv):
        for k in others:
            remote(box.at[it, k], box.at[it, k], send.at[it, k], recv.at[it, k], peer(k)).wait_recv()
        for k in others:
            remote(box.at[it, me], box.at[it, me], send.at[it, k], recv.at[it, me], peer(k)).wait_send()
        return log_sum(box[it])

    bufs = (buf_a, buf_b)
    half_rows = pl.ds(pl.multiple_of(x_hi * 8, 8), 8)

    def iteration(it, carry):
        lse_pass(lhs_y, rhs_x, bufs, GROUP, put_wide)
        fy[it, y] = wide[...] - sq_x[...]
        spread(fy, it, y, y_others, y_peer, fy_send, fy_recv)

        @pl.when(it == 0)
        def _():
            @pl.when(alone)
            def _():
                kept_here.wait()

            @pl.when(jnp.logical_not(alone))
            def _():
                shared.wait_recv()
                shared.wait_send()

            got = sbuf[...]
            columns = padded(got, centre)
            to_rows(sq_s, jnp.sum(columns * columns, axis=0, keepdims=True) * SCALE)
            to_rows(log_s, jnp.log2(got[COMPONENTS : COMPONENTS + 1, :]))
            upper, lower, unused = pieces(columns)
            set_left(lhs_s, fix_s, upper, upper, lower)

        @pl.when(it > 0)
        def _():
            last = it - 1

            @pl.when(alone)
            def _():
                pot_s[...] = pot_p[half_rows, :]

            @pl.when(jnp.logical_not(alone))
            def _():
                moved = remote(
                    pots.at[0, last], pots.at[1, last], pot_send.at[last], pot_recv.at[last],
                    partner,
                )
                moved.wait_recv()
                moved.wait_send()
                pot_s[...] = pots[1, last]

        set_weights(lhs_s, fix_s, log_s[...] + pot_s[...] - sq_s[...])
        lse_pass(lhs_s, rhs_x, bufs, HALF, put_wide)
        py[it, y] = wide[...] - sq_x[...]
        spread(py, it, y, y_others, y_peer, py_send, py_recv)

        fz[it, zx] = collect(fy, it, y, y_others, y_peer, fy_send, fy_recv)
        spread(fz, it, zx, zx_others, zx_peer, fz_send, fz_recv)
        pz[it, zx] = collect(py, it, y, y_others, y_peer, py_send, py_recv)
        spread(pz, it, zx, zx_others, zx_peer, pz_send, pz_recv)
        pot_f = -TAU * collect(fz, it, zx, zx_others, zx_peer, fz_send, fz_recv)
        set_weights(lhs_x, fix_x, log_x[...] + pot_f - sq_x[...])

        @pl.when(it == ITERS - 1)
        def _():
            fin[0, z_lo] = pot_f * (1.0 / SCALE)
            remote(
                fin.at[0, z_lo], fin.at[0, z_lo], fin_send.at[0], fin_recv.at[0], twin
            ).start()

        lse_pass(lhs_x, rhs_y, bufs, GROUP, put_wide)
        gb[it, g] = wide[...] - sq_y[...]
        spread(gb, it, g, g_others, g_peer, gb_send, gb_recv)

        new_p = -TAU * collect(pz, it, zx, zx_others, zx_peer, pz_send, pz_recv)
        pot_p[...] = 0.5 * (pot_p[...] + new_p)

        @pl.when((it < ITERS - 1) & jnp.logical_not(alone))
        def _():
            pots[0, it] = pot_p[half_rows, :]
            remote(
                pots.at[0, it], pots.at[1, it], pot_send.at[it], pot_recv.at[it], partner
            ).start()

        @pl.when(it == ITERS - 1)
        def _():
            fin[1, z_lo] = pot_p[...] * (1.0 / SCALE)
            remote(
                fin.at[1, z_lo], fin.at[1, z_lo], fin_send.at[1], fin_recv.at[1], twin
            ).start()

        pot_g = -TAU * collect(gb, it, g, g_others, g_peer, gb_send, gb_recv)
        wide[...] = pot_g

        @pl.when(it < ITERS - 1)
        def _():
            set_weights(lhs_y, fix_y, log_y[...] + pot_g - sq_y[...])

        return carry

    lax.fori_loop(0, ITERS, iteration, 0)

    tgt_out[...] = wide[pl.ds(pl.multiple_of(z_lo * 8, 8), 8), :] * (1.0 / SCALE)
    for kind in range(2):
        remote(
            fin.at[kind, 1 - z_lo], fin.at[kind, 1 - z_lo], fin_send.at[kind], fin_recv.at[kind],
            twin,
        ).wait_recv()
        remote(
            fin.at[kind, z_lo], fin.at[kind, z_lo], fin_send.at[kind], fin_recv.at[kind], twin
        ).wait_send()
    src_out[0:16, :] = fin[0, 0]
    src_out[16:32, :] = fin[0, 1]
    self_out[0:16, :] = fin[1, 0]
    self_out[16:32, :] = fin[1, 1]


def on_device(
    src_features, src_mass, section_ids, shard_counts, section_offsets, tgt_features, tgt_mass
):
    vmem = pl.BlockSpec(memory_space=pltpu.VMEM)
    contributions = pl.pallas_call(
        relay_kernel,
        out_shape=jax.ShapeDtypeStruct((4, ROWS, GROUP), F32),
        in_specs=[pl.BlockSpec(memory_space=pltpu.SMEM)] + [vmem] * 4,
        out_specs=vmem,
        scratch_shapes=[pltpu.VMEM((ROWS, WIDTH), F32)],
        compiler_params=pltpu.CompilerParams(vmem_limit_bytes=32 * 1024 * 1024),
    )(
        shard_counts,
        src_features,
        src_mass.reshape(1, CAP),
        section_ids.reshape(1, CAP),
        section_offsets,
    )
    V, D = pltpu.VMEM, pltpu.SemaphoreType.DMA
    rows16, rows8 = (16, 128), (8, 128)
    outs = pl.pallas_call(
        sinkhorn_kernel,
        out_shape=(
            jax.ShapeDtypeStruct((32, 128), F32),
            jax.ShapeDtypeStruct((8, 128), F32),
            jax.ShapeDtypeStruct((32, 128), F32),
        ),
        in_specs=[vmem] * 3,
        out_specs=(vmem, vmem, vmem),
        scratch_shapes=[
            V((ROWS, GROUP), F32), V((ROWS, GROUP), F32), V((ROWS, GROUP), F32),
            V((ROWS, GROUP), F32), V((2, ROWS, HALF), F32), V((ROWS, GROUP), F32),
            V((ROWS, HALF), F32),
            V((GROUP, 256), BF16), V((GROUP, 256), BF16), V((HALF, 256), BF16),
            V((GROUP, 128), BF16), V((GROUP, 128), BF16), V((HALF, 128), BF16),
            V((256, GROUP), BF16), V((256, GROUP), BF16),
            V((GROUP, TILE), F32), V((GROUP, TILE), F32),
            V(rows16, F32), V(rows16, F32), V(rows8, F32),
            V(rows16, F32), V(rows16, F32), V(rows8, F32),
            V(rows16, F32), V(rows8, F32), V(rows16, F32),
            V((ITERS, 4) + rows16, F32), V((ITERS, 4) + rows16, F32),
            V((ITERS, 4) + rows16, F32), V((ITERS, 4) + rows16, F32),
            V((ITERS, 8) + rows16, F32), V((2, ITERS - 1) + rows8, F32),
            V((2, 2) + rows16, F32),
            D((4,)), D((4,)), D((4,)), D((4,)), D((2,)), D((2,)), D((2,)), D,
            D((ITERS, 4)), D((ITERS, 4)), D((ITERS, 4)), D((ITERS, 4)),
            D((ITERS, 4)), D((ITERS, 4)), D((ITERS, 4)), D((ITERS, 4)),
            D((ITERS, 8)), D((ITERS, 8)), D((ITERS,)), D((ITERS,)), D((2,)), D((2,)),
        ],
        compiler_params=pltpu.CompilerParams(
            collective_id=0, has_side_effects=True, vmem_limit_bytes=48 * 1024 * 1024
        ),
    )(contributions, tgt_features, tgt_mass.reshape(1, HALF))
    return (outs[0].reshape(2 * GROUP), outs[1].reshape(HALF), outs[2].reshape(2 * GROUP))


def solution(mesh):
    return jax.shard_map(
        on_device,
        mesh=mesh,
        in_specs=(P(None, "src"), P("src"), P("src"), P(), P(), P(None, "tgt"), P("tgt")),
        out_specs=(P("src"), P("tgt"), P("src")),
        check_vma=False,
    )
```

```python
import jax
import jax.numpy as jnp
from jax import lax
from jax.experimental import pallas as pl
from jax.experimental.pallas import tpu as pltpu
from jax.sharding import PartitionSpec as P

COMPONENTS = 50
ROWS = 56
SECTIONS = 32
ITERS = 3
CAP = 8192
GROUP = 2048
HALF = 1024
SPAN = GROUP + 128
LEAD = GROUP
WIDTH = LEAD + CAP + SPAN

EPS = 0.05
TAU = 1.0 / (1.0 + EPS)
LOG2E = 1.4426950408889634
SCALE = LOG2E / EPS

F32 = jnp.float32
BF16 = jnp.bfloat16
MESH = pl.DeviceIdType.MESH
TILE = 512
CHUNK = 256


def place():
    src, tgt = lax.axis_index("src"), lax.axis_index("tgt")
    z, rest = lax.div(tgt, 8), lax.rem(tgt, 8)
    return (
        lax.div(src, 2),
        lax.rem(src, 2),
        lax.div(z, 2),
        lax.rem(z, 2),
        lax.div(rest, 2),
        lax.rem(rest, 2),
    )


def device(x_lo, core, z_hi, z_lo, y, x_hi):
    return (x_lo * 2 + core, (z_hi * 2 + z_lo) * 8 + y * 2 + x_hi)


def pieces(value):
    high = value.astype(BF16)
    rest = value - high.astype(F32)
    middle = rest.astype(BF16)
    return high, middle, (rest - middle.astype(F32)).astype(BF16)


def correct(feats_ref, mass_ref, ids_ref, offsets_ref, held, ready):
    three = jnp.concatenate([p.astype(F32) for p in pieces(offsets_ref[...])], axis=0).astype(BF16)
    for at in range(0, CAP, 1024):
        ready(at)
        ids = ids_ref[:, at : at + 1024]
        section = lax.rem(lax.broadcasted_iota(jnp.int32, (3 * SECTIONS, 1024), 0), SECTIONS)
        onehot = jnp.where(section == ids, 1.0, 0.0).astype(BF16)
        shift = lax.dot_general(
            three, onehot, (((0,), (0,)), ((), ())), preferred_element_type=F32
        )
        to = slice(LEAD + at, LEAD + at + 1024)
        held[48:ROWS, to] = jnp.zeros((ROWS - 48, 1024), F32)
        held[0:COMPONENTS, to] = feats_ref[:, at : at + 1024] - shift
        held[COMPONENTS : COMPONENTS + 1, to] = mass_ref[:, at : at + 1024]


def contribute(held, base, count, out):
    at = jnp.clip(base, -LEAD, CAP) + LEAD
    aligned = pl.multiple_of(lax.div(at, 128) * 128, 128)
    off = lax.rem(at, 128)
    turn = lax.rem(128 - off, 128)
    lane = lax.broadcasted_iota(jnp.int32, (ROWS, 128), 1)
    before = pltpu.roll(held[:, pl.ds(aligned, 128)], turn, 1)
    for t in range(GROUP // 128):
        after = pltpu.roll(
            held[:, pl.ds(pl.multiple_of(aligned + (t + 1) * 128, 128), 128)], turn, 1
        )
        value = jnp.where(lane < 128 - off, before, after)
        local = lane + (base + t * 128)
        out[:, t * 128 : (t + 1) * 128] = jnp.where((local >= 0) & (local < count), value, 0.0)
        before = after


def relay_kernel(
    counts_ref, feats_any, mass_any, ids_any, offsets_any, out_any,
    held, feats_ref, mass_ref, ids_ref, offsets_ref, out_ref, feats_sem, small_sem, out_sem,
):
    small = [
        pltpu.make_async_copy(a, b, small_sem.at[i])
        for i, (a, b) in enumerate(
            [(offsets_any, offsets_ref), (ids_any, ids_ref), (mass_any, mass_ref)]
        )
    ]
    large = [
        pltpu.make_async_copy(
            feats_any.at[:, at : at + 2048], feats_ref.at[:, at : at + 2048], feats_sem.at[i]
        )
        for i, at in enumerate(range(0, CAP, 2048))
    ]
    for copy in small + large:
        copy.start()
    x_lo, core, z_hi, z_lo, y, x_hi = place()
    mine = x_lo * 2 + core
    begin = jnp.int32(0)
    for k in range(3):
        begin = begin + jnp.where(k < mine, counts_ref[k], 0)
    count = counts_ref[mine]

    def ready(at):
        if at % 2048 == 0:
            large[at // 2048].wait()

    for copy in small:
        copy.wait()
    correct(feats_ref, mass_ref, ids_ref, offsets_ref, held, ready)
    moves = []
    for index in (3, 2, 1, 0):
        to_x, to_core = lax.rem(x_lo + index // 2, 2), lax.rem(core + index % 2, 2)
        base = (to_x * 2 + to_core) * (2 * GROUP) + z_lo * GROUP - begin
        contribute(held, base, count, out_ref.at[index])
        moves.append(
            pltpu.make_async_copy(out_ref.at[index], out_any.at[index], out_sem.at[index])
        )
        moves[-1].start()
    for copy in moves:
        copy.wait()


def log_sum(parts):
    peak = jnp.max(parts, axis=0)
    return peak + jnp.log2(jnp.sum(jnp.exp2(parts - peak[None]), axis=0))


def lse_pass(lhs, rhs, bufs, count, put):
    tiles = GROUP // TILE
    chunk = min(CHUNK, count)

    def both(j_made, made, j_used, used, peak):
        columns = rhs[:, pl.ds(pl.multiple_of(j_made * TILE, TILE), TILE)]
        top, total = None, None
        for at in range(0, count, chunk):
            s = jnp.dot(lhs[at : at + chunk, :], columns, preferred_element_type=F32)
            made[at : at + chunk, :] = s
            here = jnp.max(s, axis=0, keepdims=True)
            top = here if top is None else jnp.maximum(top, here)
            if peak is not None:
                e = jnp.exp2(used[at : at + chunk, :] - peak)
                part = jnp.sum(e, axis=0, keepdims=True)
                total = part if total is None else total + part
        if peak is not None:
            put(j_used, peak + jnp.log2(total))
        return top

    first = both(0, bufs[0], None, None, None)

    def body(pair, peak):
        j = 2 * pair
        peak = both(j + 1, bufs[1], j, bufs[0], peak)
        return both(lax.rem(j + 2, tiles), bufs[0], j + 1, bufs[1], peak)

    lax.fori_loop(0, tiles // 2, body, first)


def to_rows(ref, row):
    for r in range(row.shape[1] // 128):
        ref[r : r + 1, :] = row[:, r * 128 : (r + 1) * 128]


def set_weights(lhs, fixed, weight):
    rows = weight.shape[0]
    parts = [p.astype(F32) for p in pieces(weight)]
    stacked = jnp.concatenate(parts + [jnp.zeros((128 - 3 * rows, 128), F32)], axis=0)
    turned = stacked.T
    lane = lax.rem(lax.broadcasted_iota(jnp.int32, (128, 128), 1), rows)
    for c in range(rows):
        at = slice(c * 128, (c + 1) * 128)
        lhs[at, 128:256] = jnp.where(lane == c, turned, 0.0).astype(BF16) + fixed[at, :]


def set_left(lhs, fixed, one, two, three):
    zero = jnp.zeros((64, 128), F32)
    for c in range(one.shape[1] // 128):
        at = slice(c * 128, (c + 1) * 128)
        first = jnp.concatenate([one[:, at].astype(F32), two[:, at].astype(F32)], axis=0)
        second = jnp.concatenate([zero, three[:, at].astype(F32)], axis=0)
        lhs[at, 0:128] = first.T.astype(BF16)
        fixed[at, :] = second.T.astype(BF16)


def set_right(rhs, one, two, three):
    rhs[0:64, :] = one
    rhs[64:128, :] = two
    row = lax.broadcasted_iota(jnp.int32, (64, GROUP), 0)
    rhs[128:192, :] = jnp.where(row < 48, 1.0, 0.0).astype(BF16)
    rhs[192:256, :] = three


def padded(cells, centre):
    row = lax.broadcasted_iota(jnp.int32, cells.shape, 0)
    kept = jnp.where(row < COMPONENTS, cells - centre, 0.0)
    return jnp.concatenate([kept, jnp.zeros((64 - ROWS, cells.shape[1]), F32)], axis=0)


def sinkhorn_kernel(
    con_any, tgt_ref, tgt_mass_ref,
    src_out, tgt_out, self_out,
    con_ref,
    from_own, from_opp, opp, landed, ybuf, xfull, sbuf,
    lhs_x, lhs_y, lhs_s, fix_x, fix_y, fix_s, rhs_x, rhs_y, buf_a, buf_b,
    sq_x, sq_y, sq_s, log_x, log_y, log_s, pot_p, pot_s, wide,
    fy, fz, py, pz, gb, pots, fin,
    relay_send, relay_recv, opp_send, opp_recv, own_sem, tgt_sem, self_sem, local_sem,
    fy_send, fy_recv, fz_send, fz_recv, py_send, py_recv, pz_send, pz_recv,
    gb_send, gb_recv, pot_send, pot_recv, fin_send, fin_recv, con_sem,
):
    loads = [
        pltpu.make_async_copy(con_any.at[2 * i], con_ref.at[i], con_sem.at[i]) for i in range(2)
    ]
    for copy in loads:
        copy.start()
    x_lo, core, z_hi, z_lo, y, x_hi = place()
    sibling = device(x_lo, 1 - core, z_hi, z_lo, y, x_hi)
    twin = device(x_lo, core, z_hi, 1 - z_lo, y, x_hi)
    across = device(1 - x_lo, core, z_hi, z_lo, y, 1 - x_hi)
    straight = lax.rem(x_lo + core, 2)
    opposite = device(1 - x_lo, core, z_hi, z_lo, y, lax.rem(x_hi + straight, 2))
    y_hi, y_lo = lax.div(y, 2), lax.rem(y, 2)
    partner = device(
        lax.rem(x_lo + y_hi, 2), lax.rem(core + y_lo, 2), z_hi, lax.rem(z_lo + z_hi, 2), y, x_hi
    )
    alone = (y + z_hi) == 0
    g = x_lo * 4 + core * 2 + z_lo
    zx = z_hi * 2 + x_hi

    def y_peer(k):
        return device(x_lo, core, z_hi, z_lo, k, x_hi)

    def zx_peer(k):
        return device(x_lo, core, lax.div(k, 2), z_lo, y, lax.rem(k, 2))

    def g_peer(k):
        return device(lax.div(k, 4), lax.rem(lax.div(k, 2), 2), z_hi, lax.rem(k, 2), y, x_hi)

    y_others = [lax.rem(y + d, 4) for d in range(1, 4)]
    zx_others = [lax.rem(zx + d, 4) for d in range(1, 4)]
    g_others = [lax.rem(g + d, 8) for d in range(1, 8)]

    barrier = pltpu.get_barrier_semaphore()
    peers = [y_peer(k) for k in y_others] + [zx_peer(k) for k in zx_others]
    peers += [g_peer(k) for k in g_others] + [across]
    for peer in peers:
        pl.semaphore_signal(barrier, inc=1, device_id=peer, device_id_type=MESH)

    ybuf[z_lo, 48:ROWS, :] = jnp.zeros((ROWS - 48, HALF), F32)
    ybuf[z_lo, 0:COMPONENTS, :] = tgt_ref[...]
    ybuf[z_lo, COMPONENTS : COMPONENTS + 1, :] = tgt_mass_ref[...]

    pl.semaphore_wait(barrier, len(peers))

    def remote(src, dst, send, recv, to):
        return pltpu.make_async_remote_copy(
            src_ref=src, dst_ref=dst, send_sem=send, recv_sem=recv, device_id=to,
            device_id_type=MESH,
        )

    parts = [slice(c * 512, (c + 1) * 512) for c in range(4)]
    relays = [
        remote(con_any.at[3, :, s], from_opp.at[:, s], relay_send.at[c], relay_recv.at[c], sibling)
        for c, s in enumerate(parts)
    ]
    own = remote(con_any.at[1], from_own, own_sem.at[0], own_sem.at[1], sibling)
    tgt = remote(ybuf.at[z_lo], ybuf.at[z_lo], tgt_sem.at[0], tgt_sem.at[1], twin)
    tgt.start()

    for copy in relays:
        copy.start()
    own.start()
    onward = [
        remote(opp.at[:, s], landed.at[:, s], opp_send.at[c], opp_recv.at[c], opposite)
        for c, s in enumerate(parts)
    ]
    loads[1].wait()
    for c, s in enumerate(parts):
        relays[c].wait_recv()
        opp[:, s] = con_ref[1, :, s] + from_opp[:, s]
        onward[c].start()

    remote(ybuf.at[1 - z_lo], ybuf.at[1 - z_lo], tgt_sem.at[0], tgt_sem.at[1], twin).wait_recv()
    cells = jnp.concatenate([ybuf[0], ybuf[1]], axis=1)
    centre = jnp.sum(cells, axis=1, keepdims=True) * (1.0 / GROUP)
    kept = padded(cells, centre)
    to_rows(sq_y, jnp.sum(kept * kept, axis=0, keepdims=True) * SCALE)
    to_rows(log_y, jnp.log2(cells[COMPONENTS : COMPONENTS + 1, :]))
    high, middle, unused = pieces(kept)
    set_left(lhs_y, fix_y, high, high, middle)
    set_right(rhs_y, high, high, middle)
    set_weights(lhs_y, fix_y, log_y[...] - sq_y[...])

    loads[0].wait()
    own.wait_recv()
    for copy in onward:
        copy.wait_recv()
    cells = con_ref[0] + from_own[...] + landed[...]
    xfull[...] = cells
    half = pl.ds(pl.multiple_of(x_hi * HALF, HALF), HALF)
    shared = remote(xfull.at[:, half], sbuf, self_sem.at[0], self_sem.at[1], partner)
    kept_here = pltpu.make_async_copy(xfull.at[:, half], sbuf, local_sem)

    @pl.when(alone)
    def _():
        kept_here.start()

    @pl.when(jnp.logical_not(alone))
    def _():
        shared.start()

    kept = padded(cells, centre)
    to_rows(sq_x, jnp.sum(kept * kept, axis=0, keepdims=True) * SCALE)
    to_rows(log_x, jnp.log2(cells[COMPONENTS : COMPONENTS + 1, :]))
    high, middle, unused = pieces(kept * (2.0 * SCALE))
    set_right(rhs_x, high, middle, high)
    set_left(lhs_x, fix_x, high, middle, high)
    for copy in relays + onward + [own, tgt]:
        copy.wait_send()

    pot_p[...] = jnp.zeros_like(pot_p)
    pot_s[...] = jnp.zeros_like(pot_s)

    def put_wide(j, value):
        for r in range(TILE // 128):
            wide[pl.ds(TILE // 128 * j + r, 1), :] = value[:, r * 128 : (r + 1) * 128]

    def spread(box, it, me, others, peer, send, recv):
        for k in others:
            remote(box.at[it, me], box.at[it, me], send.at[it, k], recv.at[it, me], peer(k)).start()

    def collect(box, it, me, others, peer, send, recv):
        for k in others:
            remote(box.at[it, k], box.at[it, k], send.at[it, k], recv.at[it, k], peer(k)).wait_recv()
        for k in others:
            remote(box.at[it, me], box.at[it, me], send.at[it, k], recv.at[it, me], peer(k)).wait_send()
        return log_sum(box[it])

    bufs = (buf_a, buf_b)
    half_rows = pl.ds(pl.multiple_of(x_hi * 8, 8), 8)

    def iteration(it, carry):
        lse_pass(lhs_y, rhs_x, bufs, GROUP, put_wide)
        fy[it, y] = wide[...] - sq_x[...]
        spread(fy, it, y, y_others, y_peer, fy_send, fy_recv)

        @pl.when(it == 0)
        def _():
            @pl.when(alone)
            def _():
                kept_here.wait()

            @pl.when(jnp.logical_not(alone))
            def _():
                shared.wait_recv()
                shared.wait_send()

            got = sbuf[...]
            columns = padded(got, centre)
            to_rows(sq_s, jnp.sum(columns * columns, axis=0, keepdims=True) * SCALE)
            to_rows(log_s, jnp.log2(got[COMPONENTS : COMPONENTS + 1, :]))
            upper, lower, unused = pieces(columns)
            set_left(lhs_s, fix_s, upper, upper, lower)

        @pl.when(it > 0)
        def _():
            last = it - 1

            @pl.when(alone)
            def _():
                pot_s[...] = pot_p[half_rows, :]

            @pl.when(jnp.logical_not(alone))
            def _():
                moved = remote(
                    pots.at[0, last], pots.at[1, last], pot_send.at[last], pot_recv.at[last],
                    partner,
                )
                moved.wait_recv()
                moved.wait_send()
                pot_s[...] = pots[1, last]

        set_weights(lhs_s, fix_s, log_s[...] + pot_s[...] - sq_s[...])
        lse_pass(lhs_s, rhs_x, bufs, HALF, put_wide)
        py[it, y] = wide[...] - sq_x[...]
        spread(py, it, y, y_others, y_peer, py_send, py_recv)

        fz[it, zx] = collect(fy, it, y, y_others, y_peer, fy_send, fy_recv)
        spread(fz, it, zx, zx_others, zx_peer, fz_send, fz_recv)
        pz[it, zx] = collect(py, it, y, y_others, y_peer, py_send, py_recv)
        spread(pz, it, zx, zx_others, zx_peer, pz_send, pz_recv)
        pot_f = -TAU * collect(fz, it, zx, zx_others, zx_peer, fz_send, fz_recv)
        set_weights(lhs_x, fix_x, log_x[...] + pot_f - sq_x[...])

        @pl.when(it == ITERS - 1)
        def _():
            fin[0, z_lo] = pot_f * (1.0 / SCALE)
            remote(
                fin.at[0, z_lo], fin.at[0, z_lo], fin_send.at[0], fin_recv.at[0], twin
            ).start()

        lse_pass(lhs_x, rhs_y, bufs, GROUP, put_wide)
        gb[it, g] = wide[...] - sq_y[...]
        spread(gb, it, g, g_others, g_peer, gb_send, gb_recv)

        new_p = -TAU * collect(pz, it, zx, zx_others, zx_peer, pz_send, pz_recv)
        pot_p[...] = 0.5 * (pot_p[...] + new_p)

        @pl.when((it < ITERS - 1) & jnp.logical_not(alone))
        def _():
            pots[0, it] = pot_p[half_rows, :]
            remote(
                pots.at[0, it], pots.at[1, it], pot_send.at[it], pot_recv.at[it], partner
            ).start()

        @pl.when(it == ITERS - 1)
        def _():
            fin[1, z_lo] = pot_p[...] * (1.0 / SCALE)
            remote(
                fin.at[1, z_lo], fin.at[1, z_lo], fin_send.at[1], fin_recv.at[1], twin
            ).start()

        pot_g = -TAU * collect(gb, it, g, g_others, g_peer, gb_send, gb_recv)
        wide[...] = pot_g

        @pl.when(it < ITERS - 1)
        def _():
            set_weights(lhs_y, fix_y, log_y[...] + pot_g - sq_y[...])

        return carry

    lax.fori_loop(0, ITERS, iteration, 0)

    tgt_out[...] = wide[pl.ds(pl.multiple_of(z_lo * 8, 8), 8), :] * (1.0 / SCALE)
    for kind in range(2):
        remote(
            fin.at[kind, 1 - z_lo], fin.at[kind, 1 - z_lo], fin_send.at[kind], fin_recv.at[kind],
            twin,
        ).wait_recv()
        remote(
            fin.at[kind, z_lo], fin.at[kind, z_lo], fin_send.at[kind], fin_recv.at[kind], twin
        ).wait_send()
    src_out[0:16, :] = fin[0, 0]
    src_out[16:32, :] = fin[0, 1]
    self_out[0:16, :] = fin[1, 0]
    self_out[16:32, :] = fin[1, 1]


def on_device(
    src_features, src_mass, section_ids, shard_counts, section_offsets, tgt_features, tgt_mass
):
    vmem = pl.BlockSpec(memory_space=pltpu.VMEM)
    hbm = pl.BlockSpec(memory_space=pltpu.HBM)
    V, D = pltpu.VMEM, pltpu.SemaphoreType.DMA
    contributions = pl.pallas_call(
        relay_kernel,
        out_shape=jax.ShapeDtypeStruct((4, ROWS, GROUP), F32),
        in_specs=[pl.BlockSpec(memory_space=pltpu.SMEM)] + [hbm] * 4,
        out_specs=hbm,
        scratch_shapes=[
            V((ROWS, WIDTH), F32), V((COMPONENTS, CAP), F32), V((1, CAP), F32),
            V((1, CAP), jnp.int32), V((SECTIONS, COMPONENTS), F32), V((4, ROWS, GROUP), F32),
            D((4,)), D((3,)), D((4,)),
        ],
        compiler_params=pltpu.CompilerParams(vmem_limit_bytes=58 * 1024 * 1024),
    )(
        shard_counts,
        src_features,
        src_mass.reshape(1, CAP),
        section_ids.reshape(1, CAP),
        section_offsets.T,
    )
    rows16, rows8 = (16, 128), (8, 128)
    outs = pl.pallas_call(
        sinkhorn_kernel,
        out_shape=(
            jax.ShapeDtypeStruct((32, 128), F32),
            jax.ShapeDtypeStruct((8, 128), F32),
            jax.ShapeDtypeStruct((32, 128), F32),
        ),
        in_specs=[hbm, vmem, vmem],
        out_specs=(vmem, vmem, vmem),
        scratch_shapes=[
            V((2, ROWS, GROUP), F32),
            V((ROWS, GROUP), F32), V((ROWS, GROUP), F32), V((ROWS, GROUP), F32),
            V((ROWS, GROUP), F32), V((2, ROWS, HALF), F32), V((ROWS, GROUP), F32),
            V((ROWS, HALF), F32),
            V((GROUP, 256), BF16), V((GROUP, 256), BF16), V((HALF, 256), BF16),
            V((GROUP, 128), BF16), V((GROUP, 128), BF16), V((HALF, 128), BF16),
            V((256, GROUP), BF16), V((256, GROUP), BF16),
            V((GROUP, TILE), F32), V((GROUP, TILE), F32),
            V(rows16, F32), V(rows16, F32), V(rows8, F32),
            V(rows16, F32), V(rows16, F32), V(rows8, F32),
            V(rows16, F32), V(rows8, F32), V(rows16, F32),
            V((ITERS, 4) + rows16, F32), V((ITERS, 4) + rows16, F32),
            V((ITERS, 4) + rows16, F32), V((ITERS, 4) + rows16, F32),
            V((ITERS, 8) + rows16, F32), V((2, ITERS - 1) + rows8, F32),
            V((2, 2) + rows16, F32),
            D((4,)), D((4,)), D((4,)), D((4,)), D((2,)), D((2,)), D((2,)), D,
            D((ITERS, 4)), D((ITERS, 4)), D((ITERS, 4)), D((ITERS, 4)),
            D((ITERS, 4)), D((ITERS, 4)), D((ITERS, 4)), D((ITERS, 4)),
            D((ITERS, 8)), D((ITERS, 8)), D((ITERS,)), D((ITERS,)), D((2,)), D((2,)),
            D((2,)),
        ],
        compiler_params=pltpu.CompilerParams(
            collective_id=0, has_side_effects=True, vmem_limit_bytes=58 * 1024 * 1024
        ),
    )(contributions, tgt_features, tgt_mass.reshape(1, HALF))
    return (outs[0].reshape(2 * GROUP), outs[1].reshape(HALF), outs[2].reshape(2 * GROUP))


def solution(mesh):
    return jax.shard_map(
        on_device,
        mesh=mesh,
        in_specs=(P(None, "src"), P("src"), P("src"), P(), P(), P(None, "tgt"), P("tgt")),
        out_specs=(P("src"), P("tgt"), P("src")),
        check_vma=False,
    )
```

```python
import jax
import jax.numpy as jnp
from jax import lax
from jax.experimental import pallas as pl
from jax.experimental.pallas import tpu as pltpu
from jax.sharding import PartitionSpec as P

COMPONENTS = 50
ROWS = 56
SECTIONS = 32
ITERS = 3
CAP = 8192
GROUP = 2048
HALF = 1024
SPAN = GROUP + 128
LEAD = GROUP
WIDTH = LEAD + CAP + SPAN

EPS = 0.05
TAU = 1.0 / (1.0 + EPS)
LOG2E = 1.4426950408889634
SCALE = LOG2E / EPS

F32 = jnp.float32
BF16 = jnp.bfloat16
MESH = pl.DeviceIdType.MESH
TILE = 256
TILES = GROUP // TILE
CHUNK = 256


def place():
    src, tgt = lax.axis_index("src"), lax.axis_index("tgt")
    z, rest = lax.div(tgt, 8), lax.rem(tgt, 8)
    return (
        lax.div(src, 2),
        lax.rem(src, 2),
        lax.div(z, 2),
        lax.rem(z, 2),
        lax.div(rest, 2),
        lax.rem(rest, 2),
    )


def device(x_lo, core, z_hi, z_lo, y, x_hi):
    return (x_lo * 2 + core, (z_hi * 2 + z_lo) * 8 + y * 2 + x_hi)


def pieces(value):
    high = value.astype(BF16)
    rest = value - high.astype(F32)
    middle = rest.astype(BF16)
    return high, middle, (rest - middle.astype(F32)).astype(BF16)


def correct(feats_ref, mass_ref, ids_ref, offsets_ref, held, ready):
    three = jnp.concatenate([p.astype(F32) for p in pieces(offsets_ref[...])], axis=0).astype(BF16)
    for at in range(0, CAP, 1024):
        ready(at)
        ids = ids_ref[:, at : at + 1024]
        section = lax.rem(lax.broadcasted_iota(jnp.int32, (3 * SECTIONS, 1024), 0), SECTIONS)
        onehot = jnp.where(section == ids, 1.0, 0.0).astype(BF16)
        shift = lax.dot_general(
            three, onehot, (((0,), (0,)), ((), ())), preferred_element_type=F32
        )
        to = slice(LEAD + at, LEAD + at + 1024)
        held[48:ROWS, to] = jnp.zeros((ROWS - 48, 1024), F32)
        held[0:COMPONENTS, to] = feats_ref[:, at : at + 1024] - shift
        held[COMPONENTS : COMPONENTS + 1, to] = mass_ref[:, at : at + 1024]


def contribute(held, base, count, out):
    at = jnp.clip(base, -LEAD, CAP) + LEAD
    aligned = pl.multiple_of(lax.div(at, 128) * 128, 128)
    off = lax.rem(at, 128)
    turn = lax.rem(128 - off, 128)
    lane = lax.broadcasted_iota(jnp.int32, (ROWS, 128), 1)
    before = pltpu.roll(held[:, pl.ds(aligned, 128)], turn, 1)
    for t in range(GROUP // 128):
        after = pltpu.roll(
            held[:, pl.ds(pl.multiple_of(aligned + (t + 1) * 128, 128), 128)], turn, 1
        )
        value = jnp.where(lane < 128 - off, before, after)
        local = lane + (base + t * 128)
        out[:, t * 128 : (t + 1) * 128] = jnp.where((local >= 0) & (local < count), value, 0.0)
        before = after


def relay_kernel(
    counts_ref, feats_any, mass_any, ids_any, offsets_any, out_any,
    held, feats_ref, mass_ref, ids_ref, offsets_ref, out_ref, feats_sem, small_sem, out_sem,
):
    small = [
        pltpu.make_async_copy(a, b, small_sem.at[i])
        for i, (a, b) in enumerate(
            [(offsets_any, offsets_ref), (ids_any, ids_ref), (mass_any, mass_ref)]
        )
    ]
    large = [
        pltpu.make_async_copy(
            feats_any.at[:, at : at + 2048], feats_ref.at[:, at : at + 2048], feats_sem.at[i]
        )
        for i, at in enumerate(range(0, CAP, 2048))
    ]
    for copy in small + large:
        copy.start()
    x_lo, core, z_hi, z_lo, y, x_hi = place()
    mine = x_lo * 2 + core
    begin = jnp.int32(0)
    for k in range(3):
        begin = begin + jnp.where(k < mine, counts_ref[k], 0)
    count = counts_ref[mine]

    def ready(at):
        if at % 2048 == 0:
            large[at // 2048].wait()

    for copy in small:
        copy.wait()
    correct(feats_ref, mass_ref, ids_ref, offsets_ref, held, ready)
    moves = []
    for index in (3, 2, 1, 0):
        to_x, to_core = lax.rem(x_lo + index // 2, 2), lax.rem(core + index % 2, 2)
        base = (to_x * 2 + to_core) * (2 * GROUP) + z_lo * GROUP - begin
        contribute(held, base, count, out_ref.at[index])
        moves.append(
            pltpu.make_async_copy(out_ref.at[index], out_any.at[index], out_sem.at[index])
        )
        moves[-1].start()
    for copy in moves:
        copy.wait()


def log_sum(parts):
    peak = jnp.max(parts, axis=0)
    return peak + jnp.log2(jnp.sum(jnp.exp2(parts - peak[None]), axis=0))


def first_pass(lhs, rhs, cache, count, put):
    chunk = min(CHUNK, count)

    def both(j, peak):
        top, total = None, None
        for at in range(0, count, chunk):
            if j < TILES:
                s = jnp.dot(
                    lhs[at : at + chunk, :], rhs[:, j * TILE : (j + 1) * TILE],
                    preferred_element_type=F32,
                )
                cache[j, at : at + chunk, :] = s
                here = jnp.max(s, axis=0, keepdims=True)
                top = here if top is None else jnp.maximum(top, here)
            if peak is not None:
                e = jnp.exp2(cache[j - 1, at : at + chunk, :] - peak)
                part = jnp.sum(e, axis=0, keepdims=True)
                total = part if total is None else total + part
        if peak is not None:
            put(j - 1, peak + jnp.log2(total))
        return top

    peak = None
    for j in range(TILES + 1):
        peak = both(j, peak)


def row_pass(cache, weight, count, put):
    def body(j, carry):
        peak, total = [None, None], [None, None]
        for at in range(0, count, 128):
            w = weight[at : at + 128, :]
            for h in range(2):
                t = (cache[j, at : at + 128, h * 128 : (h + 1) * 128] + w).reshape(16, 8, 128)
                top = jnp.max(t, axis=0)
                if at:
                    top = jnp.maximum(top, peak[h])
                part = jnp.sum(jnp.exp2(t - top[None]), axis=0)
                if at:
                    part = part + total[h] * jnp.exp2(peak[h] - top)
                peak[h], total[h] = top, part
        ends = []
        for h in range(2):
            top = jnp.max(peak[h], axis=0, keepdims=True)
            part = jnp.sum(total[h] * jnp.exp2(peak[h] - top), axis=0, keepdims=True)
            ends.append(top + jnp.log2(part))
        put(j, jnp.concatenate(ends, axis=1))
        return carry

    lax.fori_loop(0, TILES, body, 0)


def column_pass(cache, weight, spread_w, peaks, totals, out):
    for r in range(16):
        spread_w[r] = jnp.broadcast_to(weight[r : r + 1, :], (8, 128))

    def body(block, carry):
        for sub in range(4):
            rows = pl.ds(pl.multiple_of(block * 64 + sub * 16, 16), 16)
            parts = []
            for r in range(16):
                lanes = slice(r % 2 * 128, r % 2 * 128 + 128)
                t = cache[r // 2, rows, lanes].reshape(2, 8, 128)
                parts.append(t + spread_w[r][None])
            tops = parts
            while len(tops) > 1:
                tops = [jnp.maximum(a, b) for a, b in zip(tops[0::2], tops[1::2])]
            sums = [jnp.exp2(t - tops[0]) for t in parts]
            while len(sums) > 1:
                sums = [a + b for a, b in zip(sums[0::2], sums[1::2])]
            peaks[rows, :] = tops[0].reshape(16, 128)
            totals[rows, :] = sums[0].reshape(16, 128)
        return carry

    lax.fori_loop(0, GROUP // 64, body, 0)
    for c in range(16):
        at = slice(c * 128, (c + 1) * 128)
        turned = peaks[at, :].T
        top = jnp.max(turned, axis=0, keepdims=True)
        total = jnp.sum(totals[at, :].T * jnp.exp2(turned - top), axis=0, keepdims=True)
        out[c : c + 1, :] = top + jnp.log2(total)


def spread_rows(wide_w, weight):
    for c in range(weight.shape[0]):
        wide_w[c * 128 : (c + 1) * 128, :] = jnp.broadcast_to(weight[c : c + 1, :], (128, 128)).T


def to_rows(ref, row):
    for r in range(row.shape[1] // 128):
        ref[r : r + 1, :] = row[:, r * 128 : (r + 1) * 128]


def set_weights(lhs, fixed, weight):
    rows = weight.shape[0]
    parts = [p.astype(F32) for p in pieces(weight)]
    stacked = jnp.concatenate(parts + [jnp.zeros((128 - 3 * rows, 128), F32)], axis=0)
    turned = stacked.T
    lane = lax.rem(lax.broadcasted_iota(jnp.int32, (128, 128), 1), rows)
    for c in range(rows):
        at = slice(c * 128, (c + 1) * 128)
        lhs[at, 128:256] = jnp.where(lane == c, turned, 0.0).astype(BF16) + fixed[at, :]


def set_left(lhs, fixed, one, two, three):
    zero = jnp.zeros((64, 128), F32)
    for c in range(one.shape[1] // 128):
        at = slice(c * 128, (c + 1) * 128)
        first = jnp.concatenate([one[:, at].astype(F32), two[:, at].astype(F32)], axis=0)
        second = jnp.concatenate([zero, three[:, at].astype(F32)], axis=0)
        lhs[at, 0:128] = first.T.astype(BF16)
        fixed[at, :] = second.T.astype(BF16)


def set_right(rhs, one, two, three):
    rhs[0:64, :] = one
    rhs[64:128, :] = two
    row = lax.broadcasted_iota(jnp.int32, (64, GROUP), 0)
    rhs[128:192, :] = jnp.where(row < 48, 1.0, 0.0).astype(BF16)
    rhs[192:256, :] = three


def padded(cells, centre):
    row = lax.broadcasted_iota(jnp.int32, cells.shape, 0)
    kept = jnp.where(row < COMPONENTS, cells - centre, 0.0)
    return jnp.concatenate([kept, jnp.zeros((64 - ROWS, cells.shape[1]), F32)], axis=0)


def sinkhorn_kernel(
    con_any, tgt_ref, tgt_mass_ref,
    src_out, tgt_out, self_out,
    con_ref,
    from_own, from_opp, opp, landed, ybuf, xfull, sbuf,
    lhs_y, lhs_s, fix_y, fix_s, rhs_x, cache_f, cache_p,
    spread_w, peaks, totals, wide_g, wide_s,
    sq_x, sq_y, sq_s, log_x, log_y, log_s, pot_p, pot_s, wide,
    fy, fz, py, pz, gb, pots, fin,
    relay_send, relay_recv, opp_send, opp_recv, own_sem, tgt_sem, self_sem, local_sem,
    fy_send, fy_recv, fz_send, fz_recv, py_send, py_recv, pz_send, pz_recv,
    gb_send, gb_recv, pot_send, pot_recv, fin_send, fin_recv, con_sem,
):
    loads = [
        pltpu.make_async_copy(con_any.at[2 * i], con_ref.at[i], con_sem.at[i]) for i in range(2)
    ]
    for copy in loads:
        copy.start()
    x_lo, core, z_hi, z_lo, y, x_hi = place()
    sibling = device(x_lo, 1 - core, z_hi, z_lo, y, x_hi)
    twin = device(x_lo, core, z_hi, 1 - z_lo, y, x_hi)
    across = device(1 - x_lo, core, z_hi, z_lo, y, 1 - x_hi)
    straight = lax.rem(x_lo + core, 2)
    opposite = device(1 - x_lo, core, z_hi, z_lo, y, lax.rem(x_hi + straight, 2))
    y_hi, y_lo = lax.div(y, 2), lax.rem(y, 2)
    partner = device(
        lax.rem(x_lo + y_hi, 2), lax.rem(core + y_lo, 2), z_hi, lax.rem(z_lo + z_hi, 2), y, x_hi
    )
    alone = (y + z_hi) == 0
    g = x_lo * 4 + core * 2 + z_lo
    zx = z_hi * 2 + x_hi

    def y_peer(k):
        return device(x_lo, core, z_hi, z_lo, k, x_hi)

    def zx_peer(k):
        return device(x_lo, core, lax.div(k, 2), z_lo, y, lax.rem(k, 2))

    def g_peer(k):
        return device(lax.div(k, 4), lax.rem(lax.div(k, 2), 2), z_hi, lax.rem(k, 2), y, x_hi)

    y_others = [lax.rem(y + d, 4) for d in range(1, 4)]
    zx_others = [lax.rem(zx + d, 4) for d in range(1, 4)]
    g_others = [lax.rem(g + d, 8) for d in range(1, 8)]

    barrier = pltpu.get_barrier_semaphore()
    peers = [y_peer(k) for k in y_others] + [zx_peer(k) for k in zx_others]
    peers += [g_peer(k) for k in g_others] + [across]
    for peer in peers:
        pl.semaphore_signal(barrier, inc=1, device_id=peer, device_id_type=MESH)

    ybuf[z_lo, 48:ROWS, :] = jnp.zeros((ROWS - 48, HALF), F32)
    ybuf[z_lo, 0:COMPONENTS, :] = tgt_ref[...]
    ybuf[z_lo, COMPONENTS : COMPONENTS + 1, :] = tgt_mass_ref[...]

    pl.semaphore_wait(barrier, len(peers))

    def remote(src, dst, send, recv, to):
        return pltpu.make_async_remote_copy(
            src_ref=src, dst_ref=dst, send_sem=send, recv_sem=recv, device_id=to,
            device_id_type=MESH,
        )

    parts = [slice(c * 512, (c + 1) * 512) for c in range(4)]
    relays = [
        remote(con_any.at[3, :, s], from_opp.at[:, s], relay_send.at[c], relay_recv.at[c], sibling)
        for c, s in enumerate(parts)
    ]
    own = remote(con_any.at[1], from_own, own_sem.at[0], own_sem.at[1], sibling)
    tgt = remote(ybuf.at[z_lo], ybuf.at[z_lo], tgt_sem.at[0], tgt_sem.at[1], twin)
    tgt.start()

    for copy in relays:
        copy.start()
    own.start()
    onward = [
        remote(opp.at[:, s], landed.at[:, s], opp_send.at[c], opp_recv.at[c], opposite)
        for c, s in enumerate(parts)
    ]
    loads[1].wait()
    for c, s in enumerate(parts):
        relays[c].wait_recv()
        opp[:, s] = con_ref[1, :, s] + from_opp[:, s]
        onward[c].start()

    remote(ybuf.at[1 - z_lo], ybuf.at[1 - z_lo], tgt_sem.at[0], tgt_sem.at[1], twin).wait_recv()
    cells = jnp.concatenate([ybuf[0], ybuf[1]], axis=1)
    centre = jnp.sum(cells, axis=1, keepdims=True) * (1.0 / GROUP)
    kept = padded(cells, centre)
    to_rows(sq_y, jnp.sum(kept * kept, axis=0, keepdims=True) * SCALE)
    to_rows(log_y, jnp.log2(cells[COMPONENTS : COMPONENTS + 1, :]))
    high, middle, unused = pieces(kept)
    set_left(lhs_y, fix_y, high, high, middle)
    set_weights(lhs_y, fix_y, log_y[...] - sq_y[...])

    loads[0].wait()
    own.wait_recv()
    for copy in onward:
        copy.wait_recv()
    cells = con_ref[0] + from_own[...] + landed[...]
    xfull[...] = cells
    half = pl.ds(pl.multiple_of(x_hi * HALF, HALF), HALF)
    shared = remote(xfull.at[:, half], sbuf, self_sem.at[0], self_sem.at[1], partner)
    kept_here = pltpu.make_async_copy(xfull.at[:, half], sbuf, local_sem)

    @pl.when(alone)
    def _():
        kept_here.start()

    @pl.when(jnp.logical_not(alone))
    def _():
        shared.start()

    kept = padded(cells, centre)
    to_rows(sq_x, jnp.sum(kept * kept, axis=0, keepdims=True) * SCALE)
    to_rows(log_x, jnp.log2(cells[COMPONENTS : COMPONENTS + 1, :]))
    high, middle, unused = pieces(kept * (2.0 * SCALE))
    set_right(rhs_x, high, middle, high)
    for copy in relays + onward + [own, tgt]:
        copy.wait_send()

    pot_p[...] = jnp.zeros_like(pot_p)
    pot_s[...] = jnp.zeros_like(pot_s)

    def put_wide(j, value):
        for r in range(TILE // 128):
            wide[pl.ds(TILE // 128 * j + r, 1), :] = value[:, r * 128 : (r + 1) * 128]

    def spread(box, it, me, others, peer, send, recv):
        for k in others:
            remote(box.at[it, me], box.at[it, me], send.at[it, k], recv.at[it, me], peer(k)).start()

    def collect(box, it, me, others, peer, send, recv):
        for k in others:
            remote(box.at[it, k], box.at[it, k], send.at[it, k], recv.at[it, k], peer(k)).wait_recv()
        for k in others:
            remote(box.at[it, me], box.at[it, me], send.at[it, k], recv.at[it, me], peer(k)).wait_send()
        return log_sum(box[it])

    half_rows = pl.ds(pl.multiple_of(x_hi * 8, 8), 8)

    def iteration(it, carry):
        @pl.when(it == 0)
        def _():
            first_pass(lhs_y, rhs_x, cache_f, GROUP, put_wide)

        @pl.when(it > 0)
        def _():
            row_pass(cache_f, wide_g, GROUP, put_wide)

        fy[it, y] = wide[...] - sq_x[...]
        spread(fy, it, y, y_others, y_peer, fy_send, fy_recv)

        @pl.when(it == 0)
        def _():
            @pl.when(alone)
            def _():
                kept_here.wait()

            @pl.when(jnp.logical_not(alone))
            def _():
                shared.wait_recv()
                shared.wait_send()

            got = sbuf[...]
            columns = padded(got, centre)
            to_rows(sq_s, jnp.sum(columns * columns, axis=0, keepdims=True) * SCALE)
            to_rows(log_s, jnp.log2(got[COMPONENTS : COMPONENTS + 1, :]))
            upper, lower, unused = pieces(columns)
            set_left(lhs_s, fix_s, upper, upper, lower)
            set_weights(lhs_s, fix_s, log_s[...] - sq_s[...])
            first_pass(lhs_s, rhs_x, cache_p, HALF, put_wide)

        @pl.when(it > 0)
        def _():
            last = it - 1

            @pl.when(alone)
            def _():
                pot_s[...] = pot_p[half_rows, :]

            @pl.when(jnp.logical_not(alone))
            def _():
                moved = remote(
                    pots.at[0, last], pots.at[1, last], pot_send.at[last], pot_recv.at[last],
                    partner,
                )
                moved.wait_recv()
                moved.wait_send()
                pot_s[...] = pots[1, last]

            spread_rows(wide_s, pot_s[...])
            row_pass(cache_p, wide_s, HALF, put_wide)

        py[it, y] = wide[...] - sq_x[...]
        spread(py, it, y, y_others, y_peer, py_send, py_recv)

        fz[it, zx] = collect(fy, it, y, y_others, y_peer, fy_send, fy_recv)
        spread(fz, it, zx, zx_others, zx_peer, fz_send, fz_recv)
        pz[it, zx] = collect(py, it, y, y_others, y_peer, py_send, py_recv)
        spread(pz, it, zx, zx_others, zx_peer, pz_send, pz_recv)
        pot_f = -TAU * collect(fz, it, zx, zx_others, zx_peer, fz_send, fz_recv)
        @pl.when(it == ITERS - 1)
        def _():
            fin[0, z_lo] = pot_f * (1.0 / SCALE)
            remote(
                fin.at[0, z_lo], fin.at[0, z_lo], fin_send.at[0], fin_recv.at[0], twin
            ).start()

        column_pass(cache_f, log_x[...] + pot_f - sq_x[...], spread_w, peaks, totals, wide)
        gb[it, g] = wide[...] - log_y[...]
        spread(gb, it, g, g_others, g_peer, gb_send, gb_recv)

        new_p = -TAU * collect(pz, it, zx, zx_others, zx_peer, pz_send, pz_recv)
        pot_p[...] = 0.5 * (pot_p[...] + new_p)

        @pl.when((it < ITERS - 1) & jnp.logical_not(alone))
        def _():
            pots[0, it] = pot_p[half_rows, :]
            remote(
                pots.at[0, it], pots.at[1, it], pot_send.at[it], pot_recv.at[it], partner
            ).start()

        @pl.when(it == ITERS - 1)
        def _():
            fin[1, z_lo] = pot_p[...] * (1.0 / SCALE)
            remote(
                fin.at[1, z_lo], fin.at[1, z_lo], fin_send.at[1], fin_recv.at[1], twin
            ).start()

        pot_g = -TAU * collect(gb, it, g, g_others, g_peer, gb_send, gb_recv)
        wide[...] = pot_g

        @pl.when(it < ITERS - 1)
        def _():
            spread_rows(wide_g, pot_g)

        return carry

    lax.fori_loop(0, ITERS, iteration, 0)

    tgt_out[...] = wide[pl.ds(pl.multiple_of(z_lo * 8, 8), 8), :] * (1.0 / SCALE)
    for kind in range(2):
        remote(
            fin.at[kind, 1 - z_lo], fin.at[kind, 1 - z_lo], fin_send.at[kind], fin_recv.at[kind],
            twin,
        ).wait_recv()
        remote(
            fin.at[kind, z_lo], fin.at[kind, z_lo], fin_send.at[kind], fin_recv.at[kind], twin
        ).wait_send()
    src_out[0:16, :] = fin[0, 0]
    src_out[16:32, :] = fin[0, 1]
    self_out[0:16, :] = fin[1, 0]
    self_out[16:32, :] = fin[1, 1]


def on_device(
    src_features, src_mass, section_ids, shard_counts, section_offsets, tgt_features, tgt_mass
):
    vmem = pl.BlockSpec(memory_space=pltpu.VMEM)
    hbm = pl.BlockSpec(memory_space=pltpu.HBM)
    V, D = pltpu.VMEM, pltpu.SemaphoreType.DMA
    contributions = pl.pallas_call(
        relay_kernel,
        out_shape=jax.ShapeDtypeStruct((4, ROWS, GROUP), F32),
        in_specs=[pl.BlockSpec(memory_space=pltpu.SMEM)] + [hbm] * 4,
        out_specs=hbm,
        scratch_shapes=[
            V((ROWS, WIDTH), F32), V((COMPONENTS, CAP), F32), V((1, CAP), F32),
            V((1, CAP), jnp.int32), V((SECTIONS, COMPONENTS), F32), V((4, ROWS, GROUP), F32),
            D((4,)), D((3,)), D((4,)),
        ],
        compiler_params=pltpu.CompilerParams(vmem_limit_bytes=58 * 1024 * 1024),
    )(
        shard_counts,
        src_features,
        src_mass.reshape(1, CAP),
        section_ids.reshape(1, CAP),
        section_offsets.T,
    )
    rows16, rows8 = (16, 128), (8, 128)
    outs = pl.pallas_call(
        sinkhorn_kernel,
        out_shape=(
            V((32, 128), F32), V((8, 128), F32), V((32, 128), F32),
        ),
        in_specs=[hbm, vmem, vmem],
        out_specs=(vmem, vmem, vmem),
        scratch_shapes=[
            V((2, ROWS, GROUP), F32),
            V((ROWS, GROUP), F32), V((ROWS, GROUP), F32), V((ROWS, GROUP), F32),
            V((ROWS, GROUP), F32), V((2, ROWS, HALF), F32), V((ROWS, GROUP), F32),
            V((ROWS, HALF), F32),
            V((GROUP, 256), BF16), V((HALF, 256), BF16),
            V((GROUP, 128), BF16), V((HALF, 128), BF16), V((256, GROUP), BF16),
            V((TILES, GROUP, TILE), F32), V((TILES, HALF, TILE), F32),
            V((16, 8, 128), F32), V((GROUP, 128), F32), V((GROUP, 128), F32),
            V((GROUP, 128), F32), V((HALF, 128), F32),
            V(rows16, F32), V(rows16, F32), V(rows8, F32),
            V(rows16, F32), V(rows16, F32), V(rows8, F32),
            V(rows16, F32), V(rows8, F32), V(rows16, F32),
            V((ITERS, 4) + rows16, F32), V((ITERS, 4) + rows16, F32),
            V((ITERS, 4) + rows16, F32), V((ITERS, 4) + rows16, F32),
            V((ITERS, 8) + rows16, F32), V((2, ITERS - 1) + rows8, F32),
            V((2, 2) + rows16, F32),
            D((4,)), D((4,)), D((4,)), D((4,)), D((2,)), D((2,)), D((2,)), D,
            D((ITERS, 4)), D((ITERS, 4)), D((ITERS, 4)), D((ITERS, 4)),
            D((ITERS, 4)), D((ITERS, 4)), D((ITERS, 4)), D((ITERS, 4)),
            D((ITERS, 8)), D((ITERS, 8)), D((ITERS,)), D((ITERS,)), D((2,)), D((2,)),
            D((2,)),
        ],
        compiler_params=pltpu.CompilerParams(
            collective_id=0, has_side_effects=True, vmem_limit_bytes=58 * 1024 * 1024
        ),
    )(contributions, tgt_features, tgt_mass.reshape(1, HALF))
    return (outs[0].reshape(2 * GROUP), outs[1].reshape(HALF), outs[2].reshape(2 * GROUP))


def solution(mesh):
    return jax.shard_map(
        on_device,
        mesh=mesh,
        in_specs=(P(None, "src"), P("src"), P("src"), P(), P(), P(None, "tgt"), P("tgt")),
        out_specs=(P("src"), P("tgt"), P("src")),
        check_vma=False,
    )
```

```python
import jax
import jax.numpy as jnp
from jax import lax
from jax.experimental import pallas as pl
from jax.experimental.pallas import tpu as pltpu
from jax.sharding import PartitionSpec as P

COMPONENTS = 50
ROWS = 56
SECTIONS = 32
ITERS = 3
CAP = 8192
GROUP = 2048
HALF = 1024
SPAN = GROUP + 128
LEAD = GROUP
WIDTH = LEAD + CAP + SPAN

EPS = 0.05
TAU = 1.0 / (1.0 + EPS)
LOG2E = 1.4426950408889634
SCALE = LOG2E / EPS

F32 = jnp.float32
BF16 = jnp.bfloat16
MESH = pl.DeviceIdType.MESH
TILE = 256
TILES = GROUP // TILE
CHUNK = 256


def place():
    src, tgt = lax.axis_index("src"), lax.axis_index("tgt")
    z, rest = lax.div(tgt, 8), lax.rem(tgt, 8)
    return (
        lax.div(src, 2),
        lax.rem(src, 2),
        lax.div(z, 2),
        lax.rem(z, 2),
        lax.div(rest, 2),
        lax.rem(rest, 2),
    )


def device(x_lo, core, z_hi, z_lo, y, x_hi):
    return (x_lo * 2 + core, (z_hi * 2 + z_lo) * 8 + y * 2 + x_hi)


def pieces(value):
    high = value.astype(BF16)
    rest = value - high.astype(F32)
    middle = rest.astype(BF16)
    return high, middle, (rest - middle.astype(F32)).astype(BF16)


def correct(feats_ref, mass_ref, ids_ref, offsets_ref, held, ready):
    three = jnp.concatenate([p.astype(F32) for p in pieces(offsets_ref[...])], axis=0).astype(BF16)
    for at in range(0, CAP, 1024):
        ready(at)
        ids = ids_ref[:, at : at + 1024]
        section = lax.rem(lax.broadcasted_iota(jnp.int32, (3 * SECTIONS, 1024), 0), SECTIONS)
        onehot = jnp.where(section == ids, 1.0, 0.0).astype(BF16)
        shift = lax.dot_general(
            three, onehot, (((0,), (0,)), ((), ())), preferred_element_type=F32
        )
        to = slice(LEAD + at, LEAD + at + 1024)
        held[48:ROWS, to] = jnp.zeros((ROWS - 48, 1024), F32)
        held[0:COMPONENTS, to] = feats_ref[:, at : at + 1024] - shift
        held[COMPONENTS : COMPONENTS + 1, to] = mass_ref[:, at : at + 1024]


def contribute(held, base, count, out):
    at = jnp.clip(base, -LEAD, CAP) + LEAD
    aligned = pl.multiple_of(lax.div(at, 128) * 128, 128)
    off = lax.rem(at, 128)
    turn = lax.rem(128 - off, 128)
    lane = lax.broadcasted_iota(jnp.int32, (ROWS, 128), 1)
    before = pltpu.roll(held[:, pl.ds(aligned, 128)], turn, 1)
    for t in range(GROUP // 128):
        after = pltpu.roll(
            held[:, pl.ds(pl.multiple_of(aligned + (t + 1) * 128, 128), 128)], turn, 1
        )
        value = jnp.where(lane < 128 - off, before, after)
        local = lane + (base + t * 128)
        out[:, t * 128 : (t + 1) * 128] = jnp.where((local >= 0) & (local < count), value, 0.0)
        before = after


def relay_kernel(
    counts_ref, feats_any, mass_any, ids_any, offsets_any, out_any,
    held, feats_ref, mass_ref, ids_ref, offsets_ref, out_ref, feats_sem, small_sem, out_sem,
):
    small = [
        pltpu.make_async_copy(a, b, small_sem.at[i])
        for i, (a, b) in enumerate(
            [(offsets_any, offsets_ref), (ids_any, ids_ref), (mass_any, mass_ref)]
        )
    ]
    large = [
        pltpu.make_async_copy(
            feats_any.at[:, at : at + 2048], feats_ref.at[:, at : at + 2048], feats_sem.at[i]
        )
        for i, at in enumerate(range(0, CAP, 2048))
    ]
    for copy in small + large:
        copy.start()
    x_lo, core, z_hi, z_lo, y, x_hi = place()
    mine = x_lo * 2 + core
    begin = jnp.int32(0)
    for k in range(3):
        begin = begin + jnp.where(k < mine, counts_ref[k], 0)
    count = counts_ref[mine]

    def ready(at):
        if at % 2048 == 0:
            large[at // 2048].wait()

    for copy in small:
        copy.wait()
    correct(feats_ref, mass_ref, ids_ref, offsets_ref, held, ready)
    moves = []
    for index in (3, 2, 1, 0):
        to_x, to_core = lax.rem(x_lo + index // 2, 2), lax.rem(core + index % 2, 2)
        base = (to_x * 2 + to_core) * (2 * GROUP) + z_lo * GROUP - begin
        contribute(held, base, count, out_ref.at[index])
        moves.append(
            pltpu.make_async_copy(out_ref.at[index], out_any.at[index], out_sem.at[index])
        )
        moves[-1].start()
    for copy in moves:
        copy.wait()


def log_sum(parts):
    peak = jnp.max(parts, axis=0)
    return peak + jnp.log2(jnp.sum(jnp.exp2(parts - peak[None]), axis=0))


def first_pass(lhs, rhs, cache, count, put):
    chunk = min(CHUNK, count)

    def both(j, peak):
        top, total = None, None
        for at in range(0, count, chunk):
            if j < TILES:
                s = jnp.dot(
                    lhs[at : at + chunk, :], rhs[:, j * TILE : (j + 1) * TILE],
                    preferred_element_type=F32,
                )
                cache[j, at : at + chunk, :] = s
                here = jnp.max(s, axis=0, keepdims=True)
                top = here if top is None else jnp.maximum(top, here)
            if peak is not None:
                e = jnp.exp2(cache[j - 1, at : at + chunk, :] - peak)
                part = jnp.sum(e, axis=0, keepdims=True)
                total = part if total is None else total + part
        if peak is not None:
            put(j - 1, peak + jnp.log2(total))
        return top

    peak = None
    for j in range(TILES + 1):
        peak = both(j, peak)


def row_pass(cache, weight, count, put):
    def body(j, carry):
        peak, total = [None, None], [None, None]
        for at in range(0, count, 128):
            w = weight[at : at + 128, :]
            for h in range(2):
                t = (cache[j, at : at + 128, h * 128 : (h + 1) * 128] + w).reshape(16, 8, 128)
                top = jnp.max(t, axis=0)
                if at:
                    top = jnp.maximum(top, peak[h])
                part = jnp.sum(jnp.exp2(t - top[None]), axis=0)
                if at:
                    part = part + total[h] * jnp.exp2(peak[h] - top)
                peak[h], total[h] = top, part
        ends = []
        for h in range(2):
            top = jnp.max(peak[h], axis=0, keepdims=True)
            part = jnp.sum(total[h] * jnp.exp2(peak[h] - top), axis=0, keepdims=True)
            ends.append(top + jnp.log2(part))
        put(j, jnp.concatenate(ends, axis=1))
        return carry

    lax.fori_loop(0, TILES, body, 0)


def column_pass(cache, weight, spread_w, peaks, totals, out):
    for r in range(16):
        spread_w[r] = jnp.broadcast_to(weight[r : r + 1, :], (8, 128))

    def body(block, carry):
        for sub in range(4):
            rows = pl.ds(pl.multiple_of(block * 64 + sub * 16, 16), 16)
            parts = []
            for r in range(16):
                lanes = slice(r % 2 * 128, r % 2 * 128 + 128)
                t = cache[r // 2, rows, lanes].reshape(2, 8, 128)
                parts.append(t + spread_w[r][None])
            tops = parts
            while len(tops) > 1:
                tops = [jnp.maximum(a, b) for a, b in zip(tops[0::2], tops[1::2])]
            sums = [jnp.exp2(t - tops[0]) for t in parts]
            while len(sums) > 1:
                sums = [a + b for a, b in zip(sums[0::2], sums[1::2])]
            peaks[rows, :] = tops[0].reshape(16, 128)
            totals[rows, :] = sums[0].reshape(16, 128)
        return carry

    lax.fori_loop(0, GROUP // 64, body, 0)
    for c in range(16):
        at = slice(c * 128, (c + 1) * 128)
        turned = peaks[at, :].T
        top = jnp.max(turned, axis=0, keepdims=True)
        total = jnp.sum(totals[at, :].T * jnp.exp2(turned - top), axis=0, keepdims=True)
        out[c : c + 1, :] = top + jnp.log2(total)


def spread_rows(wide_w, weight):
    for c in range(weight.shape[0]):
        wide_w[c * 128 : (c + 1) * 128, :] = jnp.broadcast_to(weight[c : c + 1, :], (128, 128)).T


def to_rows(ref, row):
    for r in range(row.shape[1] // 128):
        ref[r : r + 1, :] = row[:, r * 128 : (r + 1) * 128]


def set_weights(lhs, fixed, weight):
    rows = weight.shape[0]
    parts = [p.astype(F32) for p in pieces(weight)]
    stacked = jnp.concatenate(parts + [jnp.zeros((128 - 3 * rows, 128), F32)], axis=0)
    turned = stacked.T
    lane = lax.rem(lax.broadcasted_iota(jnp.int32, (128, 128), 1), rows)
    for c in range(rows):
        at = slice(c * 128, (c + 1) * 128)
        lhs[at, 128:256] = jnp.where(lane == c, turned, 0.0).astype(BF16) + fixed[at, :]


def set_left(lhs, fixed, one, two, three):
    zero = jnp.zeros((64, 128), F32)
    for c in range(one.shape[1] // 128):
        at = slice(c * 128, (c + 1) * 128)
        first = jnp.concatenate([one[:, at].astype(F32), two[:, at].astype(F32)], axis=0)
        second = jnp.concatenate([zero, three[:, at].astype(F32)], axis=0)
        lhs[at, 0:128] = first.T.astype(BF16)
        fixed[at, :] = second.T.astype(BF16)


def set_right(rhs, one, two, three):
    rhs[0:64, :] = one
    rhs[64:128, :] = two
    row = lax.broadcasted_iota(jnp.int32, (64, GROUP), 0)
    rhs[128:192, :] = jnp.where(row < 48, 1.0, 0.0).astype(BF16)
    rhs[192:256, :] = three


def padded(cells, centre):
    row = lax.broadcasted_iota(jnp.int32, cells.shape, 0)
    kept = jnp.where(row < COMPONENTS, cells - centre, 0.0)
    return jnp.concatenate([kept, jnp.zeros((64 - ROWS, cells.shape[1]), F32)], axis=0)


def sinkhorn_kernel(
    con_any, tgt_ref, tgt_mass_ref,
    src_out, tgt_out, self_out,
    con_ref,
    from_own, from_opp, opp, landed, ybuf, xfull, sbuf,
    lhs_y, lhs_s, fix_y, fix_s, rhs_x, cache_f, cache_p,
    spread_w, peaks, totals, wide_g, wide_s,
    sq_x, sq_y, sq_s, log_x, log_y, log_s, pot_p, pot_s, wide,
    fb, pb, gb, pots, fin,
    relay_send, relay_recv, opp_send, opp_recv, own_sem, tgt_sem, self_sem, local_sem,
    fb_send, fb_recv, pb_send, pb_recv,
    gb_send, gb_recv, pot_send, pot_recv, fin_send, fin_recv, con_sem,
):
    loads = [
        pltpu.make_async_copy(con_any.at[2 * i], con_ref.at[i], con_sem.at[i]) for i in range(2)
    ]
    for copy in loads:
        copy.start()
    x_lo, core, z_hi, z_lo, y, x_hi = place()
    sibling = device(x_lo, 1 - core, z_hi, z_lo, y, x_hi)
    twin = device(x_lo, core, z_hi, 1 - z_lo, y, x_hi)
    across = device(1 - x_lo, core, z_hi, z_lo, y, 1 - x_hi)
    straight = lax.rem(x_lo + core, 2)
    opposite = device(1 - x_lo, core, z_hi, z_lo, y, lax.rem(x_hi + straight, 2))
    y_hi, y_lo = lax.div(y, 2), lax.rem(y, 2)
    partner = device(
        lax.rem(x_lo + y_hi, 2), lax.rem(core + y_lo, 2), z_hi, lax.rem(z_lo + z_hi, 2), y, x_hi
    )
    alone = (y + z_hi) == 0
    g = x_lo * 4 + core * 2 + z_lo
    m = z_hi * 8 + y * 2 + x_hi

    def m_peer(k):
        return device(x_lo, core, lax.div(k, 8), z_lo, lax.rem(lax.div(k, 2), 4), lax.rem(k, 2))

    def g_peer(k):
        return device(lax.div(k, 4), lax.rem(lax.div(k, 2), 2), z_hi, lax.rem(k, 2), y, x_hi)

    m_others = [lax.rem(m + d, 16) for d in range(1, 16)]
    g_others = [lax.rem(g + d, 8) for d in range(1, 8)]

    barrier = pltpu.get_barrier_semaphore()
    peers = [m_peer(k) for k in m_others]
    peers += [g_peer(k) for k in g_others] + [across]
    for peer in peers:
        pl.semaphore_signal(barrier, inc=1, device_id=peer, device_id_type=MESH)

    ybuf[z_lo, 48:ROWS, :] = jnp.zeros((ROWS - 48, HALF), F32)
    ybuf[z_lo, 0:COMPONENTS, :] = tgt_ref[...]
    ybuf[z_lo, COMPONENTS : COMPONENTS + 1, :] = tgt_mass_ref[...]

    pl.semaphore_wait(barrier, len(peers))

    def remote(src, dst, send, recv, to):
        return pltpu.make_async_remote_copy(
            src_ref=src, dst_ref=dst, send_sem=send, recv_sem=recv, device_id=to,
            device_id_type=MESH,
        )

    parts = [slice(c * 512, (c + 1) * 512) for c in range(4)]
    relays = [
        remote(con_any.at[3, :, s], from_opp.at[:, s], relay_send.at[c], relay_recv.at[c], sibling)
        for c, s in enumerate(parts)
    ]
    own = remote(con_any.at[1], from_own, own_sem.at[0], own_sem.at[1], sibling)
    tgt = remote(ybuf.at[z_lo], ybuf.at[z_lo], tgt_sem.at[0], tgt_sem.at[1], twin)
    tgt.start()

    for copy in relays:
        copy.start()
    own.start()
    onward = [
        remote(opp.at[:, s], landed.at[:, s], opp_send.at[c], opp_recv.at[c], opposite)
        for c, s in enumerate(parts)
    ]
    loads[1].wait()
    for c, s in enumerate(parts):
        relays[c].wait_recv()
        opp[:, s] = con_ref[1, :, s] + from_opp[:, s]
        onward[c].start()

    remote(ybuf.at[1 - z_lo], ybuf.at[1 - z_lo], tgt_sem.at[0], tgt_sem.at[1], twin).wait_recv()
    cells = jnp.concatenate([ybuf[0], ybuf[1]], axis=1)
    centre = jnp.sum(cells, axis=1, keepdims=True) * (1.0 / GROUP)
    kept = padded(cells, centre)
    to_rows(sq_y, jnp.sum(kept * kept, axis=0, keepdims=True) * SCALE)
    to_rows(log_y, jnp.log2(cells[COMPONENTS : COMPONENTS + 1, :]))
    high, middle, unused = pieces(kept)
    set_left(lhs_y, fix_y, high, high, middle)
    set_weights(lhs_y, fix_y, log_y[...] - sq_y[...])

    loads[0].wait()
    own.wait_recv()
    for copy in onward:
        copy.wait_recv()
    cells = con_ref[0] + from_own[...] + landed[...]
    xfull[...] = cells
    half = pl.ds(pl.multiple_of(x_hi * HALF, HALF), HALF)
    shared = remote(xfull.at[:, half], sbuf, self_sem.at[0], self_sem.at[1], partner)
    kept_here = pltpu.make_async_copy(xfull.at[:, half], sbuf, local_sem)

    @pl.when(alone)
    def _():
        kept_here.start()

    @pl.when(jnp.logical_not(alone))
    def _():
        shared.start()

    kept = padded(cells, centre)
    to_rows(sq_x, jnp.sum(kept * kept, axis=0, keepdims=True) * SCALE)
    to_rows(log_x, jnp.log2(cells[COMPONENTS : COMPONENTS + 1, :]))
    high, middle, unused = pieces(kept * (2.0 * SCALE))
    set_right(rhs_x, high, middle, high)
    for copy in relays + onward + [own, tgt]:
        copy.wait_send()

    pot_p[...] = jnp.zeros_like(pot_p)
    pot_s[...] = jnp.zeros_like(pot_s)

    def put_wide(j, value):
        for r in range(TILE // 128):
            wide[pl.ds(TILE // 128 * j + r, 1), :] = value[:, r * 128 : (r + 1) * 128]

    def spread(box, it, me, others, peer, send, recv):
        for k in others:
            remote(box.at[it, me], box.at[it, me], send.at[it, k], recv.at[it, me], peer(k)).start()

    def collect(box, it, me, others, peer, send, recv):
        for k in others:
            remote(box.at[it, k], box.at[it, k], send.at[it, k], recv.at[it, k], peer(k)).wait_recv()
        for k in others:
            remote(box.at[it, me], box.at[it, me], send.at[it, k], recv.at[it, me], peer(k)).wait_send()
        return log_sum(box[it])

    half_rows = pl.ds(pl.multiple_of(x_hi * 8, 8), 8)

    def iteration(it, carry):
        @pl.when(it == 0)
        def _():
            first_pass(lhs_y, rhs_x, cache_f, GROUP, put_wide)

        @pl.when(it > 0)
        def _():
            row_pass(cache_f, wide_g, GROUP, put_wide)

        fb[it, m] = wide[...] - sq_x[...]
        spread(fb, it, m, m_others, m_peer, fb_send, fb_recv)

        @pl.when(it == 0)
        def _():
            @pl.when(alone)
            def _():
                kept_here.wait()

            @pl.when(jnp.logical_not(alone))
            def _():
                shared.wait_recv()
                shared.wait_send()

            got = sbuf[...]
            columns = padded(got, centre)
            to_rows(sq_s, jnp.sum(columns * columns, axis=0, keepdims=True) * SCALE)
            to_rows(log_s, jnp.log2(got[COMPONENTS : COMPONENTS + 1, :]))
            upper, lower, unused = pieces(columns)
            set_left(lhs_s, fix_s, upper, upper, lower)
            set_weights(lhs_s, fix_s, log_s[...] - sq_s[...])
            first_pass(lhs_s, rhs_x, cache_p, HALF, put_wide)

        @pl.when(it > 0)
        def _():
            last = it - 1

            @pl.when(alone)
            def _():
                pot_s[...] = pot_p[half_rows, :]

            @pl.when(jnp.logical_not(alone))
            def _():
                moved = remote(
                    pots.at[0, last], pots.at[1, last], pot_send.at[last], pot_recv.at[last],
                    partner,
                )
                moved.wait_recv()
                moved.wait_send()
                pot_s[...] = pots[1, last]

            spread_rows(wide_s, pot_s[...])
            row_pass(cache_p, wide_s, HALF, put_wide)

        pb[it, m] = wide[...] - sq_x[...]
        spread(pb, it, m, m_others, m_peer, pb_send, pb_recv)

        pot_f = -TAU * collect(fb, it, m, m_others, m_peer, fb_send, fb_recv)
        @pl.when(it == ITERS - 1)
        def _():
            fin[0, z_lo] = pot_f * (1.0 / SCALE)
            remote(
                fin.at[0, z_lo], fin.at[0, z_lo], fin_send.at[0], fin_recv.at[0], twin
            ).start()

        column_pass(cache_f, log_x[...] + pot_f - sq_x[...], spread_w, peaks, totals, wide)
        gb[it, g] = wide[...] - log_y[...]
        spread(gb, it, g, g_others, g_peer, gb_send, gb_recv)

        new_p = -TAU * collect(pb, it, m, m_others, m_peer, pb_send, pb_recv)
        pot_p[...] = 0.5 * (pot_p[...] + new_p)

        @pl.when((it < ITERS - 1) & jnp.logical_not(alone))
        def _():
            pots[0, it] = pot_p[half_rows, :]
            remote(
                pots.at[0, it], pots.at[1, it], pot_send.at[it], pot_recv.at[it], partner
            ).start()

        @pl.when(it == ITERS - 1)
        def _():
            fin[1, z_lo] = pot_p[...] * (1.0 / SCALE)
            remote(
                fin.at[1, z_lo], fin.at[1, z_lo], fin_send.at[1], fin_recv.at[1], twin
            ).start()

        pot_g = -TAU * collect(gb, it, g, g_others, g_peer, gb_send, gb_recv)
        wide[...] = pot_g

        @pl.when(it < ITERS - 1)
        def _():
            spread_rows(wide_g, pot_g)

        return carry

    lax.fori_loop(0, ITERS, iteration, 0)

    tgt_out[...] = wide[pl.ds(pl.multiple_of(z_lo * 8, 8), 8), :] * (1.0 / SCALE)
    for kind in range(2):
        remote(
            fin.at[kind, 1 - z_lo], fin.at[kind, 1 - z_lo], fin_send.at[kind], fin_recv.at[kind],
            twin,
        ).wait_recv()
        remote(
            fin.at[kind, z_lo], fin.at[kind, z_lo], fin_send.at[kind], fin_recv.at[kind], twin
        ).wait_send()
    src_out[0:16, :] = fin[0, 0]
    src_out[16:32, :] = fin[0, 1]
    self_out[0:16, :] = fin[1, 0]
    self_out[16:32, :] = fin[1, 1]


def on_device(
    src_features, src_mass, section_ids, shard_counts, section_offsets, tgt_features, tgt_mass
):
    vmem = pl.BlockSpec(memory_space=pltpu.VMEM)
    hbm = pl.BlockSpec(memory_space=pltpu.HBM)
    V, D = pltpu.VMEM, pltpu.SemaphoreType.DMA
    contributions = pl.pallas_call(
        relay_kernel,
        out_shape=jax.ShapeDtypeStruct((4, ROWS, GROUP), F32),
        in_specs=[pl.BlockSpec(memory_space=pltpu.SMEM)] + [hbm] * 4,
        out_specs=hbm,
        scratch_shapes=[
            V((ROWS, WIDTH), F32), V((COMPONENTS, CAP), F32), V((1, CAP), F32),
            V((1, CAP), jnp.int32), V((SECTIONS, COMPONENTS), F32), V((4, ROWS, GROUP), F32),
            D((4,)), D((3,)), D((4,)),
        ],
        compiler_params=pltpu.CompilerParams(vmem_limit_bytes=58 * 1024 * 1024),
    )(
        shard_counts,
        src_features,
        src_mass.reshape(1, CAP),
        section_ids.reshape(1, CAP),
        section_offsets.T,
    )
    rows16, rows8 = (16, 128), (8, 128)
    outs = pl.pallas_call(
        sinkhorn_kernel,
        out_shape=(
            V((32, 128), F32), V((8, 128), F32), V((32, 128), F32),
        ),
        in_specs=[hbm, vmem, vmem],
        out_specs=(vmem, vmem, vmem),
        scratch_shapes=[
            V((2, ROWS, GROUP), F32),
            V((ROWS, GROUP), F32), V((ROWS, GROUP), F32), V((ROWS, GROUP), F32),
            V((ROWS, GROUP), F32), V((2, ROWS, HALF), F32), V((ROWS, GROUP), F32),
            V((ROWS, HALF), F32),
            V((GROUP, 256), BF16), V((HALF, 256), BF16),
            V((GROUP, 128), BF16), V((HALF, 128), BF16), V((256, GROUP), BF16),
            V((TILES, GROUP, TILE), F32), V((TILES, HALF, TILE), F32),
            V((16, 8, 128), F32), V((GROUP, 128), F32), V((GROUP, 128), F32),
            V((GROUP, 128), F32), V((HALF, 128), F32),
            V(rows16, F32), V(rows16, F32), V(rows8, F32),
            V(rows16, F32), V(rows16, F32), V(rows8, F32),
            V(rows16, F32), V(rows8, F32), V(rows16, F32),
            V((ITERS, 16) + rows16, F32), V((ITERS, 16) + rows16, F32),
            V((ITERS, 8) + rows16, F32), V((2, ITERS - 1) + rows8, F32),
            V((2, 2) + rows16, F32),
            D((4,)), D((4,)), D((4,)), D((4,)), D((2,)), D((2,)), D((2,)), D,
            D((ITERS, 16)), D((ITERS, 16)), D((ITERS, 16)), D((ITERS, 16)),
            D((ITERS, 8)), D((ITERS, 8)), D((ITERS,)), D((ITERS,)), D((2,)), D((2,)),
            D((2,)),
        ],
        compiler_params=pltpu.CompilerParams(
            collective_id=0, has_side_effects=True, vmem_limit_bytes=58 * 1024 * 1024
        ),
    )(contributions, tgt_features, tgt_mass.reshape(1, HALF))
    return (outs[0].reshape(2 * GROUP), outs[1].reshape(HALF), outs[2].reshape(2 * GROUP))


def solution(mesh):
    return jax.shard_map(
        on_device,
        mesh=mesh,
        in_specs=(P(None, "src"), P("src"), P("src"), P(), P(), P(None, "tgt"), P("tgt")),
        out_specs=(P("src"), P("tgt"), P("src")),
        check_vma=False,
    )
```

```python
import jax
import jax.numpy as jnp
from jax import lax
from jax.experimental import pallas as pl
from jax.experimental.pallas import tpu as pltpu
from jax.sharding import PartitionSpec as P

COMPONENTS = 50
ROWS = 56
SECTIONS = 32
ITERS = 3
CAP = 8192
GROUP = 2048
HALF = 1024
SPAN = GROUP + 128
LEAD = GROUP
WIDTH = LEAD + CAP + SPAN

EPS = 0.05
TAU = 1.0 / (1.0 + EPS)
LOG2E = 1.4426950408889634
SCALE = LOG2E / EPS

F32 = jnp.float32
BF16 = jnp.bfloat16
MESH = pl.DeviceIdType.MESH
TILE = 256
TILES = GROUP // TILE
CHUNK = 256


def place():
    src, tgt = lax.axis_index("src"), lax.axis_index("tgt")
    z, rest = lax.div(tgt, 8), lax.rem(tgt, 8)
    return (
        lax.div(src, 2),
        lax.rem(src, 2),
        lax.div(z, 2),
        lax.rem(z, 2),
        lax.div(rest, 2),
        lax.rem(rest, 2),
    )


def device(x_lo, core, z_hi, z_lo, y, x_hi):
    return (x_lo * 2 + core, (z_hi * 2 + z_lo) * 8 + y * 2 + x_hi)


def pieces(value):
    high = value.astype(BF16)
    rest = value - high.astype(F32)
    middle = rest.astype(BF16)
    return high, middle, (rest - middle.astype(F32)).astype(BF16)


def correct(feats_ref, mass_ref, ids_ref, offsets_ref, held, ready):
    three = jnp.concatenate([p.astype(F32) for p in pieces(offsets_ref[...])], axis=0).astype(BF16)
    for at in range(0, CAP, 1024):
        ready(at)
        ids = ids_ref[:, at : at + 1024]
        section = lax.rem(lax.broadcasted_iota(jnp.int32, (3 * SECTIONS, 1024), 0), SECTIONS)
        onehot = jnp.where(section == ids, 1.0, 0.0).astype(BF16)
        shift = lax.dot_general(
            three, onehot, (((0,), (0,)), ((), ())), preferred_element_type=F32
        )
        to = slice(LEAD + at, LEAD + at + 1024)
        held[48:ROWS, to] = jnp.zeros((ROWS - 48, 1024), F32)
        held[0:COMPONENTS, to] = feats_ref[:, at : at + 1024] - shift
        held[COMPONENTS : COMPONENTS + 1, to] = mass_ref[:, at : at + 1024]


def contribute(held, base, count, out):
    at = jnp.clip(base, -LEAD, CAP) + LEAD
    aligned = pl.multiple_of(lax.div(at, 128) * 128, 128)
    off = lax.rem(at, 128)
    turn = lax.rem(128 - off, 128)
    lane = lax.broadcasted_iota(jnp.int32, (ROWS, 128), 1)
    before = pltpu.roll(held[:, pl.ds(aligned, 128)], turn, 1)
    for t in range(GROUP // 128):
        after = pltpu.roll(
            held[:, pl.ds(pl.multiple_of(aligned + (t + 1) * 128, 128), 128)], turn, 1
        )
        value = jnp.where(lane < 128 - off, before, after)
        local = lane + (base + t * 128)
        out[:, t * 128 : (t + 1) * 128] = jnp.where((local >= 0) & (local < count), value, 0.0)
        before = after


def relay_kernel(
    counts_ref, feats_any, mass_any, ids_any, offsets_any, out_any,
    held, feats_ref, mass_ref, ids_ref, offsets_ref, out_ref, feats_sem, small_sem, out_sem,
):
    small = [
        pltpu.make_async_copy(a, b, small_sem.at[i])
        for i, (a, b) in enumerate(
            [(offsets_any, offsets_ref), (ids_any, ids_ref), (mass_any, mass_ref)]
        )
    ]
    large = [
        pltpu.make_async_copy(
            feats_any.at[:, at : at + 2048], feats_ref.at[:, at : at + 2048], feats_sem.at[i]
        )
        for i, at in enumerate(range(0, CAP, 2048))
    ]
    for copy in small + large:
        copy.start()
    x_lo, core, z_hi, z_lo, y, x_hi = place()
    mine = x_lo * 2 + core
    begin = jnp.int32(0)
    for k in range(3):
        begin = begin + jnp.where(k < mine, counts_ref[k], 0)
    count = counts_ref[mine]

    def ready(at):
        if at % 2048 == 0:
            large[at // 2048].wait()

    for copy in small:
        copy.wait()
    correct(feats_ref, mass_ref, ids_ref, offsets_ref, held, ready)
    moves = []
    for index in (3, 2, 1, 0):
        to_x, to_core = lax.rem(x_lo + index // 2, 2), lax.rem(core + index % 2, 2)
        base = (to_x * 2 + to_core) * (2 * GROUP) + z_lo * GROUP - begin
        contribute(held, base, count, out_ref.at[index])
        moves.append(
            pltpu.make_async_copy(out_ref.at[index], out_any.at[index], out_sem.at[index])
        )
        moves[-1].start()
    for copy in moves:
        copy.wait()


def log_sum(parts):
    peak = jnp.max(parts, axis=0)
    return peak + jnp.log2(jnp.sum(jnp.exp2(parts - peak[None]), axis=0))


def first_pass(lhs, rhs, cache, count, put, ready=None):
    chunk = min(CHUNK, count)

    def both(j, peak):
        top, total = None, None
        for at in range(0, count, chunk):
            if j < TILES:
                s = jnp.dot(
                    lhs[at : at + chunk, :], rhs[:, j * TILE : (j + 1) * TILE],
                    preferred_element_type=F32,
                )
                cache[j, at : at + chunk, :] = s
                here = jnp.max(s, axis=0, keepdims=True)
                top = here if top is None else jnp.maximum(top, here)
            if peak is not None:
                e = jnp.exp2(cache[j - 1, at : at + chunk, :] - peak)
                part = jnp.sum(e, axis=0, keepdims=True)
                total = part if total is None else total + part
        if peak is not None:
            put(j - 1, peak + jnp.log2(total))
        return top

    peak = None
    for j in range(TILES + 1):
        if ready is not None and j < TILES:
            ready(j)
        peak = both(j, peak)


def row_pass(cache, weight, count, put):
    def body(j, carry):
        peak, total = [None, None], [None, None]
        for at in range(0, count, 128):
            w = weight[at : at + 128, :]
            for h in range(2):
                t = (cache[j, at : at + 128, h * 128 : (h + 1) * 128] + w).reshape(16, 8, 128)
                top = jnp.max(t, axis=0)
                if at:
                    top = jnp.maximum(top, peak[h])
                part = jnp.sum(jnp.exp2(t - top[None]), axis=0)
                if at:
                    part = part + total[h] * jnp.exp2(peak[h] - top)
                peak[h], total[h] = top, part
        ends = []
        for h in range(2):
            top = jnp.max(peak[h], axis=0, keepdims=True)
            part = jnp.sum(total[h] * jnp.exp2(peak[h] - top), axis=0, keepdims=True)
            ends.append(top + jnp.log2(part))
        put(j, jnp.concatenate(ends, axis=1))
        return carry

    lax.fori_loop(0, TILES, body, 0)


def column_pass(cache, weight, spread_w, peaks, totals, out):
    for r in range(16):
        spread_w[r] = jnp.broadcast_to(weight[r : r + 1, :], (8, 128))

    def body(block, carry):
        for sub in range(4):
            rows = pl.ds(pl.multiple_of(block * 64 + sub * 16, 16), 16)
            parts = []
            for r in range(16):
                lanes = slice(r % 2 * 128, r % 2 * 128 + 128)
                t = cache[r // 2, rows, lanes].reshape(2, 8, 128)
                parts.append(t + spread_w[r][None])
            tops = parts
            while len(tops) > 1:
                tops = [jnp.maximum(a, b) for a, b in zip(tops[0::2], tops[1::2])]
            sums = [jnp.exp2(t - tops[0]) for t in parts]
            while len(sums) > 1:
                sums = [a + b for a, b in zip(sums[0::2], sums[1::2])]
            peaks[rows, :] = tops[0].reshape(16, 128)
            totals[rows, :] = sums[0].reshape(16, 128)
        return carry

    lax.fori_loop(0, GROUP // 64, body, 0)
    for c in range(16):
        at = slice(c * 128, (c + 1) * 128)
        turned = peaks[at, :].T
        top = jnp.max(turned, axis=0, keepdims=True)
        total = jnp.sum(totals[at, :].T * jnp.exp2(turned - top), axis=0, keepdims=True)
        out[c : c + 1, :] = top + jnp.log2(total)


def spread_rows(wide_w, weight):
    for c in range(weight.shape[0]):
        wide_w[c * 128 : (c + 1) * 128, :] = jnp.broadcast_to(weight[c : c + 1, :], (128, 128)).T


def to_rows(ref, row, first=0):
    for r in range(row.shape[1] // 128):
        ref[first + r : first + r + 1, :] = row[:, r * 128 : (r + 1) * 128]


def set_weights(lhs, fixed, weight):
    rows = weight.shape[0]
    parts = [p.astype(F32) for p in pieces(weight)]
    stacked = jnp.concatenate(parts + [jnp.zeros((128 - 3 * rows, 128), F32)], axis=0)
    turned = stacked.T
    lane = lax.rem(lax.broadcasted_iota(jnp.int32, (128, 128), 1), rows)
    for c in range(rows):
        at = slice(c * 128, (c + 1) * 128)
        lhs[at, 128:256] = jnp.where(lane == c, turned, 0.0).astype(BF16) + fixed[at, :]


def set_left(lhs, fixed, one, two, three):
    zero = jnp.zeros((64, 128), F32)
    for c in range(one.shape[1] // 128):
        at = slice(c * 128, (c + 1) * 128)
        first = jnp.concatenate([one[:, at].astype(F32), two[:, at].astype(F32)], axis=0)
        second = jnp.concatenate([zero, three[:, at].astype(F32)], axis=0)
        lhs[at, 0:128] = first.T.astype(BF16)
        fixed[at, :] = second.T.astype(BF16)


def set_right(rhs, at, one, two, three):
    rhs[0:64, at] = one
    rhs[64:128, at] = two
    row = lax.broadcasted_iota(jnp.int32, three.shape, 0)
    rhs[128:192, at] = jnp.where(row < 48, 1.0, 0.0).astype(BF16)
    rhs[192:256, at] = three


def padded(cells, centre):
    row = lax.broadcasted_iota(jnp.int32, cells.shape, 0)
    kept = jnp.where(row < COMPONENTS, cells - centre, 0.0)
    return jnp.concatenate([kept, jnp.zeros((64 - ROWS, cells.shape[1]), F32)], axis=0)


def sinkhorn_kernel(
    con_any, tgt_any, tgt_mass_any,
    src_out, tgt_out, self_out,
    con_ref, tgt_ref, tgt_mass_ref,
    from_own, from_opp, opp, landed, ybuf, xfull, sbuf,
    lhs_y, lhs_s, fix_y, fix_s, rhs_x, cache_f, cache_p,
    spread_w, peaks, totals, wide_g, wide_s,
    sq_x, sq_y, sq_s, log_x, log_y, log_s, pot_p, pot_s, wide,
    fb, pb, gb, pots, fin,
    relay_send, relay_recv, opp_send, opp_recv, own_sem, tgt_sem, self_sem, local_sem,
    fb_send, fb_recv, pb_send, pb_recv,
    gb_send, gb_recv, pot_send, pot_recv, fin_send, fin_recv, con_sem,
):
    x_lo, core, z_hi, z_lo, y, x_hi = place()
    sibling = device(x_lo, 1 - core, z_hi, z_lo, y, x_hi)
    twin = device(x_lo, core, z_hi, 1 - z_lo, y, x_hi)
    across = device(1 - x_lo, core, z_hi, z_lo, y, 1 - x_hi)
    straight = lax.rem(x_lo + core, 2)
    opposite = device(1 - x_lo, core, z_hi, z_lo, y, lax.rem(x_hi + straight, 2))
    y_hi, y_lo = lax.div(y, 2), lax.rem(y, 2)
    partner = device(
        lax.rem(x_lo + y_hi, 2), lax.rem(core + y_lo, 2), z_hi, lax.rem(z_lo + z_hi, 2), y, x_hi
    )
    alone = (y + z_hi) == 0
    g = x_lo * 4 + core * 2 + z_lo
    m = z_hi * 8 + y * 2 + x_hi

    def m_peer(k):
        return device(x_lo, core, lax.div(k, 8), z_lo, lax.rem(lax.div(k, 2), 4), lax.rem(k, 2))

    def g_peer(k):
        return device(lax.div(k, 4), lax.rem(lax.div(k, 2), 2), z_hi, lax.rem(k, 2), y, x_hi)

    m_others = [lax.rem(m + d, 16) for d in range(1, 16)]
    g_others = [lax.rem(g + d, 8) for d in range(1, 8)]

    barrier = pltpu.get_barrier_semaphore()
    peers = [m_peer(k) for k in m_others]
    peers += [g_peer(k) for k in g_others] + [across]
    for peer in peers:
        pl.semaphore_signal(barrier, inc=1, device_id=peer, device_id_type=MESH)

    loads = [
        pltpu.make_async_copy(a, b, con_sem.at[i])
        for i, (a, b) in enumerate(
            [
                (tgt_any, tgt_ref),
                (tgt_mass_any, tgt_mass_ref),
                (con_any.at[2], con_ref.at[1]),
                (con_any.at[0], con_ref.at[0]),
            ]
        )
    ]
    for copy in loads:
        copy.start()
    loads[0].wait()
    loads[1].wait()
    ybuf[z_lo, 48:ROWS, :] = jnp.zeros((ROWS - 48, HALF), F32)
    ybuf[z_lo, 0:COMPONENTS, :] = tgt_ref[...]
    ybuf[z_lo, COMPONENTS : COMPONENTS + 1, :] = tgt_mass_ref[...]

    pl.semaphore_wait(barrier, len(peers))

    def remote(src, dst, send, recv, to):
        return pltpu.make_async_remote_copy(
            src_ref=src, dst_ref=dst, send_sem=send, recv_sem=recv, device_id=to,
            device_id_type=MESH,
        )

    parts = [slice(c * 512, (c + 1) * 512) for c in range(4)]
    relays = [
        remote(con_any.at[3, :, s], from_opp.at[:, s], relay_send.at[c], relay_recv.at[c], sibling)
        for c, s in enumerate(parts)
    ]
    own = remote(con_any.at[1], from_own, own_sem.at[0], own_sem.at[1], sibling)
    tgt = remote(ybuf.at[z_lo], ybuf.at[z_lo], tgt_sem.at[0], tgt_sem.at[1], twin)
    tgt.start()

    for copy in relays:
        copy.start()
    own.start()
    onward = [
        remote(opp.at[:, s], landed.at[:, s], opp_send.at[c], opp_recv.at[c], opposite)
        for c, s in enumerate(parts)
    ]
    loads[2].wait()
    for c, s in enumerate(parts):
        relays[c].wait_recv()
        opp[:, s] = con_ref[1, :, s] + from_opp[:, s]
        onward[c].start()

    remote(ybuf.at[1 - z_lo], ybuf.at[1 - z_lo], tgt_sem.at[0], tgt_sem.at[1], twin).wait_recv()
    cells = jnp.concatenate([ybuf[0], ybuf[1]], axis=1)
    centre = jnp.sum(cells, axis=1, keepdims=True) * (1.0 / GROUP)
    kept = padded(cells, centre)
    to_rows(sq_y, jnp.sum(kept * kept, axis=0, keepdims=True) * SCALE)
    to_rows(log_y, jnp.log2(cells[COMPONENTS : COMPONENTS + 1, :]))
    high, middle, unused = pieces(kept)
    set_left(lhs_y, fix_y, high, high, middle)
    set_weights(lhs_y, fix_y, log_y[...] - sq_y[...])

    def put_wide(j, value):
        for r in range(TILE // 128):
            wide[pl.ds(TILE // 128 * j + r, 1), :] = value[:, r * 128 : (r + 1) * 128]

    loads[3].wait()
    own.wait_recv()

    def arrive(j):
        if j % 2:
            return
        c = j // 2
        s = parts[c]
        onward[c].wait_recv()
        cells = con_ref[0, :, s] + from_own[:, s] + landed[:, s]
        xfull[:, s] = cells
        kept = padded(cells, centre)
        to_rows(sq_x, jnp.sum(kept * kept, axis=0, keepdims=True) * SCALE, 4 * c)
        to_rows(log_x, jnp.log2(cells[COMPONENTS : COMPONENTS + 1, :]), 4 * c)
        high, middle, unused = pieces(kept * (2.0 * SCALE))
        set_right(rhs_x, s, high, middle, high)

    first_pass(lhs_y, rhs_x, cache_f, GROUP, put_wide, arrive)
    half = pl.ds(pl.multiple_of(x_hi * HALF, HALF), HALF)
    shared = remote(xfull.at[:, half], sbuf, self_sem.at[0], self_sem.at[1], partner)
    kept_here = pltpu.make_async_copy(xfull.at[:, half], sbuf, local_sem)

    @pl.when(alone)
    def _():
        kept_here.start()

    @pl.when(jnp.logical_not(alone))
    def _():
        shared.start()

    pot_p[...] = jnp.zeros_like(pot_p)
    pot_s[...] = jnp.zeros_like(pot_s)

    def spread(box, it, me, others, peer, send, recv):
        for k in others:
            remote(box.at[it, me], box.at[it, me], send.at[it], recv.at[it], peer(k)).start()

    def all_of(box, it, others, peer, send, recv):
        part = box.at[it, pl.ds(0, len(others))]
        return remote(part, part, send.at[it], recv.at[it], peer(others[0]))

    to_m, to_g = (m_others, m_peer), (g_others, g_peer)

    half_rows = pl.ds(pl.multiple_of(x_hi * 8, 8), 8)

    def iteration(it, carry):
        @pl.when(it > 0)
        def _():
            row_pass(cache_f, wide_g, GROUP, put_wide)

        fb[it, m] = wide[...] - sq_x[...]
        spread(fb, it, m, *to_m, fb_send, fb_recv)

        @pl.when(it == 0)
        def _():
            @pl.when(alone)
            def _():
                kept_here.wait()

            @pl.when(jnp.logical_not(alone))
            def _():
                shared.wait_recv()
                shared.wait_send()

            for copy in relays + onward + [own, tgt]:
                copy.wait_send()
            got = sbuf[...]
            columns = padded(got, centre)
            to_rows(sq_s, jnp.sum(columns * columns, axis=0, keepdims=True) * SCALE)
            to_rows(log_s, jnp.log2(got[COMPONENTS : COMPONENTS + 1, :]))
            upper, lower, unused = pieces(columns)
            set_left(lhs_s, fix_s, upper, upper, lower)
            set_weights(lhs_s, fix_s, log_s[...] - sq_s[...])
            first_pass(lhs_s, rhs_x, cache_p, HALF, put_wide)

        @pl.when(it > 0)
        def _():
            last = it - 1

            @pl.when(alone)
            def _():
                pot_s[...] = pot_p[half_rows, :]

            @pl.when(jnp.logical_not(alone))
            def _():
                moved = remote(
                    pots.at[0, last], pots.at[1, last], pot_send.at[last], pot_recv.at[last],
                    partner,
                )
                moved.wait_recv()
                moved.wait_send()
                pot_s[...] = pots[1, last]

            spread_rows(wide_s, pot_s[...])
            row_pass(cache_p, wide_s, HALF, put_wide)

        pb[it, m] = wide[...] - sq_x[...]
        spread(pb, it, m, *to_m, pb_send, pb_recv)

        all_of(fb, it, *to_m, fb_send, fb_recv).wait_recv()
        pot_f = -TAU * log_sum(fb[it])
        @pl.when(it == ITERS - 1)
        def _():
            fin[0, z_lo] = pot_f * (1.0 / SCALE)
            remote(
                fin.at[0, z_lo], fin.at[0, z_lo], fin_send.at[0], fin_recv.at[0], twin
            ).start()

        column_pass(cache_f, log_x[...] + pot_f - sq_x[...], spread_w, peaks, totals, wide)
        gb[it, g] = wide[...] - log_y[...]
        spread(gb, it, g, *to_g, gb_send, gb_recv)

        all_of(pb, it, *to_m, pb_send, pb_recv).wait_recv()
        new_p = -TAU * log_sum(pb[it])
        pot_p[...] = 0.5 * (pot_p[...] + new_p)

        @pl.when((it < ITERS - 1) & jnp.logical_not(alone))
        def _():
            pots[0, it] = pot_p[half_rows, :]
            remote(
                pots.at[0, it], pots.at[1, it], pot_send.at[it], pot_recv.at[it], partner
            ).start()

        @pl.when(it == ITERS - 1)
        def _():
            fin[1, z_lo] = pot_p[...] * (1.0 / SCALE)
            remote(
                fin.at[1, z_lo], fin.at[1, z_lo], fin_send.at[1], fin_recv.at[1], twin
            ).start()

        all_of(fb, it, *to_m, fb_send, fb_recv).wait_send()
        all_of(pb, it, *to_m, pb_send, pb_recv).wait_send()
        all_of(gb, it, *to_g, gb_send, gb_recv).wait_send()
        all_of(gb, it, *to_g, gb_send, gb_recv).wait_recv()
        pot_g = -TAU * log_sum(gb[it])
        wide[...] = pot_g

        @pl.when(it < ITERS - 1)
        def _():
            spread_rows(wide_g, pot_g)

        return carry

    lax.fori_loop(0, ITERS, iteration, 0)

    tgt_out[...] = wide[pl.ds(pl.multiple_of(z_lo * 8, 8), 8), :] * (1.0 / SCALE)
    for kind in range(2):
        remote(
            fin.at[kind, 1 - z_lo], fin.at[kind, 1 - z_lo], fin_send.at[kind], fin_recv.at[kind],
            twin,
        ).wait_recv()
        remote(
            fin.at[kind, z_lo], fin.at[kind, z_lo], fin_send.at[kind], fin_recv.at[kind], twin
        ).wait_send()
    src_out[0:16, :] = fin[0, 0]
    src_out[16:32, :] = fin[0, 1]
    self_out[0:16, :] = fin[1, 0]
    self_out[16:32, :] = fin[1, 1]


def on_device(
    src_features, src_mass, section_ids, shard_counts, section_offsets, tgt_features, tgt_mass
):
    vmem = pl.BlockSpec(memory_space=pltpu.VMEM)
    hbm = pl.BlockSpec(memory_space=pltpu.HBM)
    V, D = pltpu.VMEM, pltpu.SemaphoreType.DMA
    contributions = pl.pallas_call(
        relay_kernel,
        out_shape=jax.ShapeDtypeStruct((4, ROWS, GROUP), F32),
        in_specs=[pl.BlockSpec(memory_space=pltpu.SMEM)] + [hbm] * 4,
        out_specs=hbm,
        scratch_shapes=[
            V((ROWS, WIDTH), F32), V((COMPONENTS, CAP), F32), V((1, CAP), F32),
            V((1, CAP), jnp.int32), V((SECTIONS, COMPONENTS), F32), V((4, ROWS, GROUP), F32),
            D((4,)), D((3,)), D((4,)),
        ],
        compiler_params=pltpu.CompilerParams(vmem_limit_bytes=58 * 1024 * 1024),
    )(
        shard_counts,
        src_features,
        src_mass.reshape(1, CAP),
        section_ids.reshape(1, CAP),
        section_offsets.T,
    )
    rows16, rows8 = (16, 128), (8, 128)
    outs = pl.pallas_call(
        sinkhorn_kernel,
        out_shape=(
            V((32, 128), F32), V((8, 128), F32), V((32, 128), F32),
        ),
        in_specs=[hbm] * 3,
        out_specs=(vmem, vmem, vmem),
        scratch_shapes=[
            V((2, ROWS, GROUP), F32), V((COMPONENTS, HALF), F32), V((1, HALF), F32),
            V((ROWS, GROUP), F32), V((ROWS, GROUP), F32), V((ROWS, GROUP), F32),
            V((ROWS, GROUP), F32), V((2, ROWS, HALF), F32), V((ROWS, GROUP), F32),
            V((ROWS, HALF), F32),
            V((GROUP, 256), BF16), V((HALF, 256), BF16),
            V((GROUP, 128), BF16), V((HALF, 128), BF16), V((256, GROUP), BF16),
            V((TILES, GROUP, TILE), F32), V((TILES, HALF, TILE), F32),
            V((16, 8, 128), F32), V((GROUP, 128), F32), V((GROUP, 128), F32),
            V((GROUP, 128), F32), V((HALF, 128), F32),
            V(rows16, F32), V(rows16, F32), V(rows8, F32),
            V(rows16, F32), V(rows16, F32), V(rows8, F32),
            V(rows16, F32), V(rows8, F32), V(rows16, F32),
            V((ITERS, 16) + rows16, F32), V((ITERS, 16) + rows16, F32),
            V((ITERS, 8) + rows16, F32), V((2, ITERS - 1) + rows8, F32),
            V((2, 2) + rows16, F32),
            D((4,)), D((4,)), D((4,)), D((4,)), D((2,)), D((2,)), D((2,)), D,
            D((ITERS,)), D((ITERS,)), D((ITERS,)), D((ITERS,)), D((ITERS,)), D((ITERS,)),
            D((ITERS,)), D((ITERS,)), D((2,)), D((2,)),
            D((4,)),
        ],
        compiler_params=pltpu.CompilerParams(
            collective_id=0, has_side_effects=True, vmem_limit_bytes=58 * 1024 * 1024
        ),
    )(contributions, tgt_features, tgt_mass.reshape(1, HALF))
    return (outs[0].reshape(2 * GROUP), outs[1].reshape(HALF), outs[2].reshape(2 * GROUP))


def solution(mesh):
    return jax.shard_map(
        on_device,
        mesh=mesh,
        in_specs=(P(None, "src"), P("src"), P("src"), P(), P(), P(None, "tgt"), P("tgt")),
        out_specs=(P("src"), P("tgt"), P("src")),
        check_vma=False,
    )
```

```python
import jax
import jax.numpy as jnp
from jax import lax
from jax.experimental import pallas as pl
from jax.experimental.pallas import tpu as pltpu
from jax.sharding import PartitionSpec as P

COMPONENTS = 50
ROWS = 56
SECTIONS = 32
ITERS = 3
CAP = 8192
GROUP = 2048
HALF = 1024
SPAN = GROUP + 128
LEAD = GROUP
WIDTH = LEAD + CAP + SPAN

EPS = 0.05
TAU = 1.0 / (1.0 + EPS)
LOG2E = 1.4426950408889634
SCALE = LOG2E / EPS

F32 = jnp.float32
BF16 = jnp.bfloat16
MESH = pl.DeviceIdType.MESH
TILE = 256
TILES = GROUP // TILE
CHUNK = 256


def place():
    src, tgt = lax.axis_index("src"), lax.axis_index("tgt")
    z, rest = lax.div(tgt, 8), lax.rem(tgt, 8)
    return (
        lax.div(src, 2),
        lax.rem(src, 2),
        lax.div(z, 2),
        lax.rem(z, 2),
        lax.div(rest, 2),
        lax.rem(rest, 2),
    )


def device(x_lo, core, z_hi, z_lo, y, x_hi):
    return (x_lo * 2 + core, (z_hi * 2 + z_lo) * 8 + y * 2 + x_hi)


def pieces(value):
    high = value.astype(BF16)
    rest = value - high.astype(F32)
    middle = rest.astype(BF16)
    return high, middle, (rest - middle.astype(F32)).astype(BF16)


def correct(feats_ref, mass_ref, ids_ref, offsets_ref, held, ready):
    three = jnp.concatenate([p.astype(F32) for p in pieces(offsets_ref[...])], axis=0).astype(BF16)
    for at in range(0, CAP, 1024):
        ready(at)
        ids = ids_ref[:, at : at + 1024]
        section = lax.rem(lax.broadcasted_iota(jnp.int32, (3 * SECTIONS, 1024), 0), SECTIONS)
        onehot = jnp.where(section == ids, 1.0, 0.0).astype(BF16)
        shift = lax.dot_general(
            three, onehot, (((0,), (0,)), ((), ())), preferred_element_type=F32
        )
        to = slice(LEAD + at, LEAD + at + 1024)
        held[48:ROWS, to] = jnp.zeros((ROWS - 48, 1024), F32)
        held[0:COMPONENTS, to] = feats_ref[:, at : at + 1024] - shift
        held[COMPONENTS : COMPONENTS + 1, to] = mass_ref[:, at : at + 1024]


def contribute(held, base, count, out):
    at = jnp.clip(base, -LEAD, CAP) + LEAD
    aligned = pl.multiple_of(lax.div(at, 128) * 128, 128)
    off = lax.rem(at, 128)
    turn = lax.rem(128 - off, 128)
    lane = lax.broadcasted_iota(jnp.int32, (ROWS, 128), 1)
    before = pltpu.roll(held[:, pl.ds(aligned, 128)], turn, 1)
    for t in range(GROUP // 128):
        after = pltpu.roll(
            held[:, pl.ds(pl.multiple_of(aligned + (t + 1) * 128, 128), 128)], turn, 1
        )
        value = jnp.where(lane < 128 - off, before, after)
        local = lane + (base + t * 128)
        out[:, t * 128 : (t + 1) * 128] = jnp.where((local >= 0) & (local < count), value, 0.0)
        before = after


def relay_kernel(
    counts_ref, feats_any, mass_any, ids_any, offsets_any, out_any,
    held, feats_ref, mass_ref, ids_ref, offsets_ref, out_ref, feats_sem, small_sem, out_sem,
):
    small = [
        pltpu.make_async_copy(a, b, small_sem.at[i])
        for i, (a, b) in enumerate(
            [(offsets_any, offsets_ref), (ids_any, ids_ref), (mass_any, mass_ref)]
        )
    ]
    large = [
        pltpu.make_async_copy(
            feats_any.at[:, at : at + 2048], feats_ref.at[:, at : at + 2048], feats_sem.at[i]
        )
        for i, at in enumerate(range(0, CAP, 2048))
    ]
    for copy in small + large:
        copy.start()
    x_lo, core, z_hi, z_lo, y, x_hi = place()
    mine = x_lo * 2 + core
    begin = jnp.int32(0)
    for k in range(3):
        begin = begin + jnp.where(k < mine, counts_ref[k], 0)
    count = counts_ref[mine]

    def ready(at):
        if at % 2048 == 0:
            large[at // 2048].wait()

    for copy in small:
        copy.wait()
    correct(feats_ref, mass_ref, ids_ref, offsets_ref, held, ready)
    moves = []
    for index in (3, 2, 1, 0):
        to_x, to_core = lax.rem(x_lo + index // 2, 2), lax.rem(core + index % 2, 2)
        base = (to_x * 2 + to_core) * (2 * GROUP) + z_lo * GROUP - begin
        contribute(held, base, count, out_ref.at[index])
        moves.append(
            pltpu.make_async_copy(out_ref.at[index], out_any.at[index], out_sem.at[index])
        )
        moves[-1].start()
    for copy in moves:
        copy.wait()


def log_sum(parts):
    peak = jnp.max(parts, axis=0)
    return peak + jnp.log2(jnp.sum(jnp.exp2(parts - peak[None]), axis=0))


def first_pass(lhs, rhs, cache, count, put, ready=None):
    chunk = min(CHUNK, count)

    def both(j, peak):
        top, total = None, None
        for at in range(0, count, chunk):
            if j < TILES:
                s = jnp.dot(
                    lhs[at : at + chunk, :], rhs[:, j * TILE : (j + 1) * TILE],
                    preferred_element_type=F32,
                )
                cache[j, at : at + chunk, :] = s
                here = jnp.max(s, axis=0, keepdims=True)
                top = here if top is None else jnp.maximum(top, here)
            if peak is not None:
                e = jnp.exp2(cache[j - 1, at : at + chunk, :] - peak)
                part = jnp.sum(e, axis=0, keepdims=True)
                total = part if total is None else total + part
        if peak is not None:
            put(j - 1, peak + jnp.log2(total))
        return top

    peak = None
    for j in range(TILES + 1):
        if ready is not None and j < TILES:
            ready(j)
        peak = both(j, peak)


def row_pass(cache, weight, count, put):
    def body(j, carry):
        peak, total = [None, None], [None, None]
        for at in range(0, count, 128):
            w = weight[at : at + 128, :]
            for h in range(2):
                t = (cache[j, at : at + 128, h * 128 : (h + 1) * 128] + w).reshape(16, 8, 128)
                top = jnp.max(t, axis=0)
                if at:
                    top = jnp.maximum(top, peak[h])
                part = jnp.sum(jnp.exp2(t - top[None]), axis=0)
                if at:
                    part = part + total[h] * jnp.exp2(peak[h] - top)
                peak[h], total[h] = top, part
        ends = []
        for h in range(2):
            top = jnp.max(peak[h], axis=0, keepdims=True)
            part = jnp.sum(total[h] * jnp.exp2(peak[h] - top), axis=0, keepdims=True)
            ends.append(top + jnp.log2(part))
        put(j, jnp.concatenate(ends, axis=1))
        return carry

    lax.fori_loop(0, TILES, body, 0)


def column_pass(cache, weight, spread_w, peaks, totals, out):
    for r in range(16):
        spread_w[r] = jnp.broadcast_to(weight[r : r + 1, :], (8, 128))

    def body(block, carry):
        for sub in range(8):
            rows = pl.ds(pl.multiple_of(block * 128 + sub * 16, 16), 16)
            parts = []
            for r in range(16):
                lanes = slice(r % 2 * 128, r % 2 * 128 + 128)
                t = cache[r // 2, rows, lanes].reshape(2, 8, 128)
                parts.append(t + spread_w[r][None])
            tops = parts
            while len(tops) > 1:
                tops = [jnp.maximum(a, b) for a, b in zip(tops[0::2], tops[1::2])]
            sums = [jnp.exp2(t - tops[0]) for t in parts]
            while len(sums) > 1:
                sums = [a + b for a, b in zip(sums[0::2], sums[1::2])]
            peaks[rows, :] = tops[0].reshape(16, 128)
            totals[rows, :] = sums[0].reshape(16, 128)
        return carry

    lax.fori_loop(0, GROUP // 128, body, 0)
    for c in range(16):
        at = slice(c * 128, (c + 1) * 128)
        turned = peaks[at, :].T
        top = jnp.max(turned, axis=0, keepdims=True)
        total = jnp.sum(totals[at, :].T * jnp.exp2(turned - top), axis=0, keepdims=True)
        out[c : c + 1, :] = top + jnp.log2(total)


def spread_rows(wide_w, weight):
    for c in range(weight.shape[0]):
        wide_w[c * 128 : (c + 1) * 128, :] = jnp.broadcast_to(weight[c : c + 1, :], (128, 128)).T


def to_rows(ref, row, first=0):
    for r in range(row.shape[1] // 128):
        ref[first + r : first + r + 1, :] = row[:, r * 128 : (r + 1) * 128]


def set_weights(lhs, fixed, weight):
    rows = weight.shape[0]
    parts = [p.astype(F32) for p in pieces(weight)]
    stacked = jnp.concatenate(parts + [jnp.zeros((128 - 3 * rows, 128), F32)], axis=0)
    turned = stacked.T
    lane = lax.rem(lax.broadcasted_iota(jnp.int32, (128, 128), 1), rows)
    for c in range(rows):
        at = slice(c * 128, (c + 1) * 128)
        lhs[at, 128:256] = jnp.where(lane == c, turned, 0.0).astype(BF16) + fixed[at, :]


def set_left(lhs, fixed, one, two, three):
    zero = jnp.zeros((64, 128), F32)
    for c in range(one.shape[1] // 128):
        at = slice(c * 128, (c + 1) * 128)
        first = jnp.concatenate([one[:, at].astype(F32), two[:, at].astype(F32)], axis=0)
        second = jnp.concatenate([zero, three[:, at].astype(F32)], axis=0)
        lhs[at, 0:128] = first.T.astype(BF16)
        fixed[at, :] = second.T.astype(BF16)


def set_right(rhs, at, one, two, three):
    rhs[0:64, at] = one
    rhs[64:128, at] = two
    row = lax.broadcasted_iota(jnp.int32, three.shape, 0)
    rhs[128:192, at] = jnp.where(row < 48, 1.0, 0.0).astype(BF16)
    rhs[192:256, at] = three


def padded(cells, centre):
    row = lax.broadcasted_iota(jnp.int32, cells.shape, 0)
    kept = jnp.where(row < COMPONENTS, cells - centre, 0.0)
    return jnp.concatenate([kept, jnp.zeros((64 - ROWS, cells.shape[1]), F32)], axis=0)


def sinkhorn_kernel(
    con_any, tgt_any, tgt_mass_any,
    src_out, tgt_out, self_out,
    con_ref, tgt_ref, tgt_mass_ref,
    from_own, from_opp, opp, landed, ybuf, xfull, sbuf,
    lhs_y, lhs_s, fix_y, fix_s, rhs_x, cache_f, cache_p,
    spread_w, peaks, totals, wide_g, wide_s,
    sq_x, sq_y, sq_s, log_x, log_y, log_s, pot_p, pot_s, wide,
    fb, pb, gb, pots, fin,
    relay_send, relay_recv, opp_send, opp_recv, own_sem, tgt_sem, self_sem, local_sem,
    fb_send, fb_recv, pb_send, pb_recv,
    gb_send, gb_recv, pot_send, pot_recv, fin_send, fin_recv, con_sem,
):
    x_lo, core, z_hi, z_lo, y, x_hi = place()
    sibling = device(x_lo, 1 - core, z_hi, z_lo, y, x_hi)
    twin = device(x_lo, core, z_hi, 1 - z_lo, y, x_hi)
    across = device(1 - x_lo, core, z_hi, z_lo, y, 1 - x_hi)
    straight = lax.rem(x_lo + core, 2)
    opposite = device(1 - x_lo, core, z_hi, z_lo, y, lax.rem(x_hi + straight, 2))
    y_hi, y_lo = lax.div(y, 2), lax.rem(y, 2)
    partner = device(
        lax.rem(x_lo + y_hi, 2), lax.rem(core + y_lo, 2), z_hi, lax.rem(z_lo + z_hi, 2), y, x_hi
    )
    alone = (y + z_hi) == 0
    g = x_lo * 4 + core * 2 + z_lo
    m = z_hi * 8 + y * 2 + x_hi

    def m_peer(k):
        return device(x_lo, core, lax.div(k, 8), z_lo, lax.rem(lax.div(k, 2), 4), lax.rem(k, 2))

    def g_peer(k):
        return device(lax.div(k, 4), lax.rem(lax.div(k, 2), 2), z_hi, lax.rem(k, 2), y, x_hi)

    m_others = [lax.rem(m + d, 16) for d in range(1, 16)]
    g_others = [lax.rem(g + d, 8) for d in range(1, 8)]

    barrier = pltpu.get_barrier_semaphore()
    peers = [m_peer(k) for k in m_others]
    peers += [g_peer(k) for k in g_others] + [across]
    for peer in peers:
        pl.semaphore_signal(barrier, inc=1, device_id=peer, device_id_type=MESH)

    loads = [
        pltpu.make_async_copy(a, b, con_sem.at[i])
        for i, (a, b) in enumerate(
            [
                (tgt_any, tgt_ref),
                (tgt_mass_any, tgt_mass_ref),
                (con_any.at[2], con_ref.at[1]),
                (con_any.at[0], con_ref.at[0]),
            ]
        )
    ]
    for copy in loads:
        copy.start()
    loads[0].wait()
    loads[1].wait()
    ybuf[z_lo, 48:ROWS, :] = jnp.zeros((ROWS - 48, HALF), F32)
    ybuf[z_lo, 0:COMPONENTS, :] = tgt_ref[...]
    ybuf[z_lo, COMPONENTS : COMPONENTS + 1, :] = tgt_mass_ref[...]

    pl.semaphore_wait(barrier, len(peers))

    def remote(src, dst, send, recv, to):
        return pltpu.make_async_remote_copy(
            src_ref=src, dst_ref=dst, send_sem=send, recv_sem=recv, device_id=to,
            device_id_type=MESH,
        )

    parts = [slice(c * 512, (c + 1) * 512) for c in range(4)]
    relays = [
        remote(con_any.at[3, :, s], from_opp.at[:, s], relay_send.at[c], relay_recv.at[c], sibling)
        for c, s in enumerate(parts)
    ]
    own = remote(con_any.at[1], from_own, own_sem.at[0], own_sem.at[1], sibling)
    tgt = remote(ybuf.at[z_lo], ybuf.at[z_lo], tgt_sem.at[0], tgt_sem.at[1], twin)
    tgt.start()

    for copy in relays:
        copy.start()
    own.start()
    onward = [
        remote(opp.at[:, s], landed.at[:, s], opp_send.at[c], opp_recv.at[c], opposite)
        for c, s in enumerate(parts)
    ]
    loads[2].wait()
    for c, s in enumerate(parts):
        relays[c].wait_recv()
        opp[:, s] = con_ref[1, :, s] + from_opp[:, s]
        onward[c].start()

    remote(ybuf.at[1 - z_lo], ybuf.at[1 - z_lo], tgt_sem.at[0], tgt_sem.at[1], twin).wait_recv()
    cells = jnp.concatenate([ybuf[0], ybuf[1]], axis=1)
    centre = jnp.sum(cells, axis=1, keepdims=True) * (1.0 / GROUP)
    kept = padded(cells, centre)
    to_rows(sq_y, jnp.sum(kept * kept, axis=0, keepdims=True) * SCALE)
    to_rows(log_y, jnp.log2(cells[COMPONENTS : COMPONENTS + 1, :]))
    high, middle, unused = pieces(kept)
    set_left(lhs_y, fix_y, high, high, middle)
    set_weights(lhs_y, fix_y, log_y[...] - sq_y[...])

    def put_wide(j, value):
        for r in range(TILE // 128):
            wide[pl.ds(TILE // 128 * j + r, 1), :] = value[:, r * 128 : (r + 1) * 128]

    loads[3].wait()
    own.wait_recv()

    half = pl.ds(pl.multiple_of(x_hi * HALF, HALF), HALF)
    shared = remote(xfull.at[:, half], sbuf, self_sem.at[0], self_sem.at[1], partner)
    kept_here = pltpu.make_async_copy(xfull.at[:, half], sbuf, local_sem)

    def arrive(j):
        if j % 2:
            return
        c = j // 2
        s = parts[c]
        onward[c].wait_recv()
        cells = con_ref[0, :, s] + from_own[:, s] + landed[:, s]
        xfull[:, s] = cells
        if c % 2:
            @pl.when((x_hi == c // 2) & alone)
            def _():
                kept_here.start()

            @pl.when((x_hi == c // 2) & jnp.logical_not(alone))
            def _():
                shared.start()

        kept = padded(cells, centre)
        to_rows(sq_x, jnp.sum(kept * kept, axis=0, keepdims=True) * SCALE, 4 * c)
        to_rows(log_x, jnp.log2(cells[COMPONENTS : COMPONENTS + 1, :]), 4 * c)
        high, middle, unused = pieces(kept * (2.0 * SCALE))
        set_right(rhs_x, s, high, middle, high)

    first_pass(lhs_y, rhs_x, cache_f, GROUP, put_wide, arrive)

    pot_p[...] = jnp.zeros_like(pot_p)
    pot_s[...] = jnp.zeros_like(pot_s)

    def spread(box, it, me, others, peer, send, recv):
        for k in others:
            remote(box.at[it, me], box.at[it, me], send.at[it], recv.at[it], peer(k)).start()

    def all_of(box, it, others, peer, send, recv):
        part = box.at[it, pl.ds(0, len(others))]
        return remote(part, part, send.at[it], recv.at[it], peer(others[0]))

    to_m, to_g = (m_others, m_peer), (g_others, g_peer)

    half_rows = pl.ds(pl.multiple_of(x_hi * 8, 8), 8)

    def finish_p(it):
        all_of(pb, it, *to_m, pb_send, pb_recv).wait_recv()
        all_of(pb, it, *to_m, pb_send, pb_recv).wait_send()
        pot_p[...] = 0.5 * (pot_p[...] - TAU * log_sum(pb[it]))

        @pl.when((it < ITERS - 1) & jnp.logical_not(alone))
        def _():
            pots[0, it] = pot_p[half_rows, :]
            remote(
                pots.at[0, it], pots.at[1, it], pot_send.at[it], pot_recv.at[it], partner
            ).start()

    def iteration(it, carry):
        @pl.when(it > 0)
        def _():
            row_pass(cache_f, wide_g, GROUP, put_wide)

        fb[it, m] = wide[...] - sq_x[...]
        spread(fb, it, m, *to_m, fb_send, fb_recv)

        @pl.when(it == 0)
        def _():
            @pl.when(alone)
            def _():
                kept_here.wait()

            @pl.when(jnp.logical_not(alone))
            def _():
                shared.wait_recv()
                shared.wait_send()

            for copy in relays + onward + [own, tgt]:
                copy.wait_send()
            got = sbuf[...]
            columns = padded(got, centre)
            to_rows(sq_s, jnp.sum(columns * columns, axis=0, keepdims=True) * SCALE)
            to_rows(log_s, jnp.log2(got[COMPONENTS : COMPONENTS + 1, :]))
            upper, lower, unused = pieces(columns)
            set_left(lhs_s, fix_s, upper, upper, lower)
            set_weights(lhs_s, fix_s, log_s[...] - sq_s[...])

        @pl.when(it == 1)
        def _():
            finish_p(0)

        @pl.when(it > 0)
        def _():
            last = it - 1

            @pl.when(alone)
            def _():
                pot_s[...] = pot_p[half_rows, :]

            @pl.when(jnp.logical_not(alone))
            def _():
                moved = remote(
                    pots.at[0, last], pots.at[1, last], pot_send.at[last], pot_recv.at[last],
                    partner,
                )
                moved.wait_recv()
                moved.wait_send()
                pot_s[...] = pots[1, last]

            spread_rows(wide_s, pot_s[...])
            row_pass(cache_p, wide_s, HALF, put_wide)
            pb[it, m] = wide[...] - sq_x[...]
            spread(pb, it, m, *to_m, pb_send, pb_recv)

        all_of(fb, it, *to_m, fb_send, fb_recv).wait_recv()
        pot_f = -TAU * log_sum(fb[it])
        @pl.when(it == ITERS - 1)
        def _():
            fin[0, z_lo] = pot_f * (1.0 / SCALE)
            remote(
                fin.at[0, z_lo], fin.at[0, z_lo], fin_send.at[0], fin_recv.at[0], twin
            ).start()

        column_pass(cache_f, log_x[...] + pot_f - sq_x[...], spread_w, peaks, totals, wide)
        gb[it, g] = wide[...] - log_y[...]
        spread(gb, it, g, *to_g, gb_send, gb_recv)

        @pl.when(it == 0)
        def _():
            first_pass(lhs_s, rhs_x, cache_p, HALF, put_wide)
            pb[0, m] = wide[...] - sq_x[...]
            spread(pb, 0, m, *to_m, pb_send, pb_recv)

        @pl.when(it > 0)
        def _():
            finish_p(it)

        @pl.when(it == ITERS - 1)
        def _():
            fin[1, z_lo] = pot_p[...] * (1.0 / SCALE)
            remote(
                fin.at[1, z_lo], fin.at[1, z_lo], fin_send.at[1], fin_recv.at[1], twin
            ).start()

        all_of(fb, it, *to_m, fb_send, fb_recv).wait_send()
        all_of(gb, it, *to_g, gb_send, gb_recv).wait_send()
        all_of(gb, it, *to_g, gb_send, gb_recv).wait_recv()
        pot_g = -TAU * log_sum(gb[it])
        wide[...] = pot_g

        @pl.when(it < ITERS - 1)
        def _():
            spread_rows(wide_g, pot_g)

        return carry

    lax.fori_loop(0, ITERS, iteration, 0)

    tgt_out[...] = wide[pl.ds(pl.multiple_of(z_lo * 8, 8), 8), :] * (1.0 / SCALE)
    for kind in range(2):
        remote(
            fin.at[kind, 1 - z_lo], fin.at[kind, 1 - z_lo], fin_send.at[kind], fin_recv.at[kind],
            twin,
        ).wait_recv()
        remote(
            fin.at[kind, z_lo], fin.at[kind, z_lo], fin_send.at[kind], fin_recv.at[kind], twin
        ).wait_send()
    src_out[0:16, :] = fin[0, 0]
    src_out[16:32, :] = fin[0, 1]
    self_out[0:16, :] = fin[1, 0]
    self_out[16:32, :] = fin[1, 1]


def on_device(
    src_features, src_mass, section_ids, shard_counts, section_offsets, tgt_features, tgt_mass
):
    vmem = pl.BlockSpec(memory_space=pltpu.VMEM)
    hbm = pl.BlockSpec(memory_space=pltpu.HBM)
    V, D = pltpu.VMEM, pltpu.SemaphoreType.DMA
    contributions = pl.pallas_call(
        relay_kernel,
        out_shape=jax.ShapeDtypeStruct((4, ROWS, GROUP), F32),
        in_specs=[pl.BlockSpec(memory_space=pltpu.SMEM)] + [hbm] * 4,
        out_specs=hbm,
        scratch_shapes=[
            V((ROWS, WIDTH), F32), V((COMPONENTS, CAP), F32), V((1, CAP), F32),
            V((1, CAP), jnp.int32), V((SECTIONS, COMPONENTS), F32), V((4, ROWS, GROUP), F32),
            D((4,)), D((3,)), D((4,)),
        ],
        compiler_params=pltpu.CompilerParams(vmem_limit_bytes=58 * 1024 * 1024),
    )(
        shard_counts,
        src_features,
        src_mass.reshape(1, CAP),
        section_ids.reshape(1, CAP),
        section_offsets.T,
    )
    rows16, rows8 = (16, 128), (8, 128)
    outs = pl.pallas_call(
        sinkhorn_kernel,
        out_shape=(
            V((32, 128), F32), V((8, 128), F32), V((32, 128), F32),
        ),
        in_specs=[hbm] * 3,
        out_specs=(vmem, vmem, vmem),
        scratch_shapes=[
            V((2, ROWS, GROUP), F32), V((COMPONENTS, HALF), F32), V((1, HALF), F32),
            V((ROWS, GROUP), F32), V((ROWS, GROUP), F32), V((ROWS, GROUP), F32),
            V((ROWS, GROUP), F32), V((2, ROWS, HALF), F32), V((ROWS, GROUP), F32),
            V((ROWS, HALF), F32),
            V((GROUP, 256), BF16), V((HALF, 256), BF16),
            V((GROUP, 128), BF16), V((HALF, 128), BF16), V((256, GROUP), BF16),
            V((TILES, GROUP, TILE), F32), V((TILES, HALF, TILE), F32),
            V((16, 8, 128), F32), V((GROUP, 128), F32), V((GROUP, 128), F32),
            V((GROUP, 128), F32), V((HALF, 128), F32),
            V(rows16, F32), V(rows16, F32), V(rows8, F32),
            V(rows16, F32), V(rows16, F32), V(rows8, F32),
            V(rows16, F32), V(rows8, F32), V(rows16, F32),
            V((ITERS, 16) + rows16, F32), V((ITERS, 16) + rows16, F32),
            V((ITERS, 8) + rows16, F32), V((2, ITERS - 1) + rows8, F32),
            V((2, 2) + rows16, F32),
            D((4,)), D((4,)), D((4,)), D((4,)), D((2,)), D((2,)), D((2,)), D,
            D((ITERS,)), D((ITERS,)), D((ITERS,)), D((ITERS,)), D((ITERS,)), D((ITERS,)),
            D((ITERS,)), D((ITERS,)), D((2,)), D((2,)),
            D((4,)),
        ],
        compiler_params=pltpu.CompilerParams(
            collective_id=0, has_side_effects=True, vmem_limit_bytes=58 * 1024 * 1024
        ),
    )(contributions, tgt_features, tgt_mass.reshape(1, HALF))
    return (outs[0].reshape(2 * GROUP), outs[1].reshape(HALF), outs[2].reshape(2 * GROUP))


def solution(mesh):
    return jax.shard_map(
        on_device,
        mesh=mesh,
        in_specs=(P(None, "src"), P("src"), P("src"), P(), P(), P(None, "tgt"), P("tgt")),
        out_specs=(P("src"), P("tgt"), P("src")),
        check_vma=False,
    )
```

```python
import jax
import jax.numpy as jnp
from jax import lax
from jax.experimental import pallas as pl
from jax.experimental.pallas import tpu as pltpu
from jax.sharding import PartitionSpec as P

COMPONENTS = 50
ROWS = 56
SECTIONS = 32
ITERS = 3
CAP = 8192
GROUP = 2048
HALF = 1024
SPAN = GROUP + 128
LEAD = GROUP
WIDTH = LEAD + CAP + SPAN

EPS = 0.05
TAU = 1.0 / (1.0 + EPS)
LOG2E = 1.4426950408889634
SCALE = LOG2E / EPS

F32 = jnp.float32
BF16 = jnp.bfloat16
MESH = pl.DeviceIdType.MESH
TILE = 256
TILES = GROUP // TILE
CHUNK = 256


def place():
    src, tgt = lax.axis_index("src"), lax.axis_index("tgt")
    z, rest = lax.div(tgt, 8), lax.rem(tgt, 8)
    return (
        lax.div(src, 2),
        lax.rem(src, 2),
        lax.div(z, 2),
        lax.rem(z, 2),
        lax.div(rest, 2),
        lax.rem(rest, 2),
    )


def device(x_lo, core, z_hi, z_lo, y, x_hi):
    return (x_lo * 2 + core, (z_hi * 2 + z_lo) * 8 + y * 2 + x_hi)


def pieces(value):
    high = value.astype(BF16)
    rest = value - high.astype(F32)
    middle = rest.astype(BF16)
    return high, middle, (rest - middle.astype(F32)).astype(BF16)


def correct(feats_ref, mass_ref, ids_ref, offsets_ref, held, ready):
    three = jnp.concatenate([p.astype(F32) for p in pieces(offsets_ref[...])], axis=0).astype(BF16)
    for at in range(0, CAP, 1024):
        ready(at)
        ids = ids_ref[:, at : at + 1024]
        section = lax.rem(lax.broadcasted_iota(jnp.int32, (3 * SECTIONS, 1024), 0), SECTIONS)
        onehot = jnp.where(section == ids, 1.0, 0.0).astype(BF16)
        shift = lax.dot_general(
            three, onehot, (((0,), (0,)), ((), ())), preferred_element_type=F32
        )
        to = slice(LEAD + at, LEAD + at + 1024)
        held[48:ROWS, to] = jnp.zeros((ROWS - 48, 1024), F32)
        held[0:COMPONENTS, to] = feats_ref[:, at : at + 1024] - shift
        held[COMPONENTS : COMPONENTS + 1, to] = mass_ref[:, at : at + 1024]


def contribute(held, base, count, out):
    at = jnp.clip(base, -LEAD, CAP) + LEAD
    aligned = pl.multiple_of(lax.div(at, 128) * 128, 128)
    off = lax.rem(at, 128)
    turn = lax.rem(128 - off, 128)
    lane = lax.broadcasted_iota(jnp.int32, (ROWS, 128), 1)
    before = pltpu.roll(held[:, pl.ds(aligned, 128)], turn, 1)
    for t in range(GROUP // 128):
        after = pltpu.roll(
            held[:, pl.ds(pl.multiple_of(aligned + (t + 1) * 128, 128), 128)], turn, 1
        )
        value = jnp.where(lane < 128 - off, before, after)
        local = lane + (base + t * 128)
        out[:, t * 128 : (t + 1) * 128] = jnp.where((local >= 0) & (local < count), value, 0.0)
        before = after


def relay_kernel(
    counts_ref, feats_any, mass_any, ids_any, offsets_any, out_any,
    held, feats_ref, mass_ref, ids_ref, offsets_ref, out_ref, feats_sem, small_sem, out_sem,
):
    small = [
        pltpu.make_async_copy(a, b, small_sem.at[i])
        for i, (a, b) in enumerate(
            [(offsets_any, offsets_ref), (ids_any, ids_ref), (mass_any, mass_ref)]
        )
    ]
    large = [
        pltpu.make_async_copy(
            feats_any.at[:, at : at + 2048], feats_ref.at[:, at : at + 2048], feats_sem.at[i]
        )
        for i, at in enumerate(range(0, CAP, 2048))
    ]
    for copy in small + large:
        copy.start()
    x_lo, core, z_hi, z_lo, y, x_hi = place()
    mine = x_lo * 2 + core
    begin = jnp.int32(0)
    for k in range(3):
        begin = begin + jnp.where(k < mine, counts_ref[k], 0)
    count = counts_ref[mine]

    def ready(at):
        if at % 2048 == 0:
            large[at // 2048].wait()

    for copy in small:
        copy.wait()
    correct(feats_ref, mass_ref, ids_ref, offsets_ref, held, ready)
    moves = []
    for index in (3, 2, 1, 0):
        to_x, to_core = lax.rem(x_lo + index // 2, 2), lax.rem(core + index % 2, 2)
        base = (to_x * 2 + to_core) * (2 * GROUP) + z_lo * GROUP - begin
        contribute(held, base, count, out_ref.at[index])
        moves.append(
            pltpu.make_async_copy(out_ref.at[index], out_any.at[index], out_sem.at[index])
        )
        moves[-1].start()
    for copy in moves:
        copy.wait()


def log_sum(parts):
    peak = jnp.max(parts, axis=0)
    return peak + jnp.log2(jnp.sum(jnp.exp2(parts - peak[None]), axis=0))


def tree(op, parts):
    while len(parts) > 1:
        pairs = [op(a, b) for a, b in zip(parts[0::2], parts[1::2])]
        parts = pairs + parts[len(pairs) * 2 :]
    return parts[0]


def first_pass(lhs, rhs, cache, count, put, ready=None):
    chunk = min(CHUNK, count)

    def both(j, peak):
        tops, sums = [], []
        for at in range(0, count, chunk):
            if j < TILES:
                s = jnp.dot(
                    lhs[at : at + chunk, :], rhs[:, j * TILE : (j + 1) * TILE],
                    preferred_element_type=F32,
                )
                cache[j, at : at + chunk, :] = s
                s = s.reshape(chunk // 8, 8, TILE)
                tops.append(tree(jnp.maximum, [s[i] for i in range(chunk // 8)]))
            if peak is not None:
                e = [
                    jnp.exp2(cache[j - 1, row : row + 8, :] - peak)
                    for row in range(at, at + chunk, 8)
                ]
                sums.append(tree(jnp.add, e))
        if peak is not None:
            total = jnp.sum(tree(jnp.add, sums), axis=0, keepdims=True)
            put(j - 1, peak + jnp.log2(total))
        return jnp.max(tree(jnp.maximum, tops), axis=0, keepdims=True) if tops else None

    peak = None
    for j in range(TILES + 1):
        if ready is not None and j < TILES:
            ready(j)
        peak = both(j, peak)


def row_pass(cache, weight, count, put):
    def body(j, carry):
        ends = [[], []]
        for at in range(0, count, 128):
            w = [weight[row : row + 8, :] for row in range(at, at + 128, 8)]
            for h in range(2):
                lanes = slice(h * 128, (h + 1) * 128)
                t = [cache[j, at + 8 * i : at + 8 * i + 8, lanes] + w[i] for i in range(16)]
                top = tree(jnp.maximum, t)
                ends[h].append((top, tree(jnp.add, [jnp.exp2(v - top) for v in t])))
        rows = []
        for h in range(2):
            top = tree(jnp.maximum, [v[0] for v in ends[h]])
            part = tree(jnp.add, [v[1] * jnp.exp2(v[0] - top) for v in ends[h]])
            most = jnp.max(top, axis=0, keepdims=True)
            part = jnp.sum(part * jnp.exp2(top - most), axis=0, keepdims=True)
            rows.append(most + jnp.log2(part))
        put(j, jnp.concatenate(rows, axis=1))
        return carry

    lax.fori_loop(0, TILES, body, 0)


def column_pass(cache, weight, spread_w, peaks, totals, out):
    for r in range(16):
        spread_w[r] = jnp.broadcast_to(weight[r : r + 1, :], (8, 128))

    def body(block, carry):
        for sub in range(8):
            rows = pl.ds(pl.multiple_of(block * 128 + sub * 16, 16), 16)
            parts = []
            for r in range(16):
                lanes = slice(r % 2 * 128, r % 2 * 128 + 128)
                t = cache[r // 2, rows, lanes].reshape(2, 8, 128)
                parts.append(t + spread_w[r][None])
            top = tree(jnp.maximum, parts)
            total = tree(jnp.add, [jnp.exp2(t - top) for t in parts])
            peaks[rows, :] = top.reshape(16, 128)
            totals[rows, :] = total.reshape(16, 128)
        return carry

    lax.fori_loop(0, GROUP // 128, body, 0)
    for c in range(16):
        at = slice(c * 128, (c + 1) * 128)
        turned = peaks[at, :].T
        top = jnp.max(turned, axis=0, keepdims=True)
        total = jnp.sum(totals[at, :].T * jnp.exp2(turned - top), axis=0, keepdims=True)
        out[c : c + 1, :] = top + jnp.log2(total)


def spread_rows(wide_w, weight):
    for c in range(weight.shape[0]):
        wide_w[c * 128 : (c + 1) * 128, :] = jnp.broadcast_to(weight[c : c + 1, :], (128, 128)).T


def to_rows(ref, row, first=0):
    for r in range(row.shape[1] // 128):
        ref[first + r : first + r + 1, :] = row[:, r * 128 : (r + 1) * 128]


def set_weights(lhs, fixed, weight):
    rows = weight.shape[0]
    parts = [p.astype(F32) for p in pieces(weight)]
    stacked = jnp.concatenate(parts + [jnp.zeros((128 - 3 * rows, 128), F32)], axis=0)
    turned = stacked.T
    lane = lax.rem(lax.broadcasted_iota(jnp.int32, (128, 128), 1), rows)
    for c in range(rows):
        at = slice(c * 128, (c + 1) * 128)
        lhs[at, 128:256] = jnp.where(lane == c, turned, 0.0).astype(BF16) + fixed[at, :]


def set_left(lhs, fixed, one, two, three):
    zero = jnp.zeros((64, 128), F32)
    for c in range(one.shape[1] // 128):
        at = slice(c * 128, (c + 1) * 128)
        first = jnp.concatenate([one[:, at].astype(F32), two[:, at].astype(F32)], axis=0)
        second = jnp.concatenate([zero, three[:, at].astype(F32)], axis=0)
        lhs[at, 0:128] = first.T.astype(BF16)
        fixed[at, :] = second.T.astype(BF16)


def set_right(rhs, at, one, two, three):
    rhs[0:64, at] = one
    rhs[64:128, at] = two
    row = lax.broadcasted_iota(jnp.int32, three.shape, 0)
    rhs[128:192, at] = jnp.where(row < 48, 1.0, 0.0).astype(BF16)
    rhs[192:256, at] = three


def padded(cells, centre):
    row = lax.broadcasted_iota(jnp.int32, cells.shape, 0)
    kept = jnp.where(row < COMPONENTS, cells - centre, 0.0)
    return jnp.concatenate([kept, jnp.zeros((64 - ROWS, cells.shape[1]), F32)], axis=0)


def sinkhorn_kernel(
    con_any, tgt_any, tgt_mass_any,
    src_out, tgt_out, self_out,
    con_ref, tgt_ref, tgt_mass_ref,
    from_own, from_opp, opp, landed, ybuf, xfull, sbuf,
    lhs_y, lhs_s, fix_y, fix_s, rhs_x, cache_f, cache_p,
    spread_w, peaks, totals, wide_g, wide_s,
    sq_x, sq_y, sq_s, log_x, log_y, log_s, pot_p, pot_s, wide,
    fb, pb, gb, pots, fin,
    relay_send, relay_recv, opp_send, opp_recv, own_sem, tgt_sem, self_sem, local_sem,
    fb_send, fb_recv, pb_send, pb_recv,
    gb_send, gb_recv, pot_send, pot_recv, fin_send, fin_recv, con_sem,
):
    x_lo, core, z_hi, z_lo, y, x_hi = place()
    sibling = device(x_lo, 1 - core, z_hi, z_lo, y, x_hi)
    twin = device(x_lo, core, z_hi, 1 - z_lo, y, x_hi)
    across = device(1 - x_lo, core, z_hi, z_lo, y, 1 - x_hi)
    straight = lax.rem(x_lo + core, 2)
    opposite = device(1 - x_lo, core, z_hi, z_lo, y, lax.rem(x_hi + straight, 2))
    y_hi, y_lo = lax.div(y, 2), lax.rem(y, 2)
    partner = device(
        lax.rem(x_lo + y_hi, 2), lax.rem(core + y_lo, 2), z_hi, lax.rem(z_lo + z_hi, 2), y, x_hi
    )
    alone = (y + z_hi) == 0
    g = x_lo * 4 + core * 2 + z_lo
    m = z_hi * 8 + y * 2 + x_hi

    def m_peer(k):
        return device(x_lo, core, lax.div(k, 8), z_lo, lax.rem(lax.div(k, 2), 4), lax.rem(k, 2))

    def g_peer(k):
        return device(lax.div(k, 4), lax.rem(lax.div(k, 2), 2), z_hi, lax.rem(k, 2), y, x_hi)

    m_others = [lax.rem(m + d, 16) for d in range(1, 16)]
    g_others = [lax.rem(g + d, 8) for d in range(1, 8)]

    barrier = pltpu.get_barrier_semaphore()
    peers = [m_peer(k) for k in m_others]
    peers += [g_peer(k) for k in g_others] + [across]
    for peer in peers:
        pl.semaphore_signal(barrier, inc=1, device_id=peer, device_id_type=MESH)

    loads = [
        pltpu.make_async_copy(a, b, con_sem.at[i])
        for i, (a, b) in enumerate(
            [
                (tgt_any, tgt_ref),
                (tgt_mass_any, tgt_mass_ref),
                (con_any.at[2], con_ref.at[1]),
                (con_any.at[0], con_ref.at[0]),
            ]
        )
    ]
    for copy in loads:
        copy.start()
    loads[0].wait()
    loads[1].wait()
    ybuf[z_lo, 48:ROWS, :] = jnp.zeros((ROWS - 48, HALF), F32)
    ybuf[z_lo, 0:COMPONENTS, :] = tgt_ref[...]
    ybuf[z_lo, COMPONENTS : COMPONENTS + 1, :] = tgt_mass_ref[...]

    pl.semaphore_wait(barrier, len(peers))

    def remote(src, dst, send, recv, to):
        return pltpu.make_async_remote_copy(
            src_ref=src, dst_ref=dst, send_sem=send, recv_sem=recv, device_id=to,
            device_id_type=MESH,
        )

    parts = [slice(c * 512, (c + 1) * 512) for c in range(4)]
    relays = [
        remote(con_any.at[3, :, s], from_opp.at[:, s], relay_send.at[c], relay_recv.at[c], sibling)
        for c, s in enumerate(parts)
    ]
    own = remote(con_any.at[1], from_own, own_sem.at[0], own_sem.at[1], sibling)
    tgt = remote(ybuf.at[z_lo], ybuf.at[z_lo], tgt_sem.at[0], tgt_sem.at[1], twin)
    tgt.start()

    for copy in relays:
        copy.start()
    own.start()
    onward = [
        remote(opp.at[:, s], landed.at[:, s], opp_send.at[c], opp_recv.at[c], opposite)
        for c, s in enumerate(parts)
    ]
    loads[2].wait()
    for c, s in enumerate(parts):
        relays[c].wait_recv()
        opp[:, s] = con_ref[1, :, s] + from_opp[:, s]
        onward[c].start()

    remote(ybuf.at[1 - z_lo], ybuf.at[1 - z_lo], tgt_sem.at[0], tgt_sem.at[1], twin).wait_recv()
    cells = jnp.concatenate([ybuf[0], ybuf[1]], axis=1)
    centre = jnp.sum(cells, axis=1, keepdims=True) * (1.0 / GROUP)
    kept = padded(cells, centre)
    to_rows(sq_y, jnp.sum(kept * kept, axis=0, keepdims=True) * SCALE)
    to_rows(log_y, jnp.log2(cells[COMPONENTS : COMPONENTS + 1, :]))
    high, middle, unused = pieces(kept)
    set_left(lhs_y, fix_y, high, high, middle)
    set_weights(lhs_y, fix_y, log_y[...] - sq_y[...])

    def put_wide(j, value):
        for r in range(TILE // 128):
            wide[pl.ds(TILE // 128 * j + r, 1), :] = value[:, r * 128 : (r + 1) * 128]

    loads[3].wait()
    own.wait_recv()

    half = pl.ds(pl.multiple_of(x_hi * HALF, HALF), HALF)
    shared = remote(xfull.at[:, half], sbuf, self_sem.at[0], self_sem.at[1], partner)
    kept_here = pltpu.make_async_copy(xfull.at[:, half], sbuf, local_sem)

    def arrive(j):
        if j % 2:
            return
        c = j // 2
        s = parts[c]
        onward[c].wait_recv()
        cells = con_ref[0, :, s] + from_own[:, s] + landed[:, s]
        xfull[:, s] = cells
        if c % 2:
            @pl.when((x_hi == c // 2) & alone)
            def _():
                kept_here.start()

            @pl.when((x_hi == c // 2) & jnp.logical_not(alone))
            def _():
                shared.start()

        kept = padded(cells, centre)
        to_rows(sq_x, jnp.sum(kept * kept, axis=0, keepdims=True) * SCALE, 4 * c)
        to_rows(log_x, jnp.log2(cells[COMPONENTS : COMPONENTS + 1, :]), 4 * c)
        high, middle, unused = pieces(kept * (2.0 * SCALE))
        set_right(rhs_x, s, high, middle, high)

    first_pass(lhs_y, rhs_x, cache_f, GROUP, put_wide, arrive)

    pot_p[...] = jnp.zeros_like(pot_p)
    pot_s[...] = jnp.zeros_like(pot_s)

    def spread(box, it, me, others, peer, send, recv):
        for k in others:
            remote(box.at[it, me], box.at[it, me], send.at[it], recv.at[it], peer(k)).start()

    def all_of(box, it, others, peer, send, recv):
        part = box.at[it, pl.ds(0, len(others))]
        return remote(part, part, send.at[it], recv.at[it], peer(others[0]))

    to_m, to_g = (m_others, m_peer), (g_others, g_peer)

    half_rows = pl.ds(pl.multiple_of(x_hi * 8, 8), 8)

    def finish_p(it):
        all_of(pb, it, *to_m, pb_send, pb_recv).wait_recv()
        all_of(pb, it, *to_m, pb_send, pb_recv).wait_send()
        pot_p[...] = 0.5 * (pot_p[...] - TAU * log_sum(pb[it]))

        @pl.when((it < ITERS - 1) & jnp.logical_not(alone))
        def _():
            pots[0, it] = pot_p[half_rows, :]
            remote(
                pots.at[0, it], pots.at[1, it], pot_send.at[it], pot_recv.at[it], partner
            ).start()

    def iteration(it, carry):
        @pl.when(it > 0)
        def _():
            row_pass(cache_f, wide_g, GROUP, put_wide)

        fb[it, m] = wide[...] - sq_x[...]
        spread(fb, it, m, *to_m, fb_send, fb_recv)

        @pl.when(it == 0)
        def _():
            @pl.when(alone)
            def _():
                kept_here.wait()

            @pl.when(jnp.logical_not(alone))
            def _():
                shared.wait_recv()
                shared.wait_send()

            for copy in relays + onward + [own, tgt]:
                copy.wait_send()
            got = sbuf[...]
            columns = padded(got, centre)
            to_rows(sq_s, jnp.sum(columns * columns, axis=0, keepdims=True) * SCALE)
            to_rows(log_s, jnp.log2(got[COMPONENTS : COMPONENTS + 1, :]))
            upper, lower, unused = pieces(columns)
            set_left(lhs_s, fix_s, upper, upper, lower)
            set_weights(lhs_s, fix_s, log_s[...] - sq_s[...])

        @pl.when(it == 1)
        def _():
            finish_p(0)

        @pl.when(it > 0)
        def _():
            last = it - 1

            @pl.when(alone)
            def _():
                pot_s[...] = pot_p[half_rows, :]

            @pl.when(jnp.logical_not(alone))
            def _():
                moved = remote(
                    pots.at[0, last], pots.at[1, last], pot_send.at[last], pot_recv.at[last],
                    partner,
                )
                moved.wait_recv()
                moved.wait_send()
                pot_s[...] = pots[1, last]

            spread_rows(wide_s, pot_s[...])
            row_pass(cache_p, wide_s, HALF, put_wide)
            pb[it, m] = wide[...] - sq_x[...]
            spread(pb, it, m, *to_m, pb_send, pb_recv)

        all_of(fb, it, *to_m, fb_send, fb_recv).wait_recv()
        pot_f = -TAU * log_sum(fb[it])
        @pl.when(it == ITERS - 1)
        def _():
            fin[0, z_lo] = pot_f * (1.0 / SCALE)
            remote(
                fin.at[0, z_lo], fin.at[0, z_lo], fin_send.at[0], fin_recv.at[0], twin
            ).start()

        column_pass(cache_f, log_x[...] + pot_f - sq_x[...], spread_w, peaks, totals, wide)
        gb[it, g] = wide[...] - log_y[...]
        spread(gb, it, g, *to_g, gb_send, gb_recv)

        @pl.when(it == 0)
        def _():
            first_pass(lhs_s, rhs_x, cache_p, HALF, put_wide)
            pb[0, m] = wide[...] - sq_x[...]
            spread(pb, 0, m, *to_m, pb_send, pb_recv)

        @pl.when(it > 0)
        def _():
            finish_p(it)

        @pl.when(it == ITERS - 1)
        def _():
            fin[1, z_lo] = pot_p[...] * (1.0 / SCALE)
            remote(
                fin.at[1, z_lo], fin.at[1, z_lo], fin_send.at[1], fin_recv.at[1], twin
            ).start()

        all_of(fb, it, *to_m, fb_send, fb_recv).wait_send()
        all_of(gb, it, *to_g, gb_send, gb_recv).wait_send()
        all_of(gb, it, *to_g, gb_send, gb_recv).wait_recv()
        pot_g = -TAU * log_sum(gb[it])
        wide[...] = pot_g

        @pl.when(it < ITERS - 1)
        def _():
            spread_rows(wide_g, pot_g)

        return carry

    lax.fori_loop(0, ITERS, iteration, 0)

    tgt_out[...] = wide[pl.ds(pl.multiple_of(z_lo * 8, 8), 8), :] * (1.0 / SCALE)
    for kind in range(2):
        remote(
            fin.at[kind, 1 - z_lo], fin.at[kind, 1 - z_lo], fin_send.at[kind], fin_recv.at[kind],
            twin,
        ).wait_recv()
        remote(
            fin.at[kind, z_lo], fin.at[kind, z_lo], fin_send.at[kind], fin_recv.at[kind], twin
        ).wait_send()
    src_out[0:16, :] = fin[0, 0]
    src_out[16:32, :] = fin[0, 1]
    self_out[0:16, :] = fin[1, 0]
    self_out[16:32, :] = fin[1, 1]


def on_device(
    src_features, src_mass, section_ids, shard_counts, section_offsets, tgt_features, tgt_mass
):
    vmem = pl.BlockSpec(memory_space=pltpu.VMEM)
    hbm = pl.BlockSpec(memory_space=pltpu.HBM)
    V, D = pltpu.VMEM, pltpu.SemaphoreType.DMA
    contributions = pl.pallas_call(
        relay_kernel,
        out_shape=jax.ShapeDtypeStruct((4, ROWS, GROUP), F32),
        in_specs=[pl.BlockSpec(memory_space=pltpu.SMEM)] + [hbm] * 4,
        out_specs=hbm,
        scratch_shapes=[
            V((ROWS, WIDTH), F32), V((COMPONENTS, CAP), F32), V((1, CAP), F32),
            V((1, CAP), jnp.int32), V((SECTIONS, COMPONENTS), F32), V((4, ROWS, GROUP), F32),
            D((4,)), D((3,)), D((4,)),
        ],
        compiler_params=pltpu.CompilerParams(vmem_limit_bytes=58 * 1024 * 1024),
    )(
        shard_counts,
        src_features,
        src_mass.reshape(1, CAP),
        section_ids.reshape(1, CAP),
        section_offsets.T,
    )
    rows16, rows8 = (16, 128), (8, 128)
    outs = pl.pallas_call(
        sinkhorn_kernel,
        out_shape=(
            V((32, 128), F32), V((8, 128), F32), V((32, 128), F32),
        ),
        in_specs=[hbm] * 3,
        out_specs=(vmem, vmem, vmem),
        scratch_shapes=[
            V((2, ROWS, GROUP), F32), V((COMPONENTS, HALF), F32), V((1, HALF), F32),
            V((ROWS, GROUP), F32), V((ROWS, GROUP), F32), V((ROWS, GROUP), F32),
            V((ROWS, GROUP), F32), V((2, ROWS, HALF), F32), V((ROWS, GROUP), F32),
            V((ROWS, HALF), F32),
            V((GROUP, 256), BF16), V((HALF, 256), BF16),
            V((GROUP, 128), BF16), V((HALF, 128), BF16), V((256, GROUP), BF16),
            V((TILES, GROUP, TILE), F32), V((TILES, HALF, TILE), F32),
            V((16, 8, 128), F32), V((GROUP, 128), F32), V((GROUP, 128), F32),
            V((GROUP, 128), F32), V((HALF, 128), F32),
            V(rows16, F32), V(rows16, F32), V(rows8, F32),
            V(rows16, F32), V(rows16, F32), V(rows8, F32),
            V(rows16, F32), V(rows8, F32), V(rows16, F32),
            V((ITERS, 16) + rows16, F32), V((ITERS, 16) + rows16, F32),
            V((ITERS, 8) + rows16, F32), V((2, ITERS - 1) + rows8, F32),
            V((2, 2) + rows16, F32),
            D((4,)), D((4,)), D((4,)), D((4,)), D((2,)), D((2,)), D((2,)), D,
            D((ITERS,)), D((ITERS,)), D((ITERS,)), D((ITERS,)), D((ITERS,)), D((ITERS,)),
            D((ITERS,)), D((ITERS,)), D((2,)), D((2,)),
            D((4,)),
        ],
        compiler_params=pltpu.CompilerParams(
            collective_id=0, has_side_effects=True, vmem_limit_bytes=58 * 1024 * 1024
        ),
    )(contributions, tgt_features, tgt_mass.reshape(1, HALF))
    return (outs[0].reshape(2 * GROUP), outs[1].reshape(HALF), outs[2].reshape(2 * GROUP))


def solution(mesh):
    return jax.shard_map(
        on_device,
        mesh=mesh,
        in_specs=(P(None, "src"), P("src"), P("src"), P(), P(), P(None, "tgt"), P("tgt")),
        out_specs=(P("src"), P("tgt"), P("src")),
        check_vma=False,
    )
```

```python
import jax
import jax.numpy as jnp
from jax import lax
from jax.experimental import pallas as pl
from jax.experimental.pallas import tpu as pltpu
from jax.sharding import PartitionSpec as P

COMPONENTS = 50
ROWS = 56
SECTIONS = 32
ITERS = 3
CAP = 8192
GROUP = 2048
HALF = 1024
SPAN = GROUP + 128
LEAD = GROUP
WIDTH = LEAD + CAP + SPAN

EPS = 0.05
TAU = 1.0 / (1.0 + EPS)
LOG2E = 1.4426950408889634
SCALE = LOG2E / EPS

F32 = jnp.float32
BF16 = jnp.bfloat16
MESH = pl.DeviceIdType.MESH
TILE = 256
TILES = GROUP // TILE
CHUNK = 256


def place():
    src, tgt = lax.axis_index("src"), lax.axis_index("tgt")
    z, rest = lax.div(tgt, 8), lax.rem(tgt, 8)
    return (
        lax.div(src, 2),
        lax.rem(src, 2),
        lax.div(z, 2),
        lax.rem(z, 2),
        lax.div(rest, 2),
        lax.rem(rest, 2),
    )


def device(x_lo, core, z_hi, z_lo, y, x_hi):
    return (x_lo * 2 + core, (z_hi * 2 + z_lo) * 8 + y * 2 + x_hi)


def pieces(value):
    high = value.astype(BF16)
    rest = value - high.astype(F32)
    middle = rest.astype(BF16)
    return high, middle, (rest - middle.astype(F32)).astype(BF16)


def correct(feats_ref, mass_ref, ids_ref, offsets_ref, held, ready):
    three = jnp.concatenate([p.astype(F32) for p in pieces(offsets_ref[...])], axis=0).astype(BF16)
    for at in range(0, CAP, 1024):
        ready(at)
        ids = ids_ref[:, at : at + 1024]
        section = lax.rem(lax.broadcasted_iota(jnp.int32, (3 * SECTIONS, 1024), 0), SECTIONS)
        onehot = jnp.where(section == ids, 1.0, 0.0).astype(BF16)
        shift = lax.dot_general(
            three, onehot, (((0,), (0,)), ((), ())), preferred_element_type=F32
        )
        to = slice(LEAD + at, LEAD + at + 1024)
        held[48:ROWS, to] = jnp.zeros((ROWS - 48, 1024), F32)
        held[0:COMPONENTS, to] = feats_ref[:, at : at + 1024] - shift
        held[COMPONENTS : COMPONENTS + 1, to] = mass_ref[:, at : at + 1024]


def contribute(held, base, count, out):
    at = jnp.clip(base, -LEAD, CAP) + LEAD
    aligned = pl.multiple_of(lax.div(at, 128) * 128, 128)
    off = lax.rem(at, 128)
    turn = lax.rem(128 - off, 128)
    lane = lax.broadcasted_iota(jnp.int32, (ROWS, 128), 1)
    before = pltpu.roll(held[:, pl.ds(aligned, 128)], turn, 1)
    for t in range(GROUP // 128):
        after = pltpu.roll(
            held[:, pl.ds(pl.multiple_of(aligned + (t + 1) * 128, 128), 128)], turn, 1
        )
        value = jnp.where(lane < 128 - off, before, after)
        local = lane + (base + t * 128)
        out[:, t * 128 : (t + 1) * 128] = jnp.where((local >= 0) & (local < count), value, 0.0)
        before = after


def relay_kernel(
    counts_ref, feats_any, mass_any, ids_any, offsets_any, out_any,
    held, feats_ref, mass_ref, ids_ref, offsets_ref, out_ref, feats_sem, small_sem, out_sem,
):
    small = [
        pltpu.make_async_copy(a, b, small_sem.at[i])
        for i, (a, b) in enumerate(
            [(offsets_any, offsets_ref), (ids_any, ids_ref), (mass_any, mass_ref)]
        )
    ]
    large = [
        pltpu.make_async_copy(
            feats_any.at[:, at : at + 2048], feats_ref.at[:, at : at + 2048], feats_sem.at[i]
        )
        for i, at in enumerate(range(0, CAP, 2048))
    ]
    for copy in small + large:
        copy.start()
    x_lo, core, z_hi, z_lo, y, x_hi = place()
    mine = x_lo * 2 + core
    begin = jnp.int32(0)
    for k in range(3):
        begin = begin + jnp.where(k < mine, counts_ref[k], 0)
    count = counts_ref[mine]

    def ready(at):
        if at % 2048 == 0:
            large[at // 2048].wait()

    for copy in small:
        copy.wait()
    correct(feats_ref, mass_ref, ids_ref, offsets_ref, held, ready)
    moves = []
    for index in (3, 2, 1, 0):
        to_x, to_core = lax.rem(x_lo + index // 2, 2), lax.rem(core + index % 2, 2)
        base = (to_x * 2 + to_core) * (2 * GROUP) + z_lo * GROUP - begin
        contribute(held, base, count, out_ref.at[index])
        moves.append(
            pltpu.make_async_copy(out_ref.at[index], out_any.at[index], out_sem.at[index])
        )
        moves[-1].start()
    for copy in moves:
        copy.wait()


def log_sum(parts):
    peak = jnp.max(parts, axis=0)
    return peak + jnp.log2(jnp.sum(jnp.exp2(parts - peak[None]), axis=0))


def tree(op, parts):
    while len(parts) > 1:
        pairs = [op(a, b) for a, b in zip(parts[0::2], parts[1::2])]
        parts = pairs + parts[len(pairs) * 2 :]
    return parts[0]


def first_pass(lhs, rhs, cache, count, put, ready=None):
    chunk = min(CHUNK, count)

    def both(j, peak):
        tops, sums = [], []
        for at in range(0, count, chunk):
            if j < TILES:
                s = jnp.dot(
                    lhs[at : at + chunk, :], rhs[:, j * TILE : (j + 1) * TILE],
                    preferred_element_type=F32,
                )
                cache[j, at : at + chunk, :] = s
                s = s.reshape(chunk // 8, 8, TILE)
                tops.append(tree(jnp.maximum, [s[i] for i in range(chunk // 8)]))
            if peak is not None:
                e = [
                    jnp.exp2(cache[j - 1, row : row + 8, :] - peak)
                    for row in range(at, at + chunk, 8)
                ]
                sums.append(tree(jnp.add, e))
        if peak is not None:
            total = jnp.sum(tree(jnp.add, sums), axis=0, keepdims=True)
            put(j - 1, peak + jnp.log2(total))
        return jnp.max(tree(jnp.maximum, tops), axis=0, keepdims=True) if tops else None

    peak = None
    for j in range(TILES + 1):
        if ready is not None and j < TILES:
            ready(j)
        peak = both(j, peak)


def row_pass(cache, weight, span, tiles, state, begin, end, put):
    def body(j, carry):
        ends = [[], []]
        for at in range(span[0], span[1], 128):
            w = [weight[row : row + 8, :] for row in range(at, at + 128, 8)]
            for h in range(2):
                lanes = slice(h * 128, (h + 1) * 128)
                t = [cache[j, at + 8 * i : at + 8 * i + 8, lanes] + w[i] for i in range(16)]
                top = tree(jnp.maximum, t)
                ends[h].append((top, tree(jnp.add, [jnp.exp2(v - top) for v in t])))
        rows = []
        for h in range(2):
            lanes = slice(h * 128, (h + 1) * 128)
            if not begin:
                ends[h].append((state[0, j, :, lanes], state[1, j, :, lanes]))
            top = tree(jnp.maximum, [v[0] for v in ends[h]])
            part = tree(jnp.add, [v[1] * jnp.exp2(v[0] - top) for v in ends[h]])
            if end:
                most = jnp.max(top, axis=0, keepdims=True)
                part = jnp.sum(part * jnp.exp2(top - most), axis=0, keepdims=True)
                rows.append(most + jnp.log2(part))
            else:
                state[0, j, :, lanes] = top
                state[1, j, :, lanes] = part
        if end:
            put(j, jnp.concatenate(rows, axis=1))
        return carry

    lax.fori_loop(tiles[0], tiles[1], body, 0)


def column_pass(cache, weight, half, blocks, spread_w, peaks, totals):
    for r in range(8):
        spread_w[r] = jnp.broadcast_to(weight[r : r + 1, :], (8, 128))

    def body(block, carry):
        for sub in range(4):
            rows = pl.ds(pl.multiple_of(block * 128 + sub * 32, 32), 32)
            parts = []
            for r in range(8):
                lanes = slice(r % 2 * 128, r % 2 * 128 + 128)
                t = cache[half * 4 + r // 2, rows, lanes].reshape(4, 8, 128)
                parts.append(t + spread_w[r][None])
            top = tree(jnp.maximum, parts)
            if half:
                before = peaks[rows, :].reshape(4, 8, 128)
                top = jnp.maximum(top, before)
            sums = [jnp.exp2(t - top) for t in parts]
            if half:
                sums.append(totals[rows, :].reshape(4, 8, 128) * jnp.exp2(before - top))
            peaks[rows, :] = top.reshape(32, 128)
            totals[rows, :] = tree(jnp.add, sums).reshape(32, 128)
        return carry

    lax.fori_loop(blocks[0], blocks[1], body, 0)


def over_lanes(peaks, totals, blocks, out):
    for c in range(blocks[0], blocks[1]):
        at = slice(c * 128, (c + 1) * 128)
        turned = peaks[at, :].T
        top = jnp.max(turned, axis=0, keepdims=True)
        total = jnp.sum(totals[at, :].T * jnp.exp2(turned - top), axis=0, keepdims=True)
        out[c : c + 1, :] = top + jnp.log2(total)


def spread_rows(wide_w, weight, first=0):
    for c in range(weight.shape[0]):
        at = slice((first + c) * 128, (first + c + 1) * 128)
        wide_w[at, :] = jnp.broadcast_to(weight[c : c + 1, :], (128, 128)).T


def to_rows(ref, row, first=0):
    for r in range(row.shape[1] // 128):
        ref[first + r : first + r + 1, :] = row[:, r * 128 : (r + 1) * 128]


def set_weights(lhs, fixed, weight):
    rows = weight.shape[0]
    parts = [p.astype(F32) for p in pieces(weight)]
    stacked = jnp.concatenate(parts + [jnp.zeros((128 - 3 * rows, 128), F32)], axis=0)
    turned = stacked.T
    lane = lax.rem(lax.broadcasted_iota(jnp.int32, (128, 128), 1), rows)
    for c in range(rows):
        at = slice(c * 128, (c + 1) * 128)
        lhs[at, 128:256] = jnp.where(lane == c, turned, 0.0).astype(BF16) + fixed[at, :]


def set_left(lhs, fixed, one, two, three):
    zero = jnp.zeros((64, 128), F32)
    for c in range(one.shape[1] // 128):
        at = slice(c * 128, (c + 1) * 128)
        first = jnp.concatenate([one[:, at].astype(F32), two[:, at].astype(F32)], axis=0)
        second = jnp.concatenate([zero, three[:, at].astype(F32)], axis=0)
        lhs[at, 0:128] = first.T.astype(BF16)
        fixed[at, :] = second.T.astype(BF16)


def set_right(rhs, at, one, two, three):
    rhs[0:64, at] = one
    rhs[64:128, at] = two
    row = lax.broadcasted_iota(jnp.int32, three.shape, 0)
    rhs[128:192, at] = jnp.where(row < 48, 1.0, 0.0).astype(BF16)
    rhs[192:256, at] = three


def padded(cells, centre):
    row = lax.broadcasted_iota(jnp.int32, cells.shape, 0)
    kept = jnp.where(row < COMPONENTS, cells - centre, 0.0)
    return jnp.concatenate([kept, jnp.zeros((64 - ROWS, cells.shape[1]), F32)], axis=0)


def sinkhorn_kernel(
    con_any, tgt_any, tgt_mass_any,
    src_out, tgt_out, self_out,
    con_ref, tgt_ref, tgt_mass_ref,
    from_own, from_opp, opp, landed, ybuf, xfull, sbuf,
    lhs_y, lhs_s, fix_y, fix_s, rhs_x, cache_f, cache_p,
    spread_w, peaks, totals, wide_g, wide_s, state, gwide,
    sq_x, sq_y, sq_s, log_x, log_y, log_s, pot_p, pot_s, wide, pots_f,
    fb, pb, gb, pots, fin,
    relay_send, relay_recv, opp_send, opp_recv, own_sem, tgt_sem, self_sem, local_sem,
    fb_send, fb_recv, pb_send, pb_recv,
    gb_send, gb_recv, pot_send, pot_recv, fin_send, fin_recv, con_sem,
):
    x_lo, core, z_hi, z_lo, y, x_hi = place()
    sibling = device(x_lo, 1 - core, z_hi, z_lo, y, x_hi)
    twin = device(x_lo, core, z_hi, 1 - z_lo, y, x_hi)
    across = device(1 - x_lo, core, z_hi, z_lo, y, 1 - x_hi)
    straight = lax.rem(x_lo + core, 2)
    opposite = device(1 - x_lo, core, z_hi, z_lo, y, lax.rem(x_hi + straight, 2))
    y_hi, y_lo = lax.div(y, 2), lax.rem(y, 2)
    partner = device(
        lax.rem(x_lo + y_hi, 2), lax.rem(core + y_lo, 2), z_hi, lax.rem(z_lo + z_hi, 2), y, x_hi
    )
    alone = (y + z_hi) == 0
    g = x_lo * 4 + core * 2 + z_lo
    m = z_hi * 8 + y * 2 + x_hi

    def m_peer(k):
        return device(x_lo, core, lax.div(k, 8), z_lo, lax.rem(lax.div(k, 2), 4), lax.rem(k, 2))

    def g_peer(k):
        return device(lax.div(k, 4), lax.rem(lax.div(k, 2), 2), z_hi, lax.rem(k, 2), y, x_hi)

    m_others = [lax.rem(m + d, 16) for d in range(1, 16)]
    g_others = [lax.rem(g + d, 8) for d in range(1, 8)]

    barrier = pltpu.get_barrier_semaphore()
    peers = [m_peer(k) for k in m_others]
    peers += [g_peer(k) for k in g_others] + [across]
    for peer in peers:
        pl.semaphore_signal(barrier, inc=1, device_id=peer, device_id_type=MESH)

    loads = [
        pltpu.make_async_copy(a, b, con_sem.at[i])
        for i, (a, b) in enumerate(
            [
                (tgt_any, tgt_ref),
                (tgt_mass_any, tgt_mass_ref),
                (con_any.at[2], con_ref.at[1]),
                (con_any.at[0], con_ref.at[0]),
            ]
        )
    ]
    for copy in loads:
        copy.start()
    loads[0].wait()
    loads[1].wait()
    ybuf[z_lo, 48:ROWS, :] = jnp.zeros((ROWS - 48, HALF), F32)
    ybuf[z_lo, 0:COMPONENTS, :] = tgt_ref[...]
    ybuf[z_lo, COMPONENTS : COMPONENTS + 1, :] = tgt_mass_ref[...]

    pl.semaphore_wait(barrier, len(peers))

    def remote(src, dst, send, recv, to):
        return pltpu.make_async_remote_copy(
            src_ref=src, dst_ref=dst, send_sem=send, recv_sem=recv, device_id=to,
            device_id_type=MESH,
        )

    parts = [slice(c * 512, (c + 1) * 512) for c in range(4)]
    relays = [
        remote(con_any.at[3, :, s], from_opp.at[:, s], relay_send.at[c], relay_recv.at[c], sibling)
        for c, s in enumerate(parts)
    ]
    own = remote(con_any.at[1], from_own, own_sem.at[0], own_sem.at[1], sibling)
    tgt = remote(ybuf.at[z_lo], ybuf.at[z_lo], tgt_sem.at[0], tgt_sem.at[1], twin)
    tgt.start()

    for copy in relays:
        copy.start()
    own.start()
    onward = [
        remote(opp.at[:, s], landed.at[:, s], opp_send.at[c], opp_recv.at[c], opposite)
        for c, s in enumerate(parts)
    ]
    loads[2].wait()
    for c, s in enumerate(parts):
        relays[c].wait_recv()
        opp[:, s] = con_ref[1, :, s] + from_opp[:, s]
        onward[c].start()

    remote(ybuf.at[1 - z_lo], ybuf.at[1 - z_lo], tgt_sem.at[0], tgt_sem.at[1], twin).wait_recv()
    cells = jnp.concatenate([ybuf[0], ybuf[1]], axis=1)
    centre = jnp.sum(cells, axis=1, keepdims=True) * (1.0 / GROUP)
    kept = padded(cells, centre)
    to_rows(sq_y, jnp.sum(kept * kept, axis=0, keepdims=True) * SCALE)
    to_rows(log_y, jnp.log2(cells[COMPONENTS : COMPONENTS + 1, :]))
    high, middle, unused = pieces(kept)
    set_left(lhs_y, fix_y, high, high, middle)
    set_weights(lhs_y, fix_y, log_y[...] - sq_y[...])

    def put_wide(j, value):
        for r in range(TILE // 128):
            wide[pl.ds(TILE // 128 * j + r, 1), :] = value[:, r * 128 : (r + 1) * 128]

    loads[3].wait()
    own.wait_recv()

    half = pl.ds(pl.multiple_of(x_hi * HALF, HALF), HALF)
    shared = remote(xfull.at[:, half], sbuf, self_sem.at[0], self_sem.at[1], partner)
    kept_here = pltpu.make_async_copy(xfull.at[:, half], sbuf, local_sem)

    def arrive(j):
        if j % 2:
            return
        c = j // 2
        s = parts[c]
        onward[c].wait_recv()
        cells = con_ref[0, :, s] + from_own[:, s] + landed[:, s]
        xfull[:, s] = cells
        if c % 2:
            @pl.when((x_hi == c // 2) & alone)
            def _():
                kept_here.start()

            @pl.when((x_hi == c // 2) & jnp.logical_not(alone))
            def _():
                shared.start()

        kept = padded(cells, centre)
        to_rows(sq_x, jnp.sum(kept * kept, axis=0, keepdims=True) * SCALE, 4 * c)
        to_rows(log_x, jnp.log2(cells[COMPONENTS : COMPONENTS + 1, :]), 4 * c)
        high, middle, unused = pieces(kept * (2.0 * SCALE))
        set_right(rhs_x, s, high, middle, high)

    def spread(at, me, others, peer, send, recv):
        for k in others:
            remote(at.at[me], at.at[me], send, recv, peer(k)).start()

    def all_of(at, others, peer, send, recv):
        part = at.at[pl.ds(0, len(others))]
        return remote(part, part, send, recv, peer(others[0]))

    to_m, to_g = (m_others, m_peer), (g_others, g_peer)

    def f_box(it, n):
        return fb.at[it, n], fb_send.at[it, n], fb_recv.at[it, n]

    def g_box(it, n):
        return gb.at[it, n], gb_send.at[it, n], gb_recv.at[it, n]

    def p_box(it):
        return pb.at[it], pb_send.at[it], pb_recv.at[it]

    def send_f(it, n):
        at, send, recv = f_box(it, n)
        rows = slice(8 * n, 8 * n + 8)
        at[m] = wide[rows, :] - sq_x[rows, :]
        spread(at, m, *to_m, send, recv)

    def send_p(it):
        at, send, recv = p_box(it)
        at[m] = wide[...] - sq_x[...]
        spread(at, m, *to_m, send, recv)

    def send_g(it, n):
        at, send, recv = g_box(it, n)
        rows = slice(8 * n, 8 * n + 8)
        at[g] = gwide[rows, :] - log_y[rows, :]
        spread(at, g, *to_g, send, recv)

    def put_first(j, value):
        put_wide(j, value)
        if j % 4 == 3:
            send_f(0, j // 4)

    first_pass(lhs_y, rhs_x, cache_f, GROUP, put_first, arrive)

    pot_p[...] = jnp.zeros_like(pot_p)
    pot_s[...] = jnp.zeros_like(pot_s)

    half_rows = pl.ds(pl.multiple_of(x_hi * 8, 8), 8)

    def finish_p(it):
        at, send, recv = p_box(it)
        moved = all_of(at, *to_m, send, recv)
        moved.wait_recv()
        moved.wait_send()
        pot_p[...] = 0.5 * (pot_p[...] - TAU * log_sum(pb[it]))

        @pl.when((it < ITERS - 1) & jnp.logical_not(alone))
        def _():
            pots[0, it] = pot_p[half_rows, :]
            remote(
                pots.at[0, it], pots.at[1, it], pot_send.at[it], pot_recv.at[it], partner
            ).start()

    def iteration(it, carry):
        @pl.when(it > 0)
        def _():
            for n in range(2):
                at, send, recv = g_box(it - 1, n)
                moved = all_of(at, *to_g, send, recv)
                moved.wait_recv()
                spread_rows(wide_g, -TAU * log_sum(at[...]), 8 * n)
                if n == 0:
                    row_pass(cache_f, wide_g, (0, HALF), (0, 8), state, True, False, None)
                moved.wait_send()
            for n in range(2):
                tiles = (4 * n, 4 * n + 4)
                row_pass(cache_f, wide_g, (HALF, GROUP), tiles, state, False, True, put_wide)
                send_f(it, n)

        @pl.when(it == 0)
        def _():
            @pl.when(alone)
            def _():
                kept_here.wait()

            @pl.when(jnp.logical_not(alone))
            def _():
                shared.wait_recv()
                shared.wait_send()

            for copy in relays + onward + [own, tgt]:
                copy.wait_send()
            got = sbuf[...]
            columns = padded(got, centre)
            to_rows(sq_s, jnp.sum(columns * columns, axis=0, keepdims=True) * SCALE)
            to_rows(log_s, jnp.log2(got[COMPONENTS : COMPONENTS + 1, :]))
            upper, lower, unused = pieces(columns)
            set_left(lhs_s, fix_s, upper, upper, lower)
            set_weights(lhs_s, fix_s, log_s[...] - sq_s[...])

        @pl.when(it == 1)
        def _():
            finish_p(0)

        @pl.when(it > 0)
        def _():
            last = it - 1

            @pl.when(alone)
            def _():
                pot_s[...] = pot_p[half_rows, :]

            @pl.when(jnp.logical_not(alone))
            def _():
                moved = remote(
                    pots.at[0, last], pots.at[1, last], pot_send.at[last], pot_recv.at[last],
                    partner,
                )
                moved.wait_recv()
                moved.wait_send()
                pot_s[...] = pots[1, last]

            spread_rows(wide_s, pot_s[...])
            row_pass(cache_p, wide_s, (0, HALF), (0, 8), None, True, True, put_wide)
            send_p(it)

        sent = []
        for n in range(2):
            at, send, recv = f_box(it, n)
            sent.append(all_of(at, *to_m, send, recv))
            sent[n].wait_recv()
            rows = slice(8 * n, 8 * n + 8)
            pot_f = -TAU * log_sum(at[...])
            pots_f[rows, :] = pot_f
            weight = log_x[rows, :] + pot_f - sq_x[rows, :]
            if n == 0:
                column_pass(cache_f, weight, 0, (0, 16), spread_w, peaks, totals)
        for n in range(2):
            blocks = (8 * n, 8 * n + 8)
            column_pass(cache_f, weight, 1, blocks, spread_w, peaks, totals)
            over_lanes(peaks, totals, blocks, gwide)
            send_g(it, n)

        @pl.when(it == ITERS - 1)
        def _():
            fin[0, z_lo] = pots_f[...] * (1.0 / SCALE)
            remote(
                fin.at[0, z_lo], fin.at[0, z_lo], fin_send.at[0], fin_recv.at[0], twin
            ).start()

        @pl.when(it == 0)
        def _():
            first_pass(lhs_s, rhs_x, cache_p, HALF, put_wide)
            send_p(0)

        @pl.when(it > 0)
        def _():
            finish_p(it)

        @pl.when(it == ITERS - 1)
        def _():
            fin[1, z_lo] = pot_p[...] * (1.0 / SCALE)
            remote(
                fin.at[1, z_lo], fin.at[1, z_lo], fin_send.at[1], fin_recv.at[1], twin
            ).start()

        for copy in sent:
            copy.wait_send()
        return carry

    lax.fori_loop(0, ITERS, iteration, 0)

    for n in range(2):
        at, send, recv = g_box(ITERS - 1, n)
        moved = all_of(at, *to_g, send, recv)
        moved.wait_recv()
        moved.wait_send()
    tgt_out[...] = (-TAU / SCALE) * log_sum(gb[ITERS - 1, z_lo])
    for kind in range(2):
        remote(
            fin.at[kind, 1 - z_lo], fin.at[kind, 1 - z_lo], fin_send.at[kind], fin_recv.at[kind],
            twin,
        ).wait_recv()
        remote(
            fin.at[kind, z_lo], fin.at[kind, z_lo], fin_send.at[kind], fin_recv.at[kind], twin
        ).wait_send()
    src_out[0:16, :] = fin[0, 0]
    src_out[16:32, :] = fin[0, 1]
    self_out[0:16, :] = fin[1, 0]
    self_out[16:32, :] = fin[1, 1]


def on_device(
    src_features, src_mass, section_ids, shard_counts, section_offsets, tgt_features, tgt_mass
):
    vmem = pl.BlockSpec(memory_space=pltpu.VMEM)
    hbm = pl.BlockSpec(memory_space=pltpu.HBM)
    V, D = pltpu.VMEM, pltpu.SemaphoreType.DMA
    contributions = pl.pallas_call(
        relay_kernel,
        out_shape=jax.ShapeDtypeStruct((4, ROWS, GROUP), F32),
        in_specs=[pl.BlockSpec(memory_space=pltpu.SMEM)] + [hbm] * 4,
        out_specs=hbm,
        scratch_shapes=[
            V((ROWS, WIDTH), F32), V((COMPONENTS, CAP), F32), V((1, CAP), F32),
            V((1, CAP), jnp.int32), V((SECTIONS, COMPONENTS), F32), V((4, ROWS, GROUP), F32),
            D((4,)), D((3,)), D((4,)),
        ],
        compiler_params=pltpu.CompilerParams(vmem_limit_bytes=58 * 1024 * 1024),
    )(
        shard_counts,
        src_features,
        src_mass.reshape(1, CAP),
        section_ids.reshape(1, CAP),
        section_offsets.T,
    )
    rows16, rows8 = (16, 128), (8, 128)
    outs = pl.pallas_call(
        sinkhorn_kernel,
        out_shape=(
            V((32, 128), F32), V((8, 128), F32), V((32, 128), F32),
        ),
        in_specs=[hbm] * 3,
        out_specs=(vmem, vmem, vmem),
        scratch_shapes=[
            V((2, ROWS, GROUP), F32), V((COMPONENTS, HALF), F32), V((1, HALF), F32),
            V((ROWS, GROUP), F32), V((ROWS, GROUP), F32), V((ROWS, GROUP), F32),
            V((ROWS, GROUP), F32), V((2, ROWS, HALF), F32), V((ROWS, GROUP), F32),
            V((ROWS, HALF), F32),
            V((GROUP, 256), BF16), V((HALF, 256), BF16),
            V((GROUP, 128), BF16), V((HALF, 128), BF16), V((256, GROUP), BF16),
            V((TILES, GROUP, TILE), F32), V((TILES, HALF, TILE), F32),
            V((8, 8, 128), F32), V((GROUP, 128), F32), V((GROUP, 128), F32),
            V((GROUP, 128), F32), V((HALF, 128), F32), V((2, TILES, 8, TILE), F32), V(rows16, F32),
            V(rows16, F32), V(rows16, F32), V(rows8, F32),
            V(rows16, F32), V(rows16, F32), V(rows8, F32),
            V(rows16, F32), V(rows8, F32), V(rows16, F32), V(rows16, F32),
            V((ITERS, 2, 16) + rows8, F32), V((ITERS, 16) + rows16, F32),
            V((ITERS, 2, 8) + rows8, F32), V((2, ITERS - 1) + rows8, F32),
            V((2, 2) + rows16, F32),
            D((4,)), D((4,)), D((4,)), D((4,)), D((2,)), D((2,)), D((2,)), D,
            D((ITERS, 2)), D((ITERS, 2)), D((ITERS,)), D((ITERS,)), D((ITERS, 2)), D((ITERS, 2)),
            D((ITERS,)), D((ITERS,)), D((2,)), D((2,)),
            D((4,)),
        ],
        compiler_params=pltpu.CompilerParams(
            collective_id=0, has_side_effects=True, vmem_limit_bytes=58 * 1024 * 1024
        ),
    )(contributions, tgt_features, tgt_mass.reshape(1, HALF))
    return (outs[0].reshape(2 * GROUP), outs[1].reshape(HALF), outs[2].reshape(2 * GROUP))


def solution(mesh):
    return jax.shard_map(
        on_device,
        mesh=mesh,
        in_specs=(P(None, "src"), P("src"), P("src"), P(), P(), P(None, "tgt"), P("tgt")),
        out_specs=(P("src"), P("tgt"), P("src")),
        check_vma=False,
    )
```

```python
import jax
import jax.numpy as jnp
from jax import lax
from jax.experimental import pallas as pl
from jax.experimental.pallas import tpu as pltpu
from jax.sharding import PartitionSpec as P

COMPONENTS = 50
ROWS = 56
SECTIONS = 32
ITERS = 3
CAP = 8192
GROUP = 2048
HALF = 1024
SPAN = GROUP + 128
LEAD = GROUP
WIDTH = LEAD + CAP + SPAN

EPS = 0.05
TAU = 1.0 / (1.0 + EPS)
LOG2E = 1.4426950408889634
SCALE = LOG2E / EPS

F32 = jnp.float32
BF16 = jnp.bfloat16
MESH = pl.DeviceIdType.MESH
TILE = 256
TILES = GROUP // TILE
CHUNK = 256


def place():
    src, tgt = lax.axis_index("src"), lax.axis_index("tgt")
    z, rest = lax.div(tgt, 8), lax.rem(tgt, 8)
    return (
        lax.div(src, 2),
        lax.rem(src, 2),
        lax.div(z, 2),
        lax.rem(z, 2),
        lax.div(rest, 2),
        lax.rem(rest, 2),
    )


def device(x_lo, core, z_hi, z_lo, y, x_hi):
    return (x_lo * 2 + core, (z_hi * 2 + z_lo) * 8 + y * 2 + x_hi)


def pieces(value):
    high = value.astype(BF16)
    rest = value - high.astype(F32)
    middle = rest.astype(BF16)
    return high, middle, (rest - middle.astype(F32)).astype(BF16)


def correct(feats_ref, mass_ref, ids_ref, offsets_ref, held, ready):
    three = jnp.concatenate([p.astype(F32) for p in pieces(offsets_ref[...])], axis=0).astype(BF16)
    for at in range(0, CAP, 1024):
        ready(at)
        ids = ids_ref[:, at : at + 1024]
        section = lax.broadcasted_iota(jnp.int32, (3 * SECTIONS, 1024), 0) & (SECTIONS - 1)
        onehot = jnp.where(section == ids, 1.0, 0.0).astype(BF16)
        shift = lax.dot_general(
            three, onehot, (((0,), (0,)), ((), ())), preferred_element_type=F32
        )
        to = slice(LEAD + at, LEAD + at + 1024)
        held[48:ROWS, to] = jnp.zeros((ROWS - 48, 1024), F32)
        held[0:COMPONENTS, to] = feats_ref[:, at : at + 1024] - shift
        held[COMPONENTS : COMPONENTS + 1, to] = mass_ref[:, at : at + 1024]


def contribute(held, base, count, out):
    at = jnp.clip(base, -LEAD, CAP) + LEAD
    aligned = pl.multiple_of(lax.div(at, 128) * 128, 128)
    off = lax.rem(at, 128)
    turn = lax.rem(128 - off, 128)
    lane = lax.broadcasted_iota(jnp.int32, (ROWS, 128), 1)
    before = pltpu.roll(held[:, pl.ds(aligned, 128)], turn, 1)
    for t in range(GROUP // 128):
        after = pltpu.roll(
            held[:, pl.ds(pl.multiple_of(aligned + (t + 1) * 128, 128), 128)], turn, 1
        )
        value = jnp.where(lane < 128 - off, before, after)
        local = lane + (base + t * 128)
        out[:, t * 128 : (t + 1) * 128] = jnp.where((local >= 0) & (local < count), value, 0.0)
        before = after


def relay_kernel(
    counts_ref, feats_any, mass_any, ids_any, offsets_any, out_any,
    held, feats_ref, mass_ref, ids_ref, offsets_ref, out_ref, feats_sem, small_sem, out_sem,
):
    small = [
        pltpu.make_async_copy(a, b, small_sem.at[i])
        for i, (a, b) in enumerate(
            [(offsets_any, offsets_ref), (ids_any, ids_ref), (mass_any, mass_ref)]
        )
    ]
    large = [
        pltpu.make_async_copy(
            feats_any.at[:, at : at + 2048], feats_ref.at[:, at : at + 2048], feats_sem.at[i]
        )
        for i, at in enumerate(range(0, CAP, 2048))
    ]
    for copy in small + large:
        copy.start()
    x_lo, core, z_hi, z_lo, y, x_hi = place()
    mine = x_lo * 2 + core
    begin = jnp.int32(0)
    for k in range(3):
        begin = begin + jnp.where(k < mine, counts_ref[k], 0)
    count = counts_ref[mine]

    def ready(at):
        if at % 2048 == 0:
            large[at // 2048].wait()

    for copy in small:
        copy.wait()
    correct(feats_ref, mass_ref, ids_ref, offsets_ref, held, ready)
    moves = []
    for index in (3, 2, 1, 0):
        to_x, to_core = lax.rem(x_lo + index // 2, 2), lax.rem(core + index % 2, 2)
        base = (to_x * 2 + to_core) * (2 * GROUP) + z_lo * GROUP - begin
        contribute(held, base, count, out_ref.at[index])
        moves.append(
            pltpu.make_async_copy(out_ref.at[index], out_any.at[index], out_sem.at[index])
        )
        moves[-1].start()
    for copy in moves:
        copy.wait()


def log_sum(parts):
    peak = jnp.max(parts, axis=0)
    return peak + jnp.log2(jnp.sum(jnp.exp2(parts - peak[None]), axis=0))


def tree(op, parts):
    while len(parts) > 1:
        pairs = [op(a, b) for a, b in zip(parts[0::2], parts[1::2])]
        parts = pairs + parts[len(pairs) * 2 :]
    return parts[0]


def first_pass(lhs, rhs, cache, count, put, ready=None):
    chunk = min(CHUNK, count)

    def both(j, peak):
        tops, sums = [], []
        for at in range(0, count, chunk):
            if j < TILES:
                s = jnp.dot(
                    lhs[at : at + chunk, :], rhs[:, j * TILE : (j + 1) * TILE],
                    preferred_element_type=F32,
                )
                cache[j, at : at + chunk, :] = s
                s = s.reshape(chunk // 8, 8, TILE)
                tops.append(tree(jnp.maximum, [s[i] for i in range(chunk // 8)]))
            if peak is not None:
                e = [
                    jnp.exp2(cache[j - 1, row : row + 8, :] - peak)
                    for row in range(at, at + chunk, 8)
                ]
                sums.append(tree(jnp.add, e))
        if peak is not None:
            total = jnp.sum(tree(jnp.add, sums), axis=0, keepdims=True)
            put(j - 1, peak + jnp.log2(total))
        return jnp.max(tree(jnp.maximum, tops), axis=0, keepdims=True) if tops else None

    peak = None
    for j in range(TILES + 1):
        if ready is not None and j < TILES:
            ready(j)
        peak = both(j, peak)


def row_pass(cache, weight, span, tiles, state, begin, end, put):
    def body(j, carry):
        ends = [[], []]
        for at in range(span[0], span[1], 128):
            w = [weight[row : row + 8, :] for row in range(at, at + 128, 8)]
            for h in range(2):
                lanes = slice(h * 128, (h + 1) * 128)
                t = [cache[j, at + 8 * i : at + 8 * i + 8, lanes] + w[i] for i in range(16)]
                top = tree(jnp.maximum, t)
                ends[h].append((top, tree(jnp.add, [jnp.exp2(v - top) for v in t])))
        rows = []
        for h in range(2):
            lanes = slice(h * 128, (h + 1) * 128)
            if not begin:
                ends[h].append((state[0, j, :, lanes], state[1, j, :, lanes]))
            top = tree(jnp.maximum, [v[0] for v in ends[h]])
            part = tree(jnp.add, [v[1] * jnp.exp2(v[0] - top) for v in ends[h]])
            if end:
                most = jnp.max(top, axis=0, keepdims=True)
                part = jnp.sum(part * jnp.exp2(top - most), axis=0, keepdims=True)
                rows.append(most + jnp.log2(part))
            else:
                state[0, j, :, lanes] = top
                state[1, j, :, lanes] = part
        if end:
            put(j, jnp.concatenate(rows, axis=1))
        return carry

    lax.fori_loop(tiles[0], tiles[1], body, 0)


def column_pass(cache, weight, half, blocks, spread_w, peaks, totals):
    for r in range(8):
        spread_w[r] = jnp.broadcast_to(weight[r : r + 1, :], (8, 128))

    def body(block, carry):
        for sub in range(4):
            rows = pl.ds(pl.multiple_of(block * 128 + sub * 32, 32), 32)
            parts = []
            for r in range(8):
                lanes = slice(r % 2 * 128, r % 2 * 128 + 128)
                t = cache[half * 4 + r // 2, rows, lanes].reshape(4, 8, 128)
                parts.append(t + spread_w[r][None])
            top = tree(jnp.maximum, parts)
            if half:
                before = peaks[rows, :].reshape(4, 8, 128)
                top = jnp.maximum(top, before)
            sums = [jnp.exp2(t - top) for t in parts]
            if half:
                sums.append(totals[rows, :].reshape(4, 8, 128) * jnp.exp2(before - top))
            peaks[rows, :] = top.reshape(32, 128)
            totals[rows, :] = tree(jnp.add, sums).reshape(32, 128)
        return carry

    lax.fori_loop(blocks[0], blocks[1], body, 0)


def over_lanes(peaks, totals, blocks, out):
    for c in range(blocks[0], blocks[1]):
        at = slice(c * 128, (c + 1) * 128)
        turned = peaks[at, :].T
        top = jnp.max(turned, axis=0, keepdims=True)
        total = jnp.sum(totals[at, :].T * jnp.exp2(turned - top), axis=0, keepdims=True)
        out[c : c + 1, :] = top + jnp.log2(total)


def spread_rows(wide_w, weight, first=0):
    for c in range(weight.shape[0]):
        at = slice((first + c) * 128, (first + c + 1) * 128)
        wide_w[at, :] = jnp.broadcast_to(weight[c : c + 1, :], (128, 128)).T


def to_rows(ref, row, first=0):
    for r in range(row.shape[1] // 128):
        ref[first + r : first + r + 1, :] = row[:, r * 128 : (r + 1) * 128]


def block_rows(first, c):
    return pl.ds(pl.multiple_of(first + c * 128, 128), 128)


def set_left(lhs, first, one, two, three, weight):
    rows = weight.shape[0]
    parts = [p.astype(F32) for p in pieces(weight)]
    fill = jnp.zeros((64 - 3 * rows, 128), F32)
    for c in range(rows):
        at = slice(c * 128, (c + 1) * 128)
        upper = jnp.concatenate([one[:, at].astype(F32), two[:, at].astype(F32)], axis=0)
        row = lax.broadcasted_iota(jnp.int32, (rows, 128), 0)
        chosen = [jnp.where(row == c, p, 0.0) for p in parts]
        lower = jnp.concatenate(chosen + [fill, three[:, at].astype(F32)], axis=0)
        lhs[block_rows(first, c), 0:128] = upper.T.astype(BF16)
        lhs[block_rows(first, c), 128:256] = lower.T.astype(BF16)


def set_right(rhs, at, one, two, three):
    rhs[0:64, at] = one
    rhs[64:128, at] = two
    row = lax.broadcasted_iota(jnp.int32, three.shape, 0)
    rhs[128:192, at] = jnp.where(row < 24, 1.0, 0.0).astype(BF16)
    rhs[192:256, at] = three


def padded(cells, centre):
    row = lax.broadcasted_iota(jnp.int32, cells.shape, 0)
    kept = jnp.where(row < COMPONENTS, cells - centre, 0.0)
    return jnp.concatenate([kept, jnp.zeros((64 - ROWS, cells.shape[1]), F32)], axis=0)


def sinkhorn_kernel(
    con_any, tgt_any, tgt_mass_any,
    src_out, tgt_out, self_out,
    con_ref, tgt_ref, tgt_mass_ref,
    from_own, from_opp, opp, landed, ybuf, xfull, sbuf,
    lhs_y, lhs_s, rhs_x, cache_f, cache_p,
    spread_w, peaks, totals, wide_g, wide_s, state, gwide,
    sq_x, sq_s, log_x, log_y, log_s, pot_p, pot_s, wide, pots_f,
    fb, pb, gb, pots, fin,
    relay_send, relay_recv, opp_send, opp_recv, own_sem, tgt_sem, self_sem, local_sem,
    fb_send, fb_recv, pb_send, pb_recv,
    gb_send, gb_recv, pot_send, pot_recv, fin_send, fin_recv, con_sem,
):
    x_lo, core, z_hi, z_lo, y, x_hi = place()
    sibling = device(x_lo, 1 - core, z_hi, z_lo, y, x_hi)
    twin = device(x_lo, core, z_hi, 1 - z_lo, y, x_hi)
    across = device(1 - x_lo, core, z_hi, z_lo, y, 1 - x_hi)
    straight = lax.rem(x_lo + core, 2)
    opposite = device(1 - x_lo, core, z_hi, z_lo, y, lax.rem(x_hi + straight, 2))
    y_hi, y_lo = lax.div(y, 2), lax.rem(y, 2)
    partner = device(
        lax.rem(x_lo + y_hi, 2), lax.rem(core + y_lo, 2), z_hi, lax.rem(z_lo + z_hi, 2), y, x_hi
    )
    alone = (y + z_hi) == 0
    g = x_lo * 4 + core * 2 + z_lo
    m = z_hi * 8 + y * 2 + x_hi

    def m_peer(k):
        return device(x_lo, core, lax.div(k, 8), z_lo, lax.rem(lax.div(k, 2), 4), lax.rem(k, 2))

    def g_peer(k):
        return device(lax.div(k, 4), lax.rem(lax.div(k, 2), 2), z_hi, lax.rem(k, 2), y, x_hi)

    m_others = [lax.rem(m + d, 16) for d in range(1, 16)]
    g_others = [lax.rem(g + d, 8) for d in range(1, 8)]

    barrier = pltpu.get_barrier_semaphore()
    peers = [m_peer(k) for k in m_others]
    peers += [g_peer(k) for k in g_others] + [across]
    for peer in peers:
        pl.semaphore_signal(barrier, inc=1, device_id=peer, device_id_type=MESH)

    loads = [
        pltpu.make_async_copy(a, b, con_sem.at[i])
        for i, (a, b) in enumerate(
            [
                (tgt_any, tgt_ref),
                (tgt_mass_any, tgt_mass_ref),
                (con_any.at[2], con_ref.at[1]),
                (con_any.at[0], con_ref.at[0]),
            ]
        )
    ]
    for copy in loads:
        copy.start()
    loads[0].wait()
    loads[1].wait()
    ybuf[z_lo, 48:ROWS, :] = jnp.zeros((ROWS - 48, HALF), F32)
    ybuf[z_lo, 0:COMPONENTS, :] = tgt_ref[...]
    ybuf[z_lo, COMPONENTS : COMPONENTS + 1, :] = tgt_mass_ref[...]

    pl.semaphore_wait(barrier, len(peers))

    def remote(src, dst, send, recv, to):
        return pltpu.make_async_remote_copy(
            src_ref=src, dst_ref=dst, send_sem=send, recv_sem=recv, device_id=to,
            device_id_type=MESH,
        )

    parts = [slice(c * 512, (c + 1) * 512) for c in range(4)]
    relays = [
        remote(con_any.at[3, :, s], from_opp.at[:, s], relay_send.at[c], relay_recv.at[c], sibling)
        for c, s in enumerate(parts)
    ]
    own = remote(con_any.at[1], from_own, own_sem.at[0], own_sem.at[1], sibling)
    quarter = pl.ds(pl.multiple_of(core * 512, 512), 512)
    rest = pl.ds(pl.multiple_of((1 - core) * 512, 512), 512)
    here, there = ybuf.at[z_lo, :, quarter], ybuf.at[1 - z_lo, :, quarter]
    tgt = remote(here, here, tgt_sem.at[0], tgt_sem.at[1], twin)
    tgt.start()
    passed = remote(there, there, tgt_sem.at[2], tgt_sem.at[3], sibling)

    for copy in relays:
        copy.start()
    own.start()
    onward = [
        remote(opp.at[:, s], landed.at[:, s], opp_send.at[c], opp_recv.at[c], opposite)
        for c, s in enumerate(parts)
    ]

    def target(part, centre):
        first, at = part * HALF, pl.ds(pl.multiple_of(part * 8, 8), 8)
        cells = ybuf[part]
        kept = padded(cells, centre)
        square = jnp.sum(kept * kept, axis=0, keepdims=True) * SCALE
        mass = jnp.log2(cells[COMPONENTS : COMPONENTS + 1, :])
        log_y[at, :] = jnp.concatenate([mass[:, r * 128 : (r + 1) * 128] for r in range(8)], axis=0)
        square = jnp.concatenate([square[:, r * 128 : (r + 1) * 128] for r in range(8)], axis=0)
        high, middle, unused = pieces(kept)
        set_left(lhs_y, first, high, high, middle, log_y[at, :] - square)

    def pass_on(c):
        relays[c].wait_recv()
        opp[:, parts[c]] = con_ref[1, :, parts[c]] + from_opp[:, parts[c]]
        onward[c].start()

    centre = jnp.sum(ybuf[z_lo], axis=1, keepdims=True) * (1.0 / HALF)
    loads[2].wait()
    for c in range(4):
        pass_on(c)
    target(z_lo, centre)
    remote(there, there, tgt_sem.at[0], tgt_sem.at[1], twin).wait_recv()
    passed.start()
    handed = ybuf.at[1 - z_lo, :, rest]
    remote(handed, handed, tgt_sem.at[2], tgt_sem.at[3], sibling).wait_recv()
    target(1 - z_lo, centre)

    def put_wide(j, value):
        for r in range(TILE // 128):
            wide[pl.ds(TILE // 128 * j + r, 1), :] = value[:, r * 128 : (r + 1) * 128]

    loads[3].wait()
    own.wait_recv()

    half = pl.ds(pl.multiple_of(x_hi * HALF, HALF), HALF)
    shared = remote(xfull.at[:, half], sbuf, self_sem.at[0], self_sem.at[1], partner)
    kept_here = pltpu.make_async_copy(xfull.at[:, half], sbuf, local_sem)

    def arrive(j):
        if j % 2:
            return
        c = j // 2
        s = parts[c]
        onward[c].wait_recv()
        cells = con_ref[0, :, s] + from_own[:, s] + landed[:, s]
        xfull[:, s] = cells
        if c % 2:
            @pl.when((x_hi == c // 2) & alone)
            def _():
                kept_here.start()

            @pl.when((x_hi == c // 2) & jnp.logical_not(alone))
            def _():
                shared.start()

        kept = padded(cells, centre)
        to_rows(sq_x, jnp.sum(kept * kept, axis=0, keepdims=True) * SCALE, 4 * c)
        to_rows(log_x, jnp.log2(cells[COMPONENTS : COMPONENTS + 1, :]), 4 * c)
        high, middle, unused = pieces(kept * (2.0 * SCALE))
        set_right(rhs_x, s, high, middle, high)

    def spread(at, me, others, peer, send, recv):
        for k in others:
            remote(at.at[me], at.at[me], send, recv, peer(k)).start()

    def all_of(at, others, peer, send, recv):
        part = at.at[pl.ds(0, len(others))]
        return remote(part, part, send, recv, peer(others[0]))

    to_m, to_g = (m_others, m_peer), (g_others, g_peer)

    def f_box(it, n):
        return fb.at[it, n], fb_send.at[it, n], fb_recv.at[it, n]

    def g_box(it, n):
        return gb.at[it, n], gb_send.at[it, n], gb_recv.at[it, n]

    def p_box(it):
        return pb.at[it], pb_send.at[it], pb_recv.at[it]

    def send_f(it, n):
        at, send, recv = f_box(it, n)
        rows = slice(8 * n, 8 * n + 8)
        at[m] = wide[rows, :] - sq_x[rows, :]
        spread(at, m, *to_m, send, recv)

    def send_p(it):
        at, send, recv = p_box(it)
        at[m] = wide[...] - sq_x[...]
        spread(at, m, *to_m, send, recv)

    def send_g(it, n):
        at, send, recv = g_box(it, n)
        rows = slice(8 * n, 8 * n + 8)
        at[g] = gwide[rows, :] - log_y[rows, :]
        spread(at, g, *to_g, send, recv)

    def put_first(j, value):
        put_wide(j, value)
        if j % 4 == 3:
            send_f(0, j // 4)

    first_pass(lhs_y, rhs_x, cache_f, GROUP, put_first, arrive)

    pot_p[...] = jnp.zeros_like(pot_p)
    pot_s[...] = jnp.zeros_like(pot_s)

    half_rows = pl.ds(pl.multiple_of(x_hi * 8, 8), 8)

    def finish_p(it):
        at, send, recv = p_box(it)
        moved = all_of(at, *to_m, send, recv)
        moved.wait_recv()
        moved.wait_send()
        pot_p[...] = 0.5 * (pot_p[...] - TAU * log_sum(pb[it]))

        @pl.when((it < ITERS - 1) & jnp.logical_not(alone))
        def _():
            pots[0, it] = pot_p[half_rows, :]
            remote(
                pots.at[0, it], pots.at[1, it], pot_send.at[it], pot_recv.at[it], partner
            ).start()

    def iteration(it, carry):
        @pl.when(it > 0)
        def _():
            for n in range(2):
                at, send, recv = g_box(it - 1, n)
                moved = all_of(at, *to_g, send, recv)
                moved.wait_recv()
                spread_rows(wide_g, -TAU * log_sum(at[...]), 8 * n)
                if n == 0:
                    row_pass(cache_f, wide_g, (0, HALF), (0, 8), state, True, False, None)
                moved.wait_send()
            for n in range(2):
                tiles = (4 * n, 4 * n + 4)
                row_pass(cache_f, wide_g, (HALF, GROUP), tiles, state, False, True, put_wide)
                send_f(it, n)

        @pl.when(it == 0)
        def _():
            @pl.when(alone)
            def _():
                kept_here.wait()

            @pl.when(jnp.logical_not(alone))
            def _():
                shared.wait_recv()
                shared.wait_send()

            for copy in relays + onward + [own, tgt, passed]:
                copy.wait_send()
            got = sbuf[...]
            columns = padded(got, centre)
            to_rows(sq_s, jnp.sum(columns * columns, axis=0, keepdims=True) * SCALE)
            to_rows(log_s, jnp.log2(got[COMPONENTS : COMPONENTS + 1, :]))
            upper, lower, unused = pieces(columns)
            set_left(lhs_s, 0, upper, upper, lower, log_s[...] - sq_s[...])

        @pl.when(it == 1)
        def _():
            finish_p(0)

        @pl.when(it > 0)
        def _():
            last = it - 1

            @pl.when(alone)
            def _():
                pot_s[...] = pot_p[half_rows, :]

            @pl.when(jnp.logical_not(alone))
            def _():
                moved = remote(
                    pots.at[0, last], pots.at[1, last], pot_send.at[last], pot_recv.at[last],
                    partner,
                )
                moved.wait_recv()
                moved.wait_send()
                pot_s[...] = pots[1, last]

            spread_rows(wide_s, pot_s[...])
            row_pass(cache_p, wide_s, (0, HALF), (0, 8), None, True, True, put_wide)
            send_p(it)

        sent = []
        for n in range(2):
            at, send, recv = f_box(it, n)
            sent.append(all_of(at, *to_m, send, recv))
            sent[n].wait_recv()
            rows = slice(8 * n, 8 * n + 8)
            pot_f = -TAU * log_sum(at[...])
            pots_f[rows, :] = pot_f
            weight = log_x[rows, :] + pot_f - sq_x[rows, :]
            if n == 0:
                column_pass(cache_f, weight, 0, (0, 16), spread_w, peaks, totals)
        for n in range(2):
            blocks = (8 * n, 8 * n + 8)
            column_pass(cache_f, weight, 1, blocks, spread_w, peaks, totals)
            over_lanes(peaks, totals, blocks, gwide)
            send_g(it, n)

        @pl.when(it == ITERS - 1)
        def _():
            fin[0, z_lo] = pots_f[...] * (1.0 / SCALE)
            remote(
                fin.at[0, z_lo], fin.at[0, z_lo], fin_send.at[0], fin_recv.at[0], twin
            ).start()

        @pl.when(it == 0)
        def _():
            first_pass(lhs_s, rhs_x, cache_p, HALF, put_wide)
            send_p(0)

        @pl.when(it > 0)
        def _():
            finish_p(it)

        @pl.when(it == ITERS - 1)
        def _():
            fin[1, z_lo] = pot_p[...] * (1.0 / SCALE)
            remote(
                fin.at[1, z_lo], fin.at[1, z_lo], fin_send.at[1], fin_recv.at[1], twin
            ).start()

        for copy in sent:
            copy.wait_send()
        return carry

    lax.fori_loop(0, ITERS, iteration, 0)

    for n in range(2):
        at, send, recv = g_box(ITERS - 1, n)
        moved = all_of(at, *to_g, send, recv)
        moved.wait_recv()
        moved.wait_send()
    tgt_out[...] = (-TAU / SCALE) * log_sum(gb[ITERS - 1, z_lo])
    for kind in range(2):
        remote(
            fin.at[kind, 1 - z_lo], fin.at[kind, 1 - z_lo], fin_send.at[kind], fin_recv.at[kind],
            twin,
        ).wait_recv()
        remote(
            fin.at[kind, z_lo], fin.at[kind, z_lo], fin_send.at[kind], fin_recv.at[kind], twin
        ).wait_send()
    src_out[0:16, :] = fin[0, 0]
    src_out[16:32, :] = fin[0, 1]
    self_out[0:16, :] = fin[1, 0]
    self_out[16:32, :] = fin[1, 1]


def on_device(
    src_features, src_mass, section_ids, shard_counts, section_offsets, tgt_features, tgt_mass
):
    vmem = pl.BlockSpec(memory_space=pltpu.VMEM)
    hbm = pl.BlockSpec(memory_space=pltpu.HBM)
    V, D = pltpu.VMEM, pltpu.SemaphoreType.DMA
    contributions = pl.pallas_call(
        relay_kernel,
        out_shape=jax.ShapeDtypeStruct((4, ROWS, GROUP), F32),
        in_specs=[pl.BlockSpec(memory_space=pltpu.SMEM)] + [hbm] * 4,
        out_specs=hbm,
        scratch_shapes=[
            V((ROWS, WIDTH), F32), V((COMPONENTS, CAP), F32), V((1, CAP), F32),
            V((1, CAP), jnp.int32), V((SECTIONS, COMPONENTS), F32), V((4, ROWS, GROUP), F32),
            D((4,)), D((3,)), D((4,)),
        ],
        compiler_params=pltpu.CompilerParams(vmem_limit_bytes=58 * 1024 * 1024),
    )(
        shard_counts,
        src_features,
        src_mass.reshape(1, CAP),
        section_ids.reshape(1, CAP),
        section_offsets.T,
    )
    rows16, rows8 = (16, 128), (8, 128)
    outs = pl.pallas_call(
        sinkhorn_kernel,
        out_shape=(
            V((32, 128), F32), V((8, 128), F32), V((32, 128), F32),
        ),
        in_specs=[hbm] * 3,
        out_specs=(vmem, vmem, vmem),
        scratch_shapes=[
            V((2, ROWS, GROUP), F32), V((COMPONENTS, HALF), F32), V((1, HALF), F32),
            V((ROWS, GROUP), F32), V((ROWS, GROUP), F32), V((ROWS, GROUP), F32),
            V((ROWS, GROUP), F32), V((2, ROWS, HALF), F32), V((ROWS, GROUP), F32),
            V((ROWS, HALF), F32),
            V((GROUP, 256), BF16), V((HALF, 256), BF16),
            V((256, GROUP), BF16),
            V((TILES, GROUP, TILE), F32), V((TILES, HALF, TILE), F32),
            V((8, 8, 128), F32), V((GROUP, 128), F32), V((GROUP, 128), F32),
            V((GROUP, 128), F32), V((HALF, 128), F32), V((2, TILES, 8, TILE), F32), V(rows16, F32),
            V(rows16, F32), V(rows8, F32), V(rows16, F32), V(rows16, F32), V(rows8, F32),
            V(rows16, F32), V(rows8, F32), V(rows16, F32), V(rows16, F32),
            V((ITERS, 2, 16) + rows8, F32), V((ITERS, 16) + rows16, F32),
            V((ITERS, 2, 8) + rows8, F32), V((2, ITERS - 1) + rows8, F32),
            V((2, 2) + rows16, F32),
            D((4,)), D((4,)), D((4,)), D((4,)), D((2,)), D((4,)), D((2,)), D,
            D((ITERS, 2)), D((ITERS, 2)), D((ITERS,)), D((ITERS,)), D((ITERS, 2)), D((ITERS, 2)),
            D((ITERS,)), D((ITERS,)), D((2,)), D((2,)),
            D((4,)),
        ],
        compiler_params=pltpu.CompilerParams(
            collective_id=0, has_side_effects=True, vmem_limit_bytes=58 * 1024 * 1024
        ),
    )(contributions, tgt_features, tgt_mass.reshape(1, HALF))
    return (outs[0].reshape(2 * GROUP), outs[1].reshape(HALF), outs[2].reshape(2 * GROUP))


def solution(mesh):
    return jax.shard_map(
        on_device,
        mesh=mesh,
        in_specs=(P(None, "src"), P("src"), P("src"), P(), P(), P(None, "tgt"), P("tgt")),
        out_specs=(P("src"), P("tgt"), P("src")),
        check_vma=False,
    )
```

```python
import jax
import jax.numpy as jnp
from jax import lax
from jax.experimental import pallas as pl
from jax.experimental.pallas import tpu as pltpu
from jax.sharding import PartitionSpec as P

COMPONENTS = 50
ROWS = 56
SECTIONS = 32
ITERS = 3
CAP = 8192
GROUP = 2048
HALF = 1024
SPAN = GROUP + 128
LEAD = GROUP
WIDTH = LEAD + CAP + SPAN

EPS = 0.05
TAU = 1.0 / (1.0 + EPS)
LOG2E = 1.4426950408889634
SCALE = LOG2E / EPS

F32 = jnp.float32
BF16 = jnp.bfloat16
MESH = pl.DeviceIdType.MESH
TILE = 256
TILES = GROUP // TILE
CHUNK = 256


def place():
    src, tgt = lax.axis_index("src"), lax.axis_index("tgt")
    z, rest = lax.div(tgt, 8), lax.rem(tgt, 8)
    return (
        lax.div(src, 2),
        lax.rem(src, 2),
        lax.div(z, 2),
        lax.rem(z, 2),
        lax.div(rest, 2),
        lax.rem(rest, 2),
    )


def device(x_lo, core, z_hi, z_lo, y, x_hi):
    return (x_lo * 2 + core, (z_hi * 2 + z_lo) * 8 + y * 2 + x_hi)


def pieces(value):
    high = value.astype(BF16)
    rest = value - high.astype(F32)
    middle = rest.astype(BF16)
    return high, middle, (rest - middle.astype(F32)).astype(BF16)


def correct(feats_ref, mass_ref, ids_ref, offsets_ref, held, ready):
    three = jnp.concatenate([p.astype(F32) for p in pieces(offsets_ref[...])], axis=0).astype(BF16)
    for at in range(0, CAP, 1024):
        ready(at)
        ids = ids_ref[:, at : at + 1024]
        section = lax.broadcasted_iota(jnp.int32, (3 * SECTIONS, 1024), 0) & (SECTIONS - 1)
        onehot = jnp.where(section == ids, 1.0, 0.0).astype(BF16)
        shift = lax.dot_general(
            three, onehot, (((0,), (0,)), ((), ())), preferred_element_type=F32
        )
        to = slice(LEAD + at, LEAD + at + 1024)
        held[48:ROWS, to] = jnp.zeros((ROWS - 48, 1024), F32)
        held[0:COMPONENTS, to] = feats_ref[:, at : at + 1024] - shift
        held[COMPONENTS : COMPONENTS + 1, to] = mass_ref[:, at : at + 1024]


def contribute(held, base, count, out):
    at = jnp.clip(base, -LEAD, CAP) + LEAD
    aligned = pl.multiple_of(lax.div(at, 128) * 128, 128)
    off = lax.rem(at, 128)
    turn = lax.rem(128 - off, 128)
    lane = lax.broadcasted_iota(jnp.int32, (ROWS, 128), 1)
    before = pltpu.roll(held[:, pl.ds(aligned, 128)], turn, 1)
    for t in range(GROUP // 128):
        after = pltpu.roll(
            held[:, pl.ds(pl.multiple_of(aligned + (t + 1) * 128, 128), 128)], turn, 1
        )
        value = jnp.where(lane < 128 - off, before, after)
        local = lane + (base + t * 128)
        out[:, t * 128 : (t + 1) * 128] = jnp.where((local >= 0) & (local < count), value, 0.0)
        before = after


def relay_kernel(
    counts_ref, feats_any, mass_any, ids_any, offsets_any, out_ref,
    held, feats_ref, mass_ref, ids_ref, offsets_ref, feats_sem, small_sem,
):
    small = [
        pltpu.make_async_copy(a, b, small_sem.at[i])
        for i, (a, b) in enumerate(
            [(offsets_any, offsets_ref), (ids_any, ids_ref), (mass_any, mass_ref)]
        )
    ]
    large = [
        pltpu.make_async_copy(
            feats_any.at[:, at : at + 2048], feats_ref.at[:, at : at + 2048], feats_sem.at[i]
        )
        for i, at in enumerate(range(0, CAP, 2048))
    ]
    for copy in small + large:
        copy.start()
    x_lo, core, z_hi, z_lo, y, x_hi = place()
    mine = x_lo * 2 + core
    begin = jnp.int32(0)
    for k in range(3):
        begin = begin + jnp.where(k < mine, counts_ref[k], 0)
    count = counts_ref[mine]

    def ready(at):
        if at % 2048 == 0:
            large[at // 2048].wait()

    for copy in small:
        copy.wait()
    correct(feats_ref, mass_ref, ids_ref, offsets_ref, held, ready)
    for index in range(4):
        to_x, to_core = lax.rem(x_lo + index // 2, 2), lax.rem(core + index % 2, 2)
        base = (to_x * 2 + to_core) * (2 * GROUP) + z_lo * GROUP - begin
        contribute(held, base, count, out_ref.at[index])


def log_sum(parts):
    peak = jnp.max(parts, axis=0)
    return peak + jnp.log2(jnp.sum(jnp.exp2(parts - peak[None]), axis=0))


def tree(op, parts):
    while len(parts) > 1:
        pairs = [op(a, b) for a, b in zip(parts[0::2], parts[1::2])]
        parts = pairs + parts[len(pairs) * 2 :]
    return parts[0]


def first_pass(lhs, rhs, cache, count, put, ready=None):
    chunk = min(CHUNK, count)

    def both(j, peak):
        tops, sums = [], []
        for at in range(0, count, chunk):
            if j < TILES:
                s = jnp.dot(
                    lhs[at : at + chunk, :], rhs[:, j * TILE : (j + 1) * TILE],
                    preferred_element_type=F32,
                )
                cache[j, at : at + chunk, :] = s
                s = s.reshape(chunk // 8, 8, TILE)
                tops.append(tree(jnp.maximum, [s[i] for i in range(chunk // 8)]))
            if peak is not None:
                e = [
                    jnp.exp2(cache[j - 1, row : row + 8, :] - peak)
                    for row in range(at, at + chunk, 8)
                ]
                sums.append(tree(jnp.add, e))
        if peak is not None:
            total = jnp.sum(tree(jnp.add, sums), axis=0, keepdims=True)
            put(j - 1, peak + jnp.log2(total))
        return jnp.max(tree(jnp.maximum, tops), axis=0, keepdims=True) if tops else None

    peak = None
    for j in range(TILES + 1):
        if ready is not None and j < TILES:
            ready(j)
        peak = both(j, peak)


def several(body, span, each):
    def turn(i, carry):
        for k in range(each):
            body(i * each + k)
        return carry

    lax.fori_loop(span[0] // each, span[1] // each, turn, 0)


def row_pass(cache, weight, span, tiles, state, begin, end, put):
    def body(j):
        ends = [[], []]
        for at in range(span[0], span[1], 128):
            w = [weight[row : row + 8, :] for row in range(at, at + 128, 8)]
            for h in range(2):
                lanes = slice(h * 128, (h + 1) * 128)
                t = [cache[j, at + 8 * i : at + 8 * i + 8, lanes] + w[i] for i in range(16)]
                top = tree(jnp.maximum, t)
                ends[h].append((top, tree(jnp.add, [jnp.exp2(v - top) for v in t])))
        rows = []
        for h in range(2):
            lanes = slice(h * 128, (h + 1) * 128)
            if not begin:
                ends[h].append((state[0, j, :, lanes], state[1, j, :, lanes]))
            top = tree(jnp.maximum, [v[0] for v in ends[h]])
            part = tree(jnp.add, [v[1] * jnp.exp2(v[0] - top) for v in ends[h]])
            if end:
                most = jnp.max(top, axis=0, keepdims=True)
                part = jnp.sum(part * jnp.exp2(top - most), axis=0, keepdims=True)
                rows.append(most + jnp.log2(part))
            else:
                state[0, j, :, lanes] = top
                state[1, j, :, lanes] = part
        if end:
            put(j, jnp.concatenate(rows, axis=1))

    several(body, tiles, 2)


def column_pass(cache, weight, half, blocks, spread_w, peaks, totals):
    for r in range(8):
        spread_w[r] = jnp.broadcast_to(weight[r : r + 1, :], (8, 128))

    def body(block):
        for sub in range(4):
            rows = pl.ds(pl.multiple_of(block * 128 + sub * 32, 32), 32)
            parts = []
            for r in range(8):
                lanes = slice(r % 2 * 128, r % 2 * 128 + 128)
                t = cache[half * 4 + r // 2, rows, lanes].reshape(4, 8, 128)
                parts.append(t + spread_w[r][None])
            top = tree(jnp.maximum, parts)
            if half:
                before = peaks[rows, :].reshape(4, 8, 128)
                top = jnp.maximum(top, before)
            sums = [jnp.exp2(t - top) for t in parts]
            if half:
                sums.append(totals[rows, :].reshape(4, 8, 128) * jnp.exp2(before - top))
            peaks[rows, :] = top.reshape(32, 128)
            totals[rows, :] = tree(jnp.add, sums).reshape(32, 128)

    several(body, blocks, 4)


def over_lanes(peaks, totals, blocks, out):
    for c in range(blocks[0], blocks[1]):
        at = slice(c * 128, (c + 1) * 128)
        turned = peaks[at, :].T
        top = jnp.max(turned, axis=0, keepdims=True)
        total = jnp.sum(totals[at, :].T * jnp.exp2(turned - top), axis=0, keepdims=True)
        out[c : c + 1, :] = top + jnp.log2(total)


def spread_rows(wide_w, weight, first=0):
    for c in range(weight.shape[0]):
        at = slice((first + c) * 128, (first + c + 1) * 128)
        wide_w[at, :] = jnp.broadcast_to(weight[c : c + 1, :], (128, 128)).T


def to_rows(ref, row, first=0):
    for r in range(row.shape[1] // 128):
        ref[first + r : first + r + 1, :] = row[:, r * 128 : (r + 1) * 128]


def block_rows(first, c):
    return pl.ds(pl.multiple_of(first + c * 128, 128), 128)


def set_left(lhs, first, one, two, three, weight):
    rows = weight.shape[0]
    parts = [p.astype(F32) for p in pieces(weight)]
    fill = jnp.zeros((64 - 3 * rows, 128), F32)
    for c in range(rows):
        at = slice(c * 128, (c + 1) * 128)
        upper = jnp.concatenate([one[:, at].astype(F32), two[:, at].astype(F32)], axis=0)
        row = lax.broadcasted_iota(jnp.int32, (rows, 128), 0)
        chosen = [jnp.where(row == c, p, 0.0) for p in parts]
        lower = jnp.concatenate(chosen + [fill, three[:, at].astype(F32)], axis=0)
        lhs[block_rows(first, c), 0:128] = upper.T.astype(BF16)
        lhs[block_rows(first, c), 128:256] = lower.T.astype(BF16)


def set_right(rhs, at, one, two, three):
    rhs[0:64, at] = one
    rhs[64:128, at] = two
    row = lax.broadcasted_iota(jnp.int32, three.shape, 0)
    rhs[128:192, at] = jnp.where(row < 24, 1.0, 0.0).astype(BF16)
    rhs[192:256, at] = three


def padded(cells, centre):
    row = lax.broadcasted_iota(jnp.int32, cells.shape, 0)
    kept = jnp.where(row < COMPONENTS, cells - centre, 0.0)
    return jnp.concatenate([kept, jnp.zeros((64 - ROWS, cells.shape[1]), F32)], axis=0)


def sinkhorn_kernel(
    con_ref, tgt_any, tgt_mass_any,
    src_out, tgt_out, self_out,
    tgt_ref, tgt_mass_ref,
    from_own, from_opp, opp, landed, ybuf, xfull, sbuf,
    lhs_y, lhs_s, rhs_x, cache_f, cache_p,
    spread_w, peaks, totals, wide_g, wide_s, state, gwide,
    sq_x, sq_s, log_x, log_y, log_s, pot_p, pot_s, wide, pots_f,
    fb, pb, gb, pots, fin,
    relay_send, relay_recv, opp_send, opp_recv, own_sem, tgt_sem, self_sem, local_sem,
    fb_send, fb_recv, pb_send, pb_recv,
    gb_send, gb_recv, pot_send, pot_recv, fin_send, fin_recv, con_sem,
):
    x_lo, core, z_hi, z_lo, y, x_hi = place()
    sibling = device(x_lo, 1 - core, z_hi, z_lo, y, x_hi)
    twin = device(x_lo, core, z_hi, 1 - z_lo, y, x_hi)
    across = device(1 - x_lo, core, z_hi, z_lo, y, 1 - x_hi)
    straight = lax.rem(x_lo + core, 2)
    opposite = device(1 - x_lo, core, z_hi, z_lo, y, lax.rem(x_hi + straight, 2))
    y_hi, y_lo = lax.div(y, 2), lax.rem(y, 2)
    partner = device(
        lax.rem(x_lo + y_hi, 2), lax.rem(core + y_lo, 2), z_hi, lax.rem(z_lo + z_hi, 2), y, x_hi
    )
    alone = (y + z_hi) == 0
    g = x_lo * 4 + core * 2 + z_lo
    m = z_hi * 8 + y * 2 + x_hi

    def m_peer(k):
        return device(x_lo, core, lax.div(k, 8), z_lo, lax.rem(lax.div(k, 2), 4), lax.rem(k, 2))

    def g_peer(k):
        return device(lax.div(k, 4), lax.rem(lax.div(k, 2), 2), z_hi, lax.rem(k, 2), y, x_hi)

    m_others = [lax.rem(m + d, 16) for d in range(1, 16)]
    g_others = [lax.rem(g + d, 8) for d in range(1, 8)]

    barrier = pltpu.get_barrier_semaphore()
    peers = [m_peer(k) for k in m_others]
    peers += [g_peer(k) for k in g_others] + [across]
    for peer in peers:
        pl.semaphore_signal(barrier, inc=1, device_id=peer, device_id_type=MESH)

    loads = [
        pltpu.make_async_copy(a, b, con_sem.at[i])
        for i, (a, b) in enumerate(
            [(tgt_any, tgt_ref), (tgt_mass_any, tgt_mass_ref)]
        )
    ]
    for copy in loads:
        copy.start()
    loads[0].wait()
    loads[1].wait()
    ybuf[z_lo, 48:ROWS, :] = jnp.zeros((ROWS - 48, HALF), F32)
    ybuf[z_lo, 0:COMPONENTS, :] = tgt_ref[...]
    ybuf[z_lo, COMPONENTS : COMPONENTS + 1, :] = tgt_mass_ref[...]

    pl.semaphore_wait(barrier, len(peers))

    def remote(src, dst, send, recv, to):
        return pltpu.make_async_remote_copy(
            src_ref=src, dst_ref=dst, send_sem=send, recv_sem=recv, device_id=to,
            device_id_type=MESH,
        )

    parts = [slice(c * 512, (c + 1) * 512) for c in range(4)]
    relays = [
        remote(con_ref.at[3, :, s], from_opp.at[:, s], relay_send.at[c], relay_recv.at[c], sibling)
        for c, s in enumerate(parts)
    ]
    own = remote(con_ref.at[1], from_own, own_sem.at[0], own_sem.at[1], sibling)
    quarter = pl.ds(pl.multiple_of(core * 512, 512), 512)
    rest = pl.ds(pl.multiple_of((1 - core) * 512, 512), 512)
    here, there = ybuf.at[z_lo, :, quarter], ybuf.at[1 - z_lo, :, quarter]
    tgt = remote(here, here, tgt_sem.at[0], tgt_sem.at[1], twin)
    tgt.start()
    passed = remote(there, there, tgt_sem.at[2], tgt_sem.at[3], sibling)

    for copy in relays:
        copy.start()
    own.start()
    onward = [
        remote(opp.at[:, s], landed.at[:, s], opp_send.at[c], opp_recv.at[c], opposite)
        for c, s in enumerate(parts)
    ]

    def target(part, centre):
        first, at = part * HALF, pl.ds(pl.multiple_of(part * 8, 8), 8)
        cells = ybuf[part]
        kept = padded(cells, centre)
        square = jnp.sum(kept * kept, axis=0, keepdims=True) * SCALE
        mass = jnp.log2(cells[COMPONENTS : COMPONENTS + 1, :])
        log_y[at, :] = jnp.concatenate([mass[:, r * 128 : (r + 1) * 128] for r in range(8)], axis=0)
        square = jnp.concatenate([square[:, r * 128 : (r + 1) * 128] for r in range(8)], axis=0)
        high, middle, unused = pieces(kept)
        set_left(lhs_y, first, high, high, middle, log_y[at, :] - square)

    def pass_on(c):
        relays[c].wait_recv()
        opp[:, parts[c]] = con_ref[2, :, parts[c]] + from_opp[:, parts[c]]
        onward[c].start()

    centre = jnp.sum(ybuf[z_lo], axis=1, keepdims=True) * (1.0 / HALF)
    for c in range(4):
        pass_on(c)
    target(z_lo, centre)
    remote(there, there, tgt_sem.at[0], tgt_sem.at[1], twin).wait_recv()
    passed.start()
    handed = ybuf.at[1 - z_lo, :, rest]
    remote(handed, handed, tgt_sem.at[2], tgt_sem.at[3], sibling).wait_recv()
    target(1 - z_lo, centre)

    def put_wide(j, value):
        for r in range(TILE // 128):
            wide[pl.ds(TILE // 128 * j + r, 1), :] = value[:, r * 128 : (r + 1) * 128]

    own.wait_recv()

    half = pl.ds(pl.multiple_of(x_hi * HALF, HALF), HALF)
    shared = remote(xfull.at[:, half], sbuf, self_sem.at[0], self_sem.at[1], partner)
    kept_here = pltpu.make_async_copy(xfull.at[:, half], sbuf, local_sem)

    def arrive(j):
        if j % 2:
            return
        c = j // 2
        s = parts[c]
        onward[c].wait_recv()
        cells = con_ref[0, :, s] + from_own[:, s] + landed[:, s]
        xfull[:, s] = cells
        if c % 2:
            @pl.when((x_hi == c // 2) & alone)
            def _():
                kept_here.start()

            @pl.when((x_hi == c // 2) & jnp.logical_not(alone))
            def _():
                shared.start()

        kept = padded(cells, centre)
        to_rows(sq_x, jnp.sum(kept * kept, axis=0, keepdims=True) * SCALE, 4 * c)
        to_rows(log_x, jnp.log2(cells[COMPONENTS : COMPONENTS + 1, :]), 4 * c)
        high, middle, unused = pieces(kept * (2.0 * SCALE))
        set_right(rhs_x, s, high, middle, high)

    def spread(at, me, others, peer, send, recv):
        for k in others:
            remote(at.at[me], at.at[me], send, recv, peer(k)).start()

    def all_of(at, others, peer, send, recv):
        part = at.at[pl.ds(0, len(others))]
        return remote(part, part, send, recv, peer(others[0]))

    to_m, to_g = (m_others, m_peer), (g_others, g_peer)

    def f_box(it, n):
        return fb.at[it, n], fb_send.at[it, n], fb_recv.at[it, n]

    def g_box(it, n):
        return gb.at[it, n], gb_send.at[it, n], gb_recv.at[it, n]

    def p_box(it):
        return pb.at[it], pb_send.at[it], pb_recv.at[it]

    def send_f(it, n):
        at, send, recv = f_box(it, n)
        rows = slice(8 * n, 8 * n + 8)
        at[m] = wide[rows, :] - sq_x[rows, :]
        spread(at, m, *to_m, send, recv)

    def send_p(it):
        at, send, recv = p_box(it)
        at[m] = wide[...] - sq_x[...]
        spread(at, m, *to_m, send, recv)

    def send_g(it, n):
        at, send, recv = g_box(it, n)
        rows = slice(8 * n, 8 * n + 8)
        at[g] = gwide[rows, :] - log_y[rows, :]
        spread(at, g, *to_g, send, recv)

    def put_first(j, value):
        put_wide(j, value)
        if j % 4 == 3:
            send_f(0, j // 4)

    first_pass(lhs_y, rhs_x, cache_f, GROUP, put_first, arrive)

    pot_p[...] = jnp.zeros_like(pot_p)
    pot_s[...] = jnp.zeros_like(pot_s)

    half_rows = pl.ds(pl.multiple_of(x_hi * 8, 8), 8)

    def finish_p(it):
        at, send, recv = p_box(it)
        moved = all_of(at, *to_m, send, recv)
        moved.wait_recv()
        moved.wait_send()
        pot_p[...] = 0.5 * (pot_p[...] - TAU * log_sum(pb[it]))

        @pl.when((it < ITERS - 1) & jnp.logical_not(alone))
        def _():
            pots[0, it] = pot_p[half_rows, :]
            remote(
                pots.at[0, it], pots.at[1, it], pot_send.at[it], pot_recv.at[it], partner
            ).start()

    def iteration(it, carry):
        @pl.when(it > 0)
        def _():
            for n in range(2):
                at, send, recv = g_box(it - 1, n)
                moved = all_of(at, *to_g, send, recv)
                moved.wait_recv()
                spread_rows(wide_g, -TAU * log_sum(at[...]), 8 * n)
                if n == 0:
                    row_pass(cache_f, wide_g, (0, HALF), (0, 8), state, True, False, None)
                moved.wait_send()
            for n in range(2):
                tiles = (4 * n, 4 * n + 4)
                row_pass(cache_f, wide_g, (HALF, GROUP), tiles, state, False, True, put_wide)
                send_f(it, n)

        @pl.when(it == 0)
        def _():
            @pl.when(alone)
            def _():
                kept_here.wait()

            @pl.when(jnp.logical_not(alone))
            def _():
                shared.wait_recv()
                shared.wait_send()

            for copy in relays + onward + [own, tgt, passed]:
                copy.wait_send()
            got = sbuf[...]
            columns = padded(got, centre)
            to_rows(sq_s, jnp.sum(columns * columns, axis=0, keepdims=True) * SCALE)
            to_rows(log_s, jnp.log2(got[COMPONENTS : COMPONENTS + 1, :]))
            upper, lower, unused = pieces(columns)
            set_left(lhs_s, 0, upper, upper, lower, log_s[...] - sq_s[...])

        @pl.when(it == 1)
        def _():
            finish_p(0)

        @pl.when(it > 0)
        def _():
            last = it - 1

            @pl.when(alone)
            def _():
                pot_s[...] = pot_p[half_rows, :]

            @pl.when(jnp.logical_not(alone))
            def _():
                moved = remote(
                    pots.at[0, last], pots.at[1, last], pot_send.at[last], pot_recv.at[last],
                    partner,
                )
                moved.wait_recv()
                moved.wait_send()
                pot_s[...] = pots[1, last]

            spread_rows(wide_s, pot_s[...])
            row_pass(cache_p, wide_s, (0, HALF), (0, 8), None, True, True, put_wide)
            send_p(it)

        sent = []
        for n in range(2):
            at, send, recv = f_box(it, n)
            sent.append(all_of(at, *to_m, send, recv))
            sent[n].wait_recv()
            rows = slice(8 * n, 8 * n + 8)
            pot_f = -TAU * log_sum(at[...])
            pots_f[rows, :] = pot_f
            weight = log_x[rows, :] + pot_f - sq_x[rows, :]
            if n == 0:
                column_pass(cache_f, weight, 0, (0, 16), spread_w, peaks, totals)
        for n in range(2):
            blocks = (8 * n, 8 * n + 8)
            column_pass(cache_f, weight, 1, blocks, spread_w, peaks, totals)
            over_lanes(peaks, totals, blocks, gwide)
            send_g(it, n)

        @pl.when(it == ITERS - 1)
        def _():
            fin[0, z_lo] = pots_f[...] * (1.0 / SCALE)
            remote(
                fin.at[0, z_lo], fin.at[0, z_lo], fin_send.at[0], fin_recv.at[0], twin
            ).start()

        @pl.when(it == 0)
        def _():
            first_pass(lhs_s, rhs_x, cache_p, HALF, put_wide)
            send_p(0)

        @pl.when(it > 0)
        def _():
            finish_p(it)

        @pl.when(it == ITERS - 1)
        def _():
            fin[1, z_lo] = pot_p[...] * (1.0 / SCALE)
            remote(
                fin.at[1, z_lo], fin.at[1, z_lo], fin_send.at[1], fin_recv.at[1], twin
            ).start()

        for copy in sent:
            copy.wait_send()
        return carry

    lax.fori_loop(0, ITERS, iteration, 0)

    for n in range(2):
        at, send, recv = g_box(ITERS - 1, n)
        moved = all_of(at, *to_g, send, recv)
        moved.wait_recv()
        moved.wait_send()
    tgt_out[...] = (-TAU / SCALE) * log_sum(gb[ITERS - 1, z_lo])
    for kind in range(2):
        remote(
            fin.at[kind, 1 - z_lo], fin.at[kind, 1 - z_lo], fin_send.at[kind], fin_recv.at[kind],
            twin,
        ).wait_recv()
        remote(
            fin.at[kind, z_lo], fin.at[kind, z_lo], fin_send.at[kind], fin_recv.at[kind], twin
        ).wait_send()
    src_out[0:16, :] = fin[0, 0]
    src_out[16:32, :] = fin[0, 1]
    self_out[0:16, :] = fin[1, 0]
    self_out[16:32, :] = fin[1, 1]


def store_kernel(a, b, c, a_out, b_out, c_out, sem):
    copies = [
        pltpu.make_async_copy(x, y, sem.at[i])
        for i, (x, y) in enumerate([(a, a_out), (b, b_out), (c, c_out)])
    ]
    for copy in copies:
        copy.start()
    for copy in copies:
        copy.wait()


def on_device(
    src_features, src_mass, section_ids, shard_counts, section_offsets, tgt_features, tgt_mass
):
    vmem = pl.BlockSpec(memory_space=pltpu.VMEM)
    hbm = pl.BlockSpec(memory_space=pltpu.HBM)
    V, D = pltpu.VMEM, pltpu.SemaphoreType.DMA
    contributions = pl.pallas_call(
        relay_kernel,
        out_shape=V((4, ROWS, GROUP), F32),
        in_specs=[pl.BlockSpec(memory_space=pltpu.SMEM)] + [hbm] * 4,
        out_specs=vmem,
        scratch_shapes=[
            V((ROWS, WIDTH), F32), V((COMPONENTS, CAP), F32), V((1, CAP), F32),
            V((1, CAP), jnp.int32), V((SECTIONS, COMPONENTS), F32), D((4,)), D((3,)),
        ],
        compiler_params=pltpu.CompilerParams(vmem_limit_bytes=58 * 1024 * 1024),
    )(
        shard_counts,
        src_features,
        src_mass.reshape(1, CAP),
        section_ids.reshape(1, CAP),
        section_offsets.T,
    )
    rows16, rows8 = (16, 128), (8, 128)
    outs = pl.pallas_call(
        sinkhorn_kernel,
        out_shape=(
            V((32, 128), F32), V((8, 128), F32), V((32, 128), F32),
        ),
        in_specs=[vmem, hbm, hbm],
        out_specs=(vmem, vmem, vmem),
        scratch_shapes=[
            V((COMPONENTS, HALF), F32), V((1, HALF), F32),
            V((ROWS, GROUP), F32), V((ROWS, GROUP), F32), V((ROWS, GROUP), F32),
            V((ROWS, GROUP), F32), V((2, ROWS, HALF), F32), V((ROWS, GROUP), F32),
            V((ROWS, HALF), F32),
            V((GROUP, 256), BF16), V((HALF, 256), BF16),
            V((256, GROUP), BF16),
            V((TILES, GROUP, TILE), F32), V((TILES, HALF, TILE), F32),
            V((8, 8, 128), F32), V((GROUP, 128), F32), V((GROUP, 128), F32),
            V((GROUP, 128), F32), V((HALF, 128), F32), V((2, TILES, 8, TILE), F32), V(rows16, F32),
            V(rows16, F32), V(rows8, F32), V(rows16, F32), V(rows16, F32), V(rows8, F32),
            V(rows16, F32), V(rows8, F32), V(rows16, F32), V(rows16, F32),
            V((ITERS, 2, 16) + rows8, F32), V((ITERS, 16) + rows16, F32),
            V((ITERS, 2, 8) + rows8, F32), V((2, ITERS - 1) + rows8, F32),
            V((2, 2) + rows16, F32),
            D((4,)), D((4,)), D((4,)), D((4,)), D((2,)), D((4,)), D((2,)), D,
            D((ITERS, 2)), D((ITERS, 2)), D((ITERS,)), D((ITERS,)), D((ITERS, 2)), D((ITERS, 2)),
            D((ITERS,)), D((ITERS,)), D((2,)), D((2,)),
            D((2,)),
        ],
        compiler_params=pltpu.CompilerParams(
            collective_id=0, has_side_effects=True, vmem_limit_bytes=50 * 1024 * 1024
        ),
    )(contributions, tgt_features, tgt_mass.reshape(1, HALF))
    outs = pl.pallas_call(
        store_kernel,
        out_shape=tuple(jax.ShapeDtypeStruct(o.shape, F32) for o in outs),
        in_specs=[vmem] * 3,
        out_specs=(hbm, hbm, hbm),
        scratch_shapes=[D((3,))],
    )(*outs)
    return (outs[0].reshape(2 * GROUP), outs[1].reshape(HALF), outs[2].reshape(2 * GROUP))


def solution(mesh):
    return jax.shard_map(
        on_device,
        mesh=mesh,
        in_specs=(P(None, "src"), P("src"), P("src"), P(), P(), P(None, "tgt"), P("tgt")),
        out_specs=(P("src"), P("tgt"), P("src")),
        check_vma=False,
    )
```

```python
import jax
import jax.numpy as jnp
from jax import lax
from jax.experimental import pallas as pl
from jax.experimental.pallas import tpu as pltpu
from jax.sharding import PartitionSpec as P

COMPONENTS = 50
ROWS = 56
SECTIONS = 32
ITERS = 3
CAP = 8192
GROUP = 2048
HALF = 1024
SPAN = GROUP + 128
LEAD = GROUP
WIDTH = LEAD + CAP + SPAN

EPS = 0.05
TAU = 1.0 / (1.0 + EPS)
LOG2E = 1.4426950408889634
SCALE = LOG2E / EPS

F32 = jnp.float32
BF16 = jnp.bfloat16
MESH = pl.DeviceIdType.MESH
TILE = 256
TILES = GROUP // TILE
CHUNK = 256


def place():
    src, tgt = lax.axis_index("src"), lax.axis_index("tgt")
    z, rest = lax.div(tgt, 8), lax.rem(tgt, 8)
    return (
        lax.div(src, 2),
        lax.rem(src, 2),
        lax.div(z, 2),
        lax.rem(z, 2),
        lax.div(rest, 2),
        lax.rem(rest, 2),
    )


def device(x_lo, core, z_hi, z_lo, y, x_hi):
    return (x_lo * 2 + core, (z_hi * 2 + z_lo) * 8 + y * 2 + x_hi)


def pieces(value):
    high = value.astype(BF16)
    rest = value - high.astype(F32)
    middle = rest.astype(BF16)
    return high, middle, (rest - middle.astype(F32)).astype(BF16)


def correct(feats_ref, mass_ref, ids_ref, offsets_ref, held, ready):
    three = jnp.concatenate([p.astype(F32) for p in pieces(offsets_ref[...])], axis=0).astype(BF16)
    for at in range(0, CAP, 1024):
        ready(at)
        ids = ids_ref[:, at : at + 1024]
        section = lax.broadcasted_iota(jnp.int32, (3 * SECTIONS, 1024), 0) & (SECTIONS - 1)
        onehot = jnp.where(section == ids, 1.0, 0.0).astype(BF16)
        shift = lax.dot_general(
            three, onehot, (((0,), (0,)), ((), ())), preferred_element_type=F32
        )
        to = slice(LEAD + at, LEAD + at + 1024)
        held[48:ROWS, to] = jnp.zeros((ROWS - 48, 1024), F32)
        held[0:COMPONENTS, to] = feats_ref[:, at : at + 1024] - shift
        held[COMPONENTS : COMPONENTS + 1, to] = mass_ref[:, at : at + 1024]


def contribute(held, base, count, out):
    at = jnp.clip(base, -LEAD, CAP) + LEAD
    aligned = pl.multiple_of(lax.div(at, 128) * 128, 128)
    off = lax.rem(at, 128)
    turn = lax.rem(128 - off, 128)
    lane = lax.broadcasted_iota(jnp.int32, (ROWS, 128), 1)
    before = pltpu.roll(held[:, pl.ds(aligned, 128)], turn, 1)
    for t in range(GROUP // 128):
        after = pltpu.roll(
            held[:, pl.ds(pl.multiple_of(aligned + (t + 1) * 128, 128), 128)], turn, 1
        )
        value = jnp.where(lane < 128 - off, before, after)
        local = lane + (base + t * 128)
        out[:, t * 128 : (t + 1) * 128] = jnp.where((local >= 0) & (local < count), value, 0.0)
        before = after


def relay_kernel(
    counts_ref, feats_any, mass_any, ids_any, offsets_any, out_ref,
    held, feats_ref, mass_ref, ids_ref, offsets_ref, feats_sem, small_sem,
):
    small = [
        pltpu.make_async_copy(a, b, small_sem.at[i])
        for i, (a, b) in enumerate(
            [(offsets_any, offsets_ref), (ids_any, ids_ref), (mass_any, mass_ref)]
        )
    ]
    large = [
        pltpu.make_async_copy(
            feats_any.at[:, at : at + 2048], feats_ref.at[:, at : at + 2048], feats_sem.at[i]
        )
        for i, at in enumerate(range(0, CAP, 2048))
    ]
    for copy in small + large:
        copy.start()
    x_lo, core, z_hi, z_lo, y, x_hi = place()
    mine = x_lo * 2 + core
    begin = jnp.int32(0)
    for k in range(3):
        begin = begin + jnp.where(k < mine, counts_ref[k], 0)
    count = counts_ref[mine]

    def ready(at):
        if at % 2048 == 0:
            large[at // 2048].wait()

    for copy in small:
        copy.wait()
    correct(feats_ref, mass_ref, ids_ref, offsets_ref, held, ready)
    for index in range(4):
        to_x, to_core = lax.rem(x_lo + index // 2, 2), lax.rem(core + index % 2, 2)
        straight = lax.rem(x_lo + to_core, 2) * (index // 2)
        base = (to_x * 2 + to_core) * (2 * GROUP) + lax.rem(x_hi + straight, 2) * GROUP - begin
        contribute(held, base, count, out_ref.at[index])


def log_sum(parts):
    peak = jnp.max(parts, axis=0)
    return peak + jnp.log2(jnp.sum(jnp.exp2(parts - peak[None]), axis=0))


def tree(op, parts):
    while len(parts) > 1:
        pairs = [op(a, b) for a, b in zip(parts[0::2], parts[1::2])]
        parts = pairs + parts[len(pairs) * 2 :]
    return parts[0]


def first_pass(lhs, rhs, cache, count, put, ready=None):
    chunk = min(CHUNK, count)

    def both(j, peak):
        tops, sums = [], []
        for at in range(0, count, chunk):
            if j < TILES:
                s = jnp.dot(
                    lhs[at : at + chunk, :], rhs[:, j * TILE : (j + 1) * TILE],
                    preferred_element_type=F32,
                )
                cache[j, at : at + chunk, :] = s
                s = s.reshape(chunk // 8, 8, TILE)
                tops.append(tree(jnp.maximum, [s[i] for i in range(chunk // 8)]))
            if peak is not None:
                e = [
                    jnp.exp2(cache[j - 1, row : row + 8, :] - peak)
                    for row in range(at, at + chunk, 8)
                ]
                sums.append(tree(jnp.add, e))
        if peak is not None:
            total = jnp.sum(tree(jnp.add, sums), axis=0, keepdims=True)
            put(j - 1, peak + jnp.log2(total))
        return jnp.max(tree(jnp.maximum, tops), axis=0, keepdims=True) if tops else None

    peak = None
    for j in range(TILES + 1):
        if ready is not None and j < TILES:
            ready(j)
        peak = both(j, peak)


def several(body, span, each):
    def turn(i, carry):
        for k in range(each):
            body(i * each + k)
        return carry

    lax.fori_loop(span[0] // each, span[1] // each, turn, 0)


def row_pass(cache, weight, span, tiles, state, begin, end, put):
    def body(j):
        ends = [[], []]
        for at in range(span[0], span[1], 128):
            w = [weight[row : row + 8, :] for row in range(at, at + 128, 8)]
            for h in range(2):
                lanes = slice(h * 128, (h + 1) * 128)
                t = [cache[j, at + 8 * i : at + 8 * i + 8, lanes] + w[i] for i in range(16)]
                top = tree(jnp.maximum, t)
                ends[h].append((top, tree(jnp.add, [jnp.exp2(v - top) for v in t])))
        rows = []
        for h in range(2):
            lanes = slice(h * 128, (h + 1) * 128)
            if not begin:
                ends[h].append((state[0, j, :, lanes], state[1, j, :, lanes]))
            top = tree(jnp.maximum, [v[0] for v in ends[h]])
            part = tree(jnp.add, [v[1] * jnp.exp2(v[0] - top) for v in ends[h]])
            if end:
                most = jnp.max(top, axis=0, keepdims=True)
                part = jnp.sum(part * jnp.exp2(top - most), axis=0, keepdims=True)
                rows.append(most + jnp.log2(part))
            else:
                state[0, j, :, lanes] = top
                state[1, j, :, lanes] = part
        if end:
            put(j, jnp.concatenate(rows, axis=1))

    several(body, tiles, 2)


def column_pass(cache, weight, half, blocks, spread_w, peaks, totals):
    for r in range(8):
        spread_w[r] = jnp.broadcast_to(weight[r : r + 1, :], (8, 128))

    def body(block):
        for sub in range(4):
            rows = pl.ds(pl.multiple_of(block * 128 + sub * 32, 32), 32)
            parts = []
            for r in range(8):
                lanes = slice(r % 2 * 128, r % 2 * 128 + 128)
                t = cache[half * 4 + r // 2, rows, lanes].reshape(4, 8, 128)
                parts.append(t + spread_w[r][None])
            top = tree(jnp.maximum, parts)
            if half:
                before = peaks[rows, :].reshape(4, 8, 128)
                top = jnp.maximum(top, before)
            sums = [jnp.exp2(t - top) for t in parts]
            if half:
                sums.append(totals[rows, :].reshape(4, 8, 128) * jnp.exp2(before - top))
            peaks[rows, :] = top.reshape(32, 128)
            totals[rows, :] = tree(jnp.add, sums).reshape(32, 128)

    several(body, blocks, 4)


def over_lanes(peaks, totals, blocks, out):
    for c in range(blocks[0], blocks[1]):
        at = slice(c * 128, (c + 1) * 128)
        turned = peaks[at, :].T
        top = jnp.max(turned, axis=0, keepdims=True)
        total = jnp.sum(totals[at, :].T * jnp.exp2(turned - top), axis=0, keepdims=True)
        out[c : c + 1, :] = top + jnp.log2(total)


def spread_rows(wide_w, weight, first=0):
    for c in range(weight.shape[0]):
        at = slice((first + c) * 128, (first + c + 1) * 128)
        wide_w[at, :] = jnp.broadcast_to(weight[c : c + 1, :], (128, 128)).T


def to_rows(ref, row, first=0):
    for r in range(row.shape[1] // 128):
        ref[first + r : first + r + 1, :] = row[:, r * 128 : (r + 1) * 128]


def block_rows(first, c):
    return pl.ds(pl.multiple_of(first + c * 128, 128), 128)


def set_left(lhs, first, one, two, three, weight):
    rows = weight.shape[0]
    parts = [p.astype(F32) for p in pieces(weight)]
    fill = jnp.zeros((64 - 3 * rows, 128), F32)
    for c in range(rows):
        at = slice(c * 128, (c + 1) * 128)
        upper = jnp.concatenate([one[:, at].astype(F32), two[:, at].astype(F32)], axis=0)
        row = lax.broadcasted_iota(jnp.int32, (rows, 128), 0)
        chosen = [jnp.where(row == c, p, 0.0) for p in parts]
        lower = jnp.concatenate(chosen + [fill, three[:, at].astype(F32)], axis=0)
        lhs[block_rows(first, c), 0:128] = upper.T.astype(BF16)
        lhs[block_rows(first, c), 128:256] = lower.T.astype(BF16)


def set_right(rhs, at, one, two, three):
    rhs[0:64, at] = one
    rhs[64:128, at] = two
    row = lax.broadcasted_iota(jnp.int32, three.shape, 0)
    rhs[128:192, at] = jnp.where(row < 24, 1.0, 0.0).astype(BF16)
    rhs[192:256, at] = three


def padded(cells, centre):
    row = lax.broadcasted_iota(jnp.int32, cells.shape, 0)
    kept = jnp.where(row < COMPONENTS, cells - centre, 0.0)
    return jnp.concatenate([kept, jnp.zeros((64 - ROWS, cells.shape[1]), F32)], axis=0)


def sinkhorn_kernel(
    con_ref, tgt_any, tgt_mass_any,
    src_out, tgt_out, self_out,
    tgt_ref, tgt_mass_ref,
    from_own, from_opp, opp, landed, ybuf, xfull, sbuf,
    lhs_y, lhs_s, rhs_x, cache_f, cache_p,
    spread_w, peaks, totals, wide_g, wide_s, state, gwide,
    sq_x, sq_s, log_x, log_y, log_s, pot_p, pot_s, wide, pots_f,
    fb, pb, gb, pots, fin,
    relay_send, relay_recv, opp_send, opp_recv, own_sem, tgt_sem, self_sem, local_sem,
    fb_send, fb_recv, pb_send, pb_recv,
    gb_send, gb_recv, pot_send, pot_recv, fin_send, fin_recv, con_sem,
):
    x_lo, core, z_hi, z_lo, y, x_hi = place()
    sibling = device(x_lo, 1 - core, z_hi, z_lo, y, x_hi)
    twin = device(x_lo, core, z_hi, z_lo, y, 1 - x_hi)
    across = device(1 - x_lo, core, z_hi, z_lo, y, 1 - x_hi)
    straight = lax.rem(x_lo + core, 2)
    opposite = device(1 - x_lo, core, z_hi, z_lo, y, lax.rem(x_hi + straight, 2))
    y_hi, y_lo = lax.div(y, 2), lax.rem(y, 2)
    partner = device(
        lax.rem(x_lo + y_hi, 2), lax.rem(core + y_lo, 2), z_hi, z_lo, y, lax.rem(x_hi + z_hi, 2)
    )
    alone = (y + z_hi) == 0
    g = x_lo * 4 + core * 2 + x_hi
    m = z_hi * 8 + z_lo * 4 + y

    def m_peer(k):
        return device(x_lo, core, lax.div(k, 8), lax.rem(lax.div(k, 4), 2), lax.rem(k, 4), x_hi)

    def g_peer(k):
        return device(lax.div(k, 4), lax.rem(lax.div(k, 2), 2), z_hi, z_lo, y, lax.rem(k, 2))

    m_others = [lax.rem(m + d, 16) for d in range(1, 16)]
    g_others = [lax.rem(g + d, 8) for d in range(1, 8)]

    barrier = pltpu.get_barrier_semaphore()
    peers = [m_peer(k) for k in m_others]
    peers += [g_peer(k) for k in g_others]
    for peer in peers:
        pl.semaphore_signal(barrier, inc=1, device_id=peer, device_id_type=MESH)

    loads = [
        pltpu.make_async_copy(a, b, con_sem.at[i])
        for i, (a, b) in enumerate(
            [(tgt_any, tgt_ref), (tgt_mass_any, tgt_mass_ref)]
        )
    ]
    for copy in loads:
        copy.start()
    loads[0].wait()
    loads[1].wait()
    ybuf[x_hi, 48:ROWS, :] = jnp.zeros((ROWS - 48, HALF), F32)
    ybuf[x_hi, 0:COMPONENTS, :] = tgt_ref[...]
    ybuf[x_hi, COMPONENTS : COMPONENTS + 1, :] = tgt_mass_ref[...]

    pl.semaphore_wait(barrier, len(peers))

    def remote(src, dst, send, recv, to):
        return pltpu.make_async_remote_copy(
            src_ref=src, dst_ref=dst, send_sem=send, recv_sem=recv, device_id=to,
            device_id_type=MESH,
        )

    parts = [slice(c * 512, (c + 1) * 512) for c in range(4)]
    relays = [
        remote(con_ref.at[3, :, s], from_opp.at[:, s], relay_send.at[c], relay_recv.at[c], sibling)
        for c, s in enumerate(parts)
    ]
    own = remote(con_ref.at[1], from_own, own_sem.at[0], own_sem.at[1], sibling)
    quarter = pl.ds(pl.multiple_of(core * 512, 512), 512)
    rest = pl.ds(pl.multiple_of((1 - core) * 512, 512), 512)
    here, there = ybuf.at[x_hi, :, quarter], ybuf.at[1 - x_hi, :, quarter]
    tgt = remote(here, here, tgt_sem.at[0], tgt_sem.at[1], across)
    tgt.start()
    passed = remote(there, there, tgt_sem.at[2], tgt_sem.at[3], sibling)

    for copy in relays:
        copy.start()
    own.start()
    onward = [
        remote(opp.at[:, s], landed.at[:, s], opp_send.at[c], opp_recv.at[c], opposite)
        for c, s in enumerate(parts)
    ]

    def target(part, centre):
        first, at = part * HALF, pl.ds(pl.multiple_of(part * 8, 8), 8)
        cells = ybuf[part]
        kept = padded(cells, centre)
        square = jnp.sum(kept * kept, axis=0, keepdims=True) * SCALE
        mass = jnp.log2(cells[COMPONENTS : COMPONENTS + 1, :])
        log_y[at, :] = jnp.concatenate([mass[:, r * 128 : (r + 1) * 128] for r in range(8)], axis=0)
        square = jnp.concatenate([square[:, r * 128 : (r + 1) * 128] for r in range(8)], axis=0)
        high, middle, unused = pieces(kept)
        set_left(lhs_y, first, high, high, middle, log_y[at, :] - square)

    def pass_on(c):
        relays[c].wait_recv()
        opp[:, parts[c]] = con_ref[2, :, parts[c]] + from_opp[:, parts[c]]
        onward[c].start()

    centre = jnp.sum(ybuf[x_hi], axis=1, keepdims=True) * (1.0 / HALF)
    for c in range(4):
        pass_on(c)
    target(x_hi, centre)
    remote(there, there, tgt_sem.at[0], tgt_sem.at[1], across).wait_recv()
    passed.start()
    handed = ybuf.at[1 - x_hi, :, rest]
    remote(handed, handed, tgt_sem.at[2], tgt_sem.at[3], sibling).wait_recv()
    target(1 - x_hi, centre)

    def put_wide(j, value):
        for r in range(TILE // 128):
            wide[pl.ds(TILE // 128 * j + r, 1), :] = value[:, r * 128 : (r + 1) * 128]

    own.wait_recv()

    half = pl.ds(pl.multiple_of(z_lo * HALF, HALF), HALF)
    shared = remote(xfull.at[:, half], sbuf, self_sem.at[0], self_sem.at[1], partner)
    kept_here = pltpu.make_async_copy(xfull.at[:, half], sbuf, local_sem)

    def arrive(j):
        if j % 2:
            return
        c = j // 2
        s = parts[c]
        onward[c].wait_recv()
        cells = con_ref[0, :, s] + from_own[:, s] + landed[:, s]
        xfull[:, s] = cells
        if c % 2:
            @pl.when((z_lo == c // 2) & alone)
            def _():
                kept_here.start()

            @pl.when((z_lo == c // 2) & jnp.logical_not(alone))
            def _():
                shared.start()

        kept = padded(cells, centre)
        to_rows(sq_x, jnp.sum(kept * kept, axis=0, keepdims=True) * SCALE, 4 * c)
        to_rows(log_x, jnp.log2(cells[COMPONENTS : COMPONENTS + 1, :]), 4 * c)
        high, middle, unused = pieces(kept * (2.0 * SCALE))
        set_right(rhs_x, s, high, middle, high)

    def spread(at, me, others, peer, send, recv):
        for k in others:
            remote(at.at[me], at.at[me], send, recv, peer(k)).start()

    def all_of(at, others, peer, send, recv):
        part = at.at[pl.ds(0, len(others))]
        return remote(part, part, send, recv, peer(others[0]))

    to_m, to_g = (m_others, m_peer), (g_others, g_peer)

    def f_box(it, n):
        return fb.at[it, n], fb_send.at[it, n], fb_recv.at[it, n]

    def g_box(it, n):
        return gb.at[it, n], gb_send.at[it, n], gb_recv.at[it, n]

    def p_box(it):
        return pb.at[it], pb_send.at[it], pb_recv.at[it]

    def send_f(it, n):
        at, send, recv = f_box(it, n)
        rows = slice(8 * n, 8 * n + 8)
        at[m] = wide[rows, :] - sq_x[rows, :]
        spread(at, m, *to_m, send, recv)

    def send_p(it):
        at, send, recv = p_box(it)
        at[m] = wide[...] - sq_x[...]
        spread(at, m, *to_m, send, recv)

    def send_g(it, n):
        at, send, recv = g_box(it, n)
        rows = slice(8 * n, 8 * n + 8)
        at[g] = gwide[rows, :] - log_y[rows, :]
        spread(at, g, *to_g, send, recv)

    def put_first(j, value):
        put_wide(j, value)
        if j % 4 == 3:
            send_f(0, j // 4)

    first_pass(lhs_y, rhs_x, cache_f, GROUP, put_first, arrive)

    pot_p[...] = jnp.zeros_like(pot_p)
    pot_s[...] = jnp.zeros_like(pot_s)

    half_rows = pl.ds(pl.multiple_of(z_lo * 8, 8), 8)

    def finish_p(it):
        at, send, recv = p_box(it)
        moved = all_of(at, *to_m, send, recv)
        moved.wait_recv()
        moved.wait_send()
        pot_p[...] = 0.5 * (pot_p[...] - TAU * log_sum(pb[it]))

        @pl.when((it < ITERS - 1) & jnp.logical_not(alone))
        def _():
            pots[0, it] = pot_p[half_rows, :]
            remote(
                pots.at[0, it], pots.at[1, it], pot_send.at[it], pot_recv.at[it], partner
            ).start()

    def iteration(it, carry):
        @pl.when(it > 0)
        def _():
            for n in range(2):
                at, send, recv = g_box(it - 1, n)
                moved = all_of(at, *to_g, send, recv)
                moved.wait_recv()
                spread_rows(wide_g, -TAU * log_sum(at[...]), 8 * n)
                if n == 0:
                    row_pass(cache_f, wide_g, (0, HALF), (0, 8), state, True, False, None)
                moved.wait_send()
            for n in range(2):
                tiles = (4 * n, 4 * n + 4)
                row_pass(cache_f, wide_g, (HALF, GROUP), tiles, state, False, True, put_wide)
                send_f(it, n)

        @pl.when(it == 0)
        def _():
            @pl.when(alone)
            def _():
                kept_here.wait()

            @pl.when(jnp.logical_not(alone))
            def _():
                shared.wait_recv()
                shared.wait_send()

            for copy in relays + onward + [own, tgt, passed]:
                copy.wait_send()
            got = sbuf[...]
            columns = padded(got, centre)
            to_rows(sq_s, jnp.sum(columns * columns, axis=0, keepdims=True) * SCALE)
            to_rows(log_s, jnp.log2(got[COMPONENTS : COMPONENTS + 1, :]))
            upper, lower, unused = pieces(columns)
            set_left(lhs_s, 0, upper, upper, lower, log_s[...] - sq_s[...])

        @pl.when(it == 1)
        def _():
            finish_p(0)

        @pl.when(it > 0)
        def _():
            last = it - 1

            @pl.when(alone)
            def _():
                pot_s[...] = pot_p[half_rows, :]

            @pl.when(jnp.logical_not(alone))
            def _():
                moved = remote(
                    pots.at[0, last], pots.at[1, last], pot_send.at[last], pot_recv.at[last],
                    partner,
                )
                moved.wait_recv()
                moved.wait_send()
                pot_s[...] = pots[1, last]

            spread_rows(wide_s, pot_s[...])
            row_pass(cache_p, wide_s, (0, HALF), (0, 8), None, True, True, put_wide)
            send_p(it)

        sent = []
        for n in range(2):
            at, send, recv = f_box(it, n)
            sent.append(all_of(at, *to_m, send, recv))
            sent[n].wait_recv()
            rows = slice(8 * n, 8 * n + 8)
            pot_f = -TAU * log_sum(at[...])
            pots_f[rows, :] = pot_f
            weight = log_x[rows, :] + pot_f - sq_x[rows, :]
            if n == 0:
                column_pass(cache_f, weight, 0, (0, 16), spread_w, peaks, totals)
        for n in range(2):
            blocks = (8 * n, 8 * n + 8)
            column_pass(cache_f, weight, 1, blocks, spread_w, peaks, totals)
            over_lanes(peaks, totals, blocks, gwide)
            send_g(it, n)

        @pl.when(it == ITERS - 1)
        def _():
            fin[0, x_hi] = pots_f[...] * (1.0 / SCALE)
            remote(
                fin.at[0, x_hi], fin.at[0, x_hi], fin_send.at[0], fin_recv.at[0], twin
            ).start()

        @pl.when(it == 0)
        def _():
            first_pass(lhs_s, rhs_x, cache_p, HALF, put_wide)
            send_p(0)

        @pl.when(it > 0)
        def _():
            finish_p(it)

        @pl.when(it == ITERS - 1)
        def _():
            fin[1, x_hi] = pot_p[...] * (1.0 / SCALE)
            remote(
                fin.at[1, x_hi], fin.at[1, x_hi], fin_send.at[1], fin_recv.at[1], twin
            ).start()

        for copy in sent:
            copy.wait_send()
        return carry

    lax.fori_loop(0, ITERS, iteration, 0)

    for n in range(2):
        at, send, recv = g_box(ITERS - 1, n)
        moved = all_of(at, *to_g, send, recv)
        moved.wait_recv()
        moved.wait_send()
    tgt_out[...] = (-TAU / SCALE) * log_sum(gb[ITERS - 1, x_hi])
    for kind in range(2):
        remote(
            fin.at[kind, 1 - x_hi], fin.at[kind, 1 - x_hi], fin_send.at[kind], fin_recv.at[kind],
            twin,
        ).wait_recv()
        remote(
            fin.at[kind, x_hi], fin.at[kind, x_hi], fin_send.at[kind], fin_recv.at[kind], twin
        ).wait_send()
    src_out[0:16, :] = fin[0, 0]
    src_out[16:32, :] = fin[0, 1]
    self_out[0:16, :] = fin[1, 0]
    self_out[16:32, :] = fin[1, 1]


def on_device(
    src_features, src_mass, section_ids, shard_counts, section_offsets, tgt_features, tgt_mass
):
    vmem = pl.BlockSpec(memory_space=pltpu.VMEM)
    hbm = pl.BlockSpec(memory_space=pltpu.HBM)
    V, D = pltpu.VMEM, pltpu.SemaphoreType.DMA
    contributions = pl.pallas_call(
        relay_kernel,
        out_shape=V((4, ROWS, GROUP), F32),
        in_specs=[pl.BlockSpec(memory_space=pltpu.SMEM)] + [hbm] * 4,
        out_specs=vmem,
        scratch_shapes=[
            V((ROWS, WIDTH), F32), V((COMPONENTS, CAP), F32), V((1, CAP), F32),
            V((1, CAP), jnp.int32), V((SECTIONS, COMPONENTS), F32), D((4,)), D((3,)),
        ],
        compiler_params=pltpu.CompilerParams(vmem_limit_bytes=58 * 1024 * 1024),
    )(
        shard_counts,
        src_features,
        src_mass.reshape(1, CAP),
        section_ids.reshape(1, CAP),
        section_offsets.T,
    )
    rows16, rows8 = (16, 128), (8, 128)
    outs = pl.pallas_call(
        sinkhorn_kernel,
        out_shape=(
            V((32, 128), F32), V((8, 128), F32), V((32, 128), F32),
        ),
        in_specs=[vmem, hbm, hbm],
        out_specs=(vmem, vmem, vmem),
        scratch_shapes=[
            V((COMPONENTS, HALF), F32), V((1, HALF), F32),
            V((ROWS, GROUP), F32), V((ROWS, GROUP), F32), V((ROWS, GROUP), F32),
            V((ROWS, GROUP), F32), V((2, ROWS, HALF), F32), V((ROWS, GROUP), F32),
            V((ROWS, HALF), F32),
            V((GROUP, 256), BF16), V((HALF, 256), BF16),
            V((256, GROUP), BF16),
            V((TILES, GROUP, TILE), F32), V((TILES, HALF, TILE), F32),
            V((8, 8, 128), F32), V((GROUP, 128), F32), V((GROUP, 128), F32),
            V((GROUP, 128), F32), V((HALF, 128), F32), V((2, TILES, 8, TILE), F32), V(rows16, F32),
            V(rows16, F32), V(rows8, F32), V(rows16, F32), V(rows16, F32), V(rows8, F32),
            V(rows16, F32), V(rows8, F32), V(rows16, F32), V(rows16, F32),
            V((ITERS, 2, 16) + rows8, F32), V((ITERS, 16) + rows16, F32),
            V((ITERS, 2, 8) + rows8, F32), V((2, ITERS - 1) + rows8, F32),
            V((2, 2) + rows16, F32),
            D((4,)), D((4,)), D((4,)), D((4,)), D((2,)), D((4,)), D((2,)), D,
            D((ITERS, 2)), D((ITERS, 2)), D((ITERS,)), D((ITERS,)), D((ITERS, 2)), D((ITERS, 2)),
            D((ITERS,)), D((ITERS,)), D((2,)), D((2,)),
            D((2,)),
        ],
        compiler_params=pltpu.CompilerParams(
            collective_id=0, has_side_effects=True, vmem_limit_bytes=50 * 1024 * 1024
        ),
    )(contributions, tgt_features, tgt_mass.reshape(1, HALF))
    return (outs[0].reshape(2 * GROUP), outs[1].reshape(HALF), outs[2].reshape(2 * GROUP))


def solution(mesh):
    return jax.shard_map(
        on_device,
        mesh=mesh,
        in_specs=(P(None, "src"), P("src"), P("src"), P(), P(), P(None, "tgt"), P("tgt")),
        out_specs=(P("src"), P("tgt"), P("src")),
        check_vma=False,
    )
```

```python
import jax
import jax.numpy as jnp
from jax import lax
from jax.experimental import pallas as pl
from jax.experimental.pallas import tpu as pltpu
from jax.sharding import PartitionSpec as P

COMPONENTS = 50
ROWS = 56
SECTIONS = 32
ITERS = 3
CAP = 8192
GROUP = 2048
HALF = 1024
SPAN = GROUP + 128
LEAD = GROUP
WIDTH = LEAD + CAP + SPAN

EPS = 0.05
TAU = 1.0 / (1.0 + EPS)
LOG2E = 1.4426950408889634
SCALE = LOG2E / EPS

F32 = jnp.float32
BF16 = jnp.bfloat16
MESH = pl.DeviceIdType.MESH
TILE = 256
TILES = GROUP // TILE
CHUNK = 256


def place():
    src, tgt = lax.axis_index("src"), lax.axis_index("tgt")
    z, rest = lax.div(tgt, 8), lax.rem(tgt, 8)
    return (
        lax.div(src, 2),
        lax.rem(src, 2),
        lax.div(z, 2),
        lax.rem(z, 2),
        lax.div(rest, 2),
        lax.rem(rest, 2),
    )


def device(x_lo, core, z_hi, z_lo, y, x_hi):
    return (x_lo * 2 + core, (z_hi * 2 + z_lo) * 8 + y * 2 + x_hi)


def pieces(value):
    high = value.astype(BF16)
    rest = value - high.astype(F32)
    middle = rest.astype(BF16)
    return high, middle, (rest - middle.astype(F32)).astype(BF16)


def correct(feats_ref, mass_ref, ids_ref, offsets_ref, held, ready):
    three = jnp.concatenate([p.astype(F32) for p in pieces(offsets_ref[...])], axis=0).astype(BF16)
    for at in range(0, CAP, 1024):
        ready(at)
        ids = ids_ref[:, at : at + 1024]
        section = lax.broadcasted_iota(jnp.int32, (3 * SECTIONS, 1024), 0) & (SECTIONS - 1)
        onehot = jnp.where(section == ids, 1.0, 0.0).astype(BF16)
        shift = lax.dot_general(
            three, onehot, (((0,), (0,)), ((), ())), preferred_element_type=F32
        )
        to = slice(LEAD + at, LEAD + at + 1024)
        held[48:ROWS, to] = jnp.zeros((ROWS - 48, 1024), F32)
        held[0:COMPONENTS, to] = feats_ref[:, at : at + 1024] - shift
        held[COMPONENTS : COMPONENTS + 1, to] = mass_ref[:, at : at + 1024]


def contribute(held, base, count, out):
    at = jnp.clip(base, -LEAD, CAP) + LEAD
    aligned = pl.multiple_of(lax.div(at, 128) * 128, 128)
    off = lax.rem(at, 128)
    turn = lax.rem(128 - off, 128)
    lane = lax.broadcasted_iota(jnp.int32, (ROWS, 128), 1)
    before = pltpu.roll(held[:, pl.ds(aligned, 128)], turn, 1)
    for t in range(GROUP // 128):
        after = pltpu.roll(
            held[:, pl.ds(pl.multiple_of(aligned + (t + 1) * 128, 128), 128)], turn, 1
        )
        value = jnp.where(lane < 128 - off, before, after)
        local = lane + (base + t * 128)
        out[:, t * 128 : (t + 1) * 128] = jnp.where((local >= 0) & (local < count), value, 0.0)
        before = after


def relay_kernel(
    counts_ref, feats_any, mass_any, ids_any, offsets_any, out_ref,
    held, feats_ref, mass_ref, ids_ref, offsets_ref, feats_sem, small_sem,
):
    small = [
        pltpu.make_async_copy(a, b, small_sem.at[i])
        for i, (a, b) in enumerate(
            [(offsets_any, offsets_ref), (ids_any, ids_ref), (mass_any, mass_ref)]
        )
    ]
    large = [
        pltpu.make_async_copy(
            feats_any.at[:, at : at + 2048], feats_ref.at[:, at : at + 2048], feats_sem.at[i]
        )
        for i, at in enumerate(range(0, CAP, 2048))
    ]
    for copy in small + large:
        copy.start()
    x_lo, core, z_hi, z_lo, y, x_hi = place()
    mine = x_lo * 2 + core
    begin = jnp.int32(0)
    for k in range(3):
        begin = begin + jnp.where(k < mine, counts_ref[k], 0)
    count = counts_ref[mine]

    def ready(at):
        if at % 2048 == 0:
            large[at // 2048].wait()

    for copy in small:
        copy.wait()
    correct(feats_ref, mass_ref, ids_ref, offsets_ref, held, ready)
    for index in range(4):
        to_x, to_core = lax.rem(x_lo + index // 2, 2), lax.rem(core + index % 2, 2)
        straight = lax.rem(x_lo + to_core, 2) * (index // 2)
        base = (to_x * 2 + to_core) * (2 * GROUP) + lax.rem(x_hi + straight, 2) * GROUP - begin
        contribute(held, base, count, out_ref.at[index])


def log_sum(parts):
    peak = jnp.max(parts, axis=0)
    return peak + jnp.log2(jnp.sum(jnp.exp2(parts - peak[None]), axis=0))


def tree(op, parts):
    while len(parts) > 1:
        pairs = [op(a, b) for a, b in zip(parts[0::2], parts[1::2])]
        parts = pairs + parts[len(pairs) * 2 :]
    return parts[0]


def first_pass(lhs, rhs, cache, count, put, ready=None):
    chunk = min(CHUNK, count)

    def both(j, peak):
        tops, sums = [], []
        for at in range(0, count, chunk):
            if j < TILES:
                s = jnp.dot(
                    lhs[at : at + chunk, :], rhs[:, j * TILE : (j + 1) * TILE],
                    preferred_element_type=F32,
                )
                cache[j, at : at + chunk, :] = s
                s = s.reshape(chunk // 8, 8, TILE)
                tops.append(tree(jnp.maximum, [s[i] for i in range(chunk // 8)]))
            if peak is not None:
                e = [
                    jnp.exp2(cache[j - 1, row : row + 8, :] - peak)
                    for row in range(at, at + chunk, 8)
                ]
                sums.append(tree(jnp.add, e))
        if peak is not None:
            total = jnp.sum(tree(jnp.add, sums), axis=0, keepdims=True)
            put(j - 1, peak + jnp.log2(total))
        return jnp.max(tree(jnp.maximum, tops), axis=0, keepdims=True) if tops else None

    peak = None
    for j in range(TILES + 1):
        if ready is not None and j < TILES:
            ready(j)
        peak = both(j, peak)


def several(body, span, each):
    def turn(i, carry):
        for k in range(each):
            body(i * each + k)
        return carry

    lax.fori_loop(span[0] // each, span[1] // each, turn, 0)


def row_pass(cache, weight, span, tiles, state, begin, end, put):
    def body(j):
        ends = [[], []]
        for at in range(span[0], span[1], 128):
            w = [weight[row : row + 8, :] for row in range(at, at + 128, 8)]
            for h in range(2):
                lanes = slice(h * 128, (h + 1) * 128)
                t = [cache[j, at + 8 * i : at + 8 * i + 8, lanes] + w[i] for i in range(16)]
                top = tree(jnp.maximum, t)
                ends[h].append((top, tree(jnp.add, [jnp.exp2(v - top) for v in t])))
        rows = []
        for h in range(2):
            lanes = slice(h * 128, (h + 1) * 128)
            if not begin:
                ends[h].append((state[0, j, :, lanes], state[1, j, :, lanes]))
            top = tree(jnp.maximum, [v[0] for v in ends[h]])
            part = tree(jnp.add, [v[1] * jnp.exp2(v[0] - top) for v in ends[h]])
            if end:
                most = jnp.max(top, axis=0, keepdims=True)
                part = jnp.sum(part * jnp.exp2(top - most), axis=0, keepdims=True)
                rows.append(most + jnp.log2(part))
            else:
                state[0, j, :, lanes] = top
                state[1, j, :, lanes] = part
        if end:
            put(j, jnp.concatenate(rows, axis=1))

    several(body, tiles, 2)


def column_pass(cache, weight, half, blocks, spread_w, peaks, totals):
    for r in range(8):
        spread_w[r] = jnp.broadcast_to(weight[r : r + 1, :], (8, 128))

    def body(block):
        for sub in range(4):
            rows = pl.ds(pl.multiple_of(block * 128 + sub * 32, 32), 32)
            parts = []
            for r in range(8):
                lanes = slice(r % 2 * 128, r % 2 * 128 + 128)
                t = cache[half * 4 + r // 2, rows, lanes].reshape(4, 8, 128)
                parts.append(t + spread_w[r][None])
            top = tree(jnp.maximum, parts)
            if half:
                before = peaks[rows, :].reshape(4, 8, 128)
                top = jnp.maximum(top, before)
            sums = [jnp.exp2(t - top) for t in parts]
            if half:
                sums.append(totals[rows, :].reshape(4, 8, 128) * jnp.exp2(before - top))
            peaks[rows, :] = top.reshape(32, 128)
            totals[rows, :] = tree(jnp.add, sums).reshape(32, 128)

    several(body, blocks, 4)


def over_lanes(peaks, totals, blocks, out):
    for c in range(blocks[0], blocks[1]):
        at = slice(c * 128, (c + 1) * 128)
        turned = peaks[at, :].T
        top = jnp.max(turned, axis=0, keepdims=True)
        total = jnp.sum(totals[at, :].T * jnp.exp2(turned - top), axis=0, keepdims=True)
        out[c : c + 1, :] = top + jnp.log2(total)


def spread_rows(wide_w, weight, first=0):
    for c in range(weight.shape[0]):
        at = slice((first + c) * 128, (first + c + 1) * 128)
        wide_w[at, :] = jnp.broadcast_to(weight[c : c + 1, :], (128, 128)).T


def to_rows(ref, row, first=0):
    for r in range(row.shape[1] // 128):
        ref[first + r : first + r + 1, :] = row[:, r * 128 : (r + 1) * 128]


def block_rows(first, c):
    return pl.ds(pl.multiple_of(first + c * 128, 128), 128)


def set_left(lhs, first, one, two, three, weight):
    rows = weight.shape[0]
    parts = [p.astype(F32) for p in pieces(weight)]
    fill = jnp.zeros((64 - 3 * rows, 128), F32)
    for c in range(rows):
        at = slice(c * 128, (c + 1) * 128)
        upper = jnp.concatenate([one[:, at].astype(F32), two[:, at].astype(F32)], axis=0)
        row = lax.broadcasted_iota(jnp.int32, (rows, 128), 0)
        chosen = [jnp.where(row == c, p, 0.0) for p in parts]
        lower = jnp.concatenate(chosen + [fill, three[:, at].astype(F32)], axis=0)
        lhs[block_rows(first, c), 0:128] = upper.T.astype(BF16)
        lhs[block_rows(first, c), 128:256] = lower.T.astype(BF16)


def set_right(rhs, at, one, two, three):
    rhs[0:64, at] = one
    rhs[64:128, at] = two
    row = lax.broadcasted_iota(jnp.int32, three.shape, 0)
    rhs[128:192, at] = jnp.where(row < 24, 1.0, 0.0).astype(BF16)
    rhs[192:256, at] = three


def padded(cells, centre):
    row = lax.broadcasted_iota(jnp.int32, cells.shape, 0)
    kept = jnp.where(row < COMPONENTS, cells - centre, 0.0)
    return jnp.concatenate([kept, jnp.zeros((64 - ROWS, cells.shape[1]), F32)], axis=0)


def sinkhorn_kernel(
    con_ref, tgt_any, tgt_mass_any,
    src_out, tgt_out, self_out,
    tgt_ref, tgt_mass_ref,
    from_own, from_opp, opp, landed, ybuf, xfull, sbuf,
    lhs_y, lhs_s, rhs_x, cache_f, cache_p,
    spread_w, peaks, totals, wide_g, wide_s, state, gwide,
    sq_x, sq_s, log_x, log_y, log_s, pot_p, pot_s, wide, pots_f,
    fb, pb, gb, pots, fin,
    relay_send, relay_recv, opp_send, opp_recv, own_sem, tgt_sem, self_sem, local_sem,
    fb_send, fb_recv, pb_send, pb_recv,
    gb_send, gb_recv, pot_send, pot_recv, fin_send, fin_recv, con_sem,
):
    x_lo, core, z_hi, z_lo, y, x_hi = place()
    sibling = device(x_lo, 1 - core, z_hi, z_lo, y, x_hi)
    twin = device(x_lo, core, z_hi, z_lo, y, 1 - x_hi)
    across = device(1 - x_lo, core, z_hi, z_lo, y, 1 - x_hi)
    straight = lax.rem(x_lo + core, 2)
    opposite = device(1 - x_lo, core, z_hi, z_lo, y, lax.rem(x_hi + straight, 2))
    y_hi, y_lo = lax.div(y, 2), lax.rem(y, 2)
    partner = device(
        lax.rem(x_lo + y_hi, 2), lax.rem(core + y_lo, 2), z_hi, z_lo, y, lax.rem(x_hi + z_hi, 2)
    )
    alone = (y + z_hi) == 0
    g = x_lo * 4 + core * 2 + x_hi
    m = z_hi * 8 + z_lo * 4 + y

    def m_peer(k):
        return device(x_lo, core, lax.div(k, 8), lax.rem(lax.div(k, 4), 2), lax.rem(k, 4), x_hi)

    def g_peer(k):
        return device(lax.div(k, 4), lax.rem(lax.div(k, 2), 2), z_hi, z_lo, y, lax.rem(k, 2))

    m_others = [lax.rem(m + d, 16) for d in range(1, 16)]
    g_others = [lax.rem(g + d, 8) for d in range(1, 8)]

    barrier = pltpu.get_barrier_semaphore()
    peers = [m_peer(k) for k in m_others]
    peers += [g_peer(k) for k in g_others]
    for peer in peers:
        pl.semaphore_signal(barrier, inc=1, device_id=peer, device_id_type=MESH)

    loads = [
        pltpu.make_async_copy(a, b, con_sem.at[i])
        for i, (a, b) in enumerate(
            [(tgt_any, tgt_ref), (tgt_mass_any, tgt_mass_ref)]
        )
    ]
    for copy in loads:
        copy.start()
    loads[0].wait()
    loads[1].wait()
    ybuf[x_hi, 48:ROWS, :] = jnp.zeros((ROWS - 48, HALF), F32)
    ybuf[x_hi, 0:COMPONENTS, :] = tgt_ref[...]
    ybuf[x_hi, COMPONENTS : COMPONENTS + 1, :] = tgt_mass_ref[...]

    pl.semaphore_wait(barrier, len(peers))

    def remote(src, dst, send, recv, to):
        return pltpu.make_async_remote_copy(
            src_ref=src, dst_ref=dst, send_sem=send, recv_sem=recv, device_id=to,
            device_id_type=MESH,
        )

    parts = [slice(c * 512, (c + 1) * 512) for c in range(4)]
    relays = [
        remote(con_ref.at[3, :, s], from_opp.at[:, s], relay_send.at[c], relay_recv.at[c], sibling)
        for c, s in enumerate(parts)
    ]
    own = remote(con_ref.at[1], from_own, own_sem.at[0], own_sem.at[1], sibling)
    quarter = pl.ds(pl.multiple_of(core * 512, 512), 512)
    rest = pl.ds(pl.multiple_of((1 - core) * 512, 512), 512)
    here, there = ybuf.at[x_hi, :, quarter], ybuf.at[1 - x_hi, :, quarter]
    tgt = remote(here, here, tgt_sem.at[0], tgt_sem.at[1], across)
    tgt.start()
    passed = remote(there, there, tgt_sem.at[2], tgt_sem.at[3], sibling)

    for copy in relays:
        copy.start()
    own.start()
    onward = [
        remote(opp.at[:, s], landed.at[:, s], opp_send.at[c], opp_recv.at[c], opposite)
        for c, s in enumerate(parts)
    ]

    def target(part, centre):
        first, at = part * HALF, pl.ds(pl.multiple_of(part * 8, 8), 8)
        cells = ybuf[part]
        kept = padded(cells, centre)
        square = jnp.sum(kept * kept, axis=0, keepdims=True) * SCALE
        mass = jnp.log2(cells[COMPONENTS : COMPONENTS + 1, :])
        log_y[at, :] = jnp.concatenate([mass[:, r * 128 : (r + 1) * 128] for r in range(8)], axis=0)
        square = jnp.concatenate([square[:, r * 128 : (r + 1) * 128] for r in range(8)], axis=0)
        high, middle, unused = pieces(kept)
        set_left(lhs_y, first, high, high, middle, log_y[at, :] - square)

    def pass_on(c):
        relays[c].wait_recv()
        opp[:, parts[c]] = con_ref[2, :, parts[c]] + from_opp[:, parts[c]]
        onward[c].start()

    centre = jnp.sum(ybuf[x_hi], axis=1, keepdims=True) * (1.0 / HALF)
    for c in range(4):
        pass_on(c)
    target(x_hi, centre)
    remote(there, there, tgt_sem.at[0], tgt_sem.at[1], across).wait_recv()
    passed.start()
    handed = ybuf.at[1 - x_hi, :, rest]
    remote(handed, handed, tgt_sem.at[2], tgt_sem.at[3], sibling).wait_recv()
    target(1 - x_hi, centre)

    def put_wide(j, value):
        for r in range(TILE // 128):
            wide[pl.ds(TILE // 128 * j + r, 1), :] = value[:, r * 128 : (r + 1) * 128]

    own.wait_recv()

    half = pl.ds(pl.multiple_of(z_lo * HALF, HALF), HALF)
    shared = remote(xfull.at[:, half], sbuf, self_sem.at[0], self_sem.at[1], partner)
    kept_here = pltpu.make_async_copy(xfull.at[:, half], sbuf, local_sem)

    def arrive(j):
        if j % 2:
            return
        c = j // 2
        s = parts[c]
        onward[c].wait_recv()
        cells = con_ref[0, :, s] + from_own[:, s] + landed[:, s]
        xfull[:, s] = cells
        if c % 2:
            @pl.when((z_lo == c // 2) & alone)
            def _():
                kept_here.start()

            @pl.when((z_lo == c // 2) & jnp.logical_not(alone))
            def _():
                shared.start()

        kept = padded(cells, centre)
        to_rows(sq_x, jnp.sum(kept * kept, axis=0, keepdims=True) * SCALE, 4 * c)
        to_rows(log_x, jnp.log2(cells[COMPONENTS : COMPONENTS + 1, :]), 4 * c)
        high, middle, unused = pieces(kept * (2.0 * SCALE))
        set_right(rhs_x, s, high, middle, high)

    def spread(at, me, others, peer, send, recv):
        for k in others:
            remote(at.at[me], at.at[me], send, recv, peer(k)).start()

    def all_of(at, others, peer, send, recv):
        part = at.at[pl.ds(0, len(others))]
        return remote(part, part, send, recv, peer(others[0]))

    to_m, to_g = (m_others, m_peer), (g_others, g_peer)

    def f_box(it, n):
        return fb.at[it, n], fb_send.at[it, n], fb_recv.at[it, n]

    def g_box(it, n):
        return gb.at[it, n], gb_send.at[it, n], gb_recv.at[it, n]

    def p_box(it):
        return pb.at[it], pb_send.at[it], pb_recv.at[it]

    def send_f(it, n):
        at, send, recv = f_box(it, n)
        rows = slice(8 * n, 8 * n + 8)
        at[m] = wide[rows, :] - sq_x[rows, :]
        spread(at, m, *to_m, send, recv)

    def send_p(it):
        at, send, recv = p_box(it)
        at[m] = wide[...] - sq_x[...]
        spread(at, m, *to_m, send, recv)

    def send_g(it, n):
        at, send, recv = g_box(it, n)
        rows = slice(8 * n, 8 * n + 8)
        at[g] = gwide[rows, :] - log_y[rows, :]
        spread(at, g, *to_g, send, recv)

    def put_first(j, value):
        put_wide(j, value)
        if j % 4 == 3:
            send_f(0, j // 4)

    first_pass(lhs_y, rhs_x, cache_f, GROUP, put_first, arrive)

    pot_p[...] = jnp.zeros_like(pot_p)
    pot_s[...] = jnp.zeros_like(pot_s)

    half_rows = pl.ds(pl.multiple_of(z_lo * 8, 8), 8)

    def finish_p(it):
        at, send, recv = p_box(it)
        moved = all_of(at, *to_m, send, recv)
        moved.wait_recv()
        moved.wait_send()
        pot_p[...] = 0.5 * (pot_p[...] - TAU * log_sum(pb[it]))

        @pl.when((it < ITERS - 1) & jnp.logical_not(alone))
        def _():
            pots[0, it] = pot_p[half_rows, :]
            remote(
                pots.at[0, it], pots.at[1, it], pot_send.at[it], pot_recv.at[it], partner
            ).start()

    def iteration(it, carry):
        @pl.when(it > 0)
        def _():
            for n in range(2):
                at, send, recv = g_box(it - 1, n)
                moved = all_of(at, *to_g, send, recv)
                moved.wait_recv()
                spread_rows(wide_g, -TAU * log_sum(at[...]), 8 * n)
                if n == 0:
                    row_pass(cache_f, wide_g, (0, HALF), (0, 8), state, True, False, None)
                moved.wait_send()

            @pl.when(it == 1)
            def _():
                finish_p(0)

            for n in range(2):
                tiles = (4 * n, 4 * n + 4)
                row_pass(cache_f, wide_g, (HALF, GROUP), tiles, state, False, True, put_wide)
                send_f(it, n)

        @pl.when(it == 0)
        def _():
            @pl.when(alone)
            def _():
                kept_here.wait()

            @pl.when(jnp.logical_not(alone))
            def _():
                shared.wait_recv()
                shared.wait_send()

            for copy in relays + onward + [own, tgt, passed]:
                copy.wait_send()
            got = sbuf[...]
            columns = padded(got, centre)
            to_rows(sq_s, jnp.sum(columns * columns, axis=0, keepdims=True) * SCALE)
            to_rows(log_s, jnp.log2(got[COMPONENTS : COMPONENTS + 1, :]))
            upper, lower, unused = pieces(columns)
            set_left(lhs_s, 0, upper, upper, lower, log_s[...] - sq_s[...])

        @pl.when(it > 0)
        def _():
            last = it - 1

            @pl.when(alone)
            def _():
                pot_s[...] = pot_p[half_rows, :]

            @pl.when(jnp.logical_not(alone))
            def _():
                moved = remote(
                    pots.at[0, last], pots.at[1, last], pot_send.at[last], pot_recv.at[last],
                    partner,
                )
                moved.wait_recv()
                moved.wait_send()
                pot_s[...] = pots[1, last]

            spread_rows(wide_s, pot_s[...])
            row_pass(cache_p, wide_s, (0, HALF), (0, 8), None, True, True, put_wide)
            send_p(it)

        sent = []
        for n in range(2):
            at, send, recv = f_box(it, n)
            sent.append(all_of(at, *to_m, send, recv))
            sent[n].wait_recv()
            rows = slice(8 * n, 8 * n + 8)
            pot_f = -TAU * log_sum(at[...])
            pots_f[rows, :] = pot_f
            weight = log_x[rows, :] + pot_f - sq_x[rows, :]
            if n == 0:
                column_pass(cache_f, weight, 0, (0, 16), spread_w, peaks, totals)
        for n in range(2):
            blocks = (8 * n, 8 * n + 8)
            column_pass(cache_f, weight, 1, blocks, spread_w, peaks, totals)
            over_lanes(peaks, totals, blocks, gwide)
            send_g(it, n)

        @pl.when(it == ITERS - 1)
        def _():
            fin[0, x_hi] = pots_f[...] * (1.0 / SCALE)
            remote(
                fin.at[0, x_hi], fin.at[0, x_hi], fin_send.at[0], fin_recv.at[0], twin
            ).start()

        @pl.when(it == 0)
        def _():
            first_pass(lhs_s, rhs_x, cache_p, HALF, put_wide)
            send_p(0)

        @pl.when(it > 0)
        def _():
            finish_p(it)

        @pl.when(it == ITERS - 1)
        def _():
            fin[1, x_hi] = pot_p[...] * (1.0 / SCALE)
            remote(
                fin.at[1, x_hi], fin.at[1, x_hi], fin_send.at[1], fin_recv.at[1], twin
            ).start()

        for copy in sent:
            copy.wait_send()
        return carry

    lax.fori_loop(0, ITERS, iteration, 0)

    for n in range(2):
        at, send, recv = g_box(ITERS - 1, n)
        moved = all_of(at, *to_g, send, recv)
        moved.wait_recv()
        moved.wait_send()
    tgt_out[...] = (-TAU / SCALE) * log_sum(gb[ITERS - 1, x_hi])
    for kind in range(2):
        remote(
            fin.at[kind, 1 - x_hi], fin.at[kind, 1 - x_hi], fin_send.at[kind], fin_recv.at[kind],
            twin,
        ).wait_recv()
        remote(
            fin.at[kind, x_hi], fin.at[kind, x_hi], fin_send.at[kind], fin_recv.at[kind], twin
        ).wait_send()
    src_out[0:16, :] = fin[0, 0]
    src_out[16:32, :] = fin[0, 1]
    self_out[0:16, :] = fin[1, 0]
    self_out[16:32, :] = fin[1, 1]


def on_device(
    src_features, src_mass, section_ids, shard_counts, section_offsets, tgt_features, tgt_mass
):
    vmem = pl.BlockSpec(memory_space=pltpu.VMEM)
    hbm = pl.BlockSpec(memory_space=pltpu.HBM)
    V, D = pltpu.VMEM, pltpu.SemaphoreType.DMA
    contributions = pl.pallas_call(
        relay_kernel,
        out_shape=V((4, ROWS, GROUP), F32),
        in_specs=[pl.BlockSpec(memory_space=pltpu.SMEM)] + [hbm] * 4,
        out_specs=vmem,
        scratch_shapes=[
            V((ROWS, WIDTH), F32), V((COMPONENTS, CAP), F32), V((1, CAP), F32),
            V((1, CAP), jnp.int32), V((SECTIONS, COMPONENTS), F32), D((4,)), D((3,)),
        ],
        compiler_params=pltpu.CompilerParams(vmem_limit_bytes=58 * 1024 * 1024),
    )(
        shard_counts,
        src_features,
        src_mass.reshape(1, CAP),
        section_ids.reshape(1, CAP),
        section_offsets.T,
    )
    rows16, rows8 = (16, 128), (8, 128)
    outs = pl.pallas_call(
        sinkhorn_kernel,
        out_shape=(
            V((32, 128), F32), V((8, 128), F32), V((32, 128), F32),
        ),
        in_specs=[vmem, hbm, hbm],
        out_specs=(vmem, vmem, vmem),
        scratch_shapes=[
            V((COMPONENTS, HALF), F32), V((1, HALF), F32),
            V((ROWS, GROUP), F32), V((ROWS, GROUP), F32), V((ROWS, GROUP), F32),
            V((ROWS, GROUP), F32), V((2, ROWS, HALF), F32), V((ROWS, GROUP), F32),
            V((ROWS, HALF), F32),
            V((GROUP, 256), BF16), V((HALF, 256), BF16),
            V((256, GROUP), BF16),
            V((TILES, GROUP, TILE), F32), V((TILES, HALF, TILE), F32),
            V((8, 8, 128), F32), V((GROUP, 128), F32), V((GROUP, 128), F32),
            V((GROUP, 128), F32), V((HALF, 128), F32), V((2, TILES, 8, TILE), F32), V(rows16, F32),
            V(rows16, F32), V(rows8, F32), V(rows16, F32), V(rows16, F32), V(rows8, F32),
            V(rows16, F32), V(rows8, F32), V(rows16, F32), V(rows16, F32),
            V((ITERS, 2, 16) + rows8, F32), V((ITERS, 16) + rows16, F32),
            V((ITERS, 2, 8) + rows8, F32), V((2, ITERS - 1) + rows8, F32),
            V((2, 2) + rows16, F32),
            D((4,)), D((4,)), D((4,)), D((4,)), D((2,)), D((4,)), D((2,)), D,
            D((ITERS, 2)), D((ITERS, 2)), D((ITERS,)), D((ITERS,)), D((ITERS, 2)), D((ITERS, 2)),
            D((ITERS,)), D((ITERS,)), D((2,)), D((2,)),
            D((2,)),
        ],
        compiler_params=pltpu.CompilerParams(
            collective_id=0, has_side_effects=True, vmem_limit_bytes=50 * 1024 * 1024
        ),
    )(contributions, tgt_features, tgt_mass.reshape(1, HALF))
    return (outs[0].reshape(2 * GROUP), outs[1].reshape(HALF), outs[2].reshape(2 * GROUP))


def solution(mesh):
    return jax.shard_map(
        on_device,
        mesh=mesh,
        in_specs=(P(None, "src"), P("src"), P("src"), P(), P(), P(None, "tgt"), P("tgt")),
        out_specs=(P("src"), P("tgt"), P("src")),
        check_vma=False,
    )
```
